128 devices in a mesh: leaf: 32 (over x, y, core), sub: 4 (over z).
Axes of the slice: x: 4, y: 4, z: 4, core: 2. Of those that a mesh axis runs over, the one named last changes fastest.
Arguments:
- points: float32 [2, 1048576], P(None, ('leaf', 'sub')), may hold values from 0 to 1
- probes: float32 [16, 1048576], P(None, ('leaf', 'sub')), may hold values from -6 to 6
- basis: float32 [4096, 256, 64], P(('leaf', 'sub')), may hold values from -0.375 to 0.375
- transfer_leaf: float32 [4096, 64, 64], P(('leaf', 'sub')), may hold values from -0.125 to 0.125
- transfer_box: float32 [128, 64, 64], P(('leaf', 'sub')), may hold values from -0.375 to 0.375
- couple_leaf: float32 [4096, 27, 64, 64], P(('leaf', 'sub')), may hold values from -0.15625 to 0.15625
- couple_box: float32 [128, 27, 64, 64], P(('leaf', 'sub')), may hold values from -0.15625 to 0.15625
- couple_column: float32 [32, 4, 64, 64], P('leaf'), may hold values from -0.375 to 0.375
- near_list: int32 [4096, 9], P(('leaf', 'sub')), may hold values from -1 to 4095, as said below
- far_list: int32 [4096, 27], P(('leaf', 'sub')), may hold values from -1 to 4095, as said below
- box_list: int32 [128, 27], P(('leaf', 'sub')), may hold values from -1 to 127, as said below
- column_list: int32 [32, 4], P('leaf'), may hold values from -1 to 31, as said below
Outputs:
- product: float32 [16, 1048576], P(None, ('leaf', 'sub'))
The draws below stay inside these ranges and needn't reach their ends.
Inputs may be any that keep to these rules, and one draw needn't show every extreme that they name: `near_list`: each entry is a leaf whose index differs from the row's leaf by at most 8; entry 0 is the leaf itself; in every row some entries may be -1 and they stand after the valid ones; the first leaf of every box has no -1 and its entry 1 lies exactly 8 away. `far_list`: each valid entry is a leaf whose box (index // 32) differs from the row's box by at most 4, and entry 0 of every row lies exactly 4 boxes away; entries -1 stand after the valid ones; the first leaf of every box has none. Entries may repeat. `box_list`: valid entries are any boxes and may repeat; entries -1 stand after the valid ones; at least 13 entries of every row are valid. `column_list`: valid entries are any columns and may repeat; entries -1 stand after the valid ones; at least 2 entries of every row are valid.
All inputs are finite; a program needn't handle non-finite values.
Results may differ from the reference program's by a relative error of at most 0.0003.
Values sent between devices are 32-bit elements; how exact they have to be, the bound alone decides.
No kernel may reach another device: no remote copies, remote signals or barrier semaphores. Data moves between devices by JAX's collectives and lax.ppermute only.
A program may use at most 128 MiB of HBM per device.

```python
import math
import jax
import jax.numpy as jnp
from jax import lax

LEAF = 256
RANK = 64
PROBES = 16
LEAVES_DEV = 32
NEAR_REACH = 8
FAR_REACH = 4
NEAR_COUNT = 9
FAR_LEAF = 27
FAR_BOX = 27
FAR_COLUMN = 4
BOXES = 128
COLUMNS = 32
CLUSTERS = 4096
POINT_TOTAL = 1048576
N_SUB = 4


def reflect_index(centre, offset, upper):
    target = centre + offset
    return jnp.where((target < 0) | (target >= upper), centre - offset, target)


def draw_near_list(key, part):
    key = jax.random.fold_in(key, 11)
    key_offset, key_count = jax.random.split(key)
    leaves = jnp.arange(CLUSTERS, dtype=jnp.int32)[:, None]
    column = jnp.arange(NEAR_COUNT, dtype=jnp.int32)[None, :]
    offset = jax.random.randint(key_offset, (CLUSTERS, NEAR_COUNT), -NEAR_REACH, NEAR_REACH + 1, dtype=jnp.int32)
    offset = jnp.where(column == 0, 0, offset)
    offset = jnp.where(column == 1, NEAR_REACH, offset)
    source = reflect_index(leaves, offset, CLUSTERS)
    count = jax.random.randint(key_count, (CLUSTERS, 1), 4, NEAR_COUNT + 1, dtype=jnp.int32)
    count = jnp.where(leaves % LEAVES_DEV == 0, NEAR_COUNT, count)
    return jnp.where(column < count, source, -1).astype(jnp.int32)


def draw_far_list(key, part):
    key = jax.random.fold_in(key, 23)
    key_offset, key_leaf, key_count = jax.random.split(key, 3)
    leaves = jnp.arange(CLUSTERS, dtype=jnp.int32)[:, None]
    column = jnp.arange(FAR_LEAF, dtype=jnp.int32)[None, :]
    offset = jax.random.randint(key_offset, (CLUSTERS, FAR_LEAF), -FAR_REACH, FAR_REACH + 1, dtype=jnp.int32)
    offset = jnp.where(column == 0, FAR_REACH, offset)
    source_box = reflect_index(leaves // LEAVES_DEV, offset, BOXES)
    source = source_box * LEAVES_DEV + jax.random.randint(key_leaf, (CLUSTERS, FAR_LEAF), 0, LEAVES_DEV, dtype=jnp.int32)
    count = jax.random.randint(key_count, (CLUSTERS, 1), FAR_LEAF // 2, FAR_LEAF + 1, dtype=jnp.int32)
    count = jnp.where(leaves % LEAVES_DEV == 0, FAR_LEAF, count)
    return jnp.where(column < count, source, -1).astype(jnp.int32)


def padded_list(key, rows, length, upper):
    key_source, key_count = jax.random.split(key)
    column = jnp.arange(length, dtype=jnp.int32)[None, :]
    source = jax.random.randint(key_source, (rows, length), 0, upper, dtype=jnp.int32)
    count = jax.random.randint(key_count, (rows, 1), length // 2, length + 1, dtype=jnp.int32)
    count = jnp.where(jnp.arange(rows, dtype=jnp.int32)[:, None] == 0, length, count)
    return jnp.where(column < count, source, -1).astype(jnp.int32)


def draw_box_list(key, part):
    key = jax.random.fold_in(key, 37)
    return padded_list(key, BOXES, FAR_BOX, BOXES)


def draw_column_list(key, part):
    key = jax.random.fold_in(key, 41)
    return padded_list(key, COLUMNS, FAR_COLUMN, COLUMNS)


def shard_levels(stream_key, shape, cuts, least, largest):
    def one(position, shards_of):
        steps = jax.random.uniform(jax.random.fold_in(jax.random.fold_in(stream_key, 6), position), (shards_of,), jnp.float32, least / len(cuts), largest / len(cuts))
        return jnp.repeat(jnp.exp(steps), shape[position] // shards_of).reshape((-1,) + (1,) * (len(shape) - position - 1))

    factor_of = one(*cuts[0])
    for cut in cuts[1:]:
        factor_of = factor_of * one(*cut)
    return factor_of


def normal_values(stream_key, shape, spread, bound, pieces=(), held_as=jnp.bfloat16):
    drawn = jax.random.normal(stream_key, shape, jnp.float32) * spread
    if len(pieces) > 0:
        drawn = shard_levels(stream_key, shape, pieces, -0.22, 0.18) * drawn
    return jnp.clip(drawn, min=-bound, max=bound).astype(held_as)


def setup_inputs(seed: int = 0) -> dict:
    splits = jax.random.split(jax.random.key(seed), 13)
    return {
        "points": jnp.clip(1.0 * jax.random.uniform(splits[0], (2, POINT_TOTAL), jnp.float32) ** shard_levels(splits[0], (2, POINT_TOTAL), ((1, 128),), -0.2, 0.2), 0.0, 1.0),
        "probes": normal_values(splits[1], (PROBES, POINT_TOTAL), 1.0, 6.0, ((1, 128),), jnp.float32),
        "basis": normal_values(splits[2], (CLUSTERS, LEAF, RANK), LEAF ** -0.5, 0.375, ((0, 128),), jnp.float32),
        "transfer_leaf": normal_values(splits[3], (CLUSTERS, RANK, RANK), (RANK * LEAVES_DEV) ** -0.5, 0.125, ((0, 128),), jnp.float32),
        "transfer_box": normal_values(splits[4], (BOXES, RANK, RANK), (RANK * N_SUB) ** -0.5, 0.375, ((0, 128),), jnp.float32),
        "couple_leaf": normal_values(splits[5], (CLUSTERS, FAR_LEAF, RANK, RANK), (RANK * FAR_LEAF) ** -0.5, 0.15625, ((0, 128),), jnp.float32),
        "couple_box": normal_values(splits[6], (BOXES, FAR_BOX, RANK, RANK), (RANK * FAR_BOX) ** -0.5, 0.15625, ((0, 128),), jnp.float32),
        "couple_column": normal_values(splits[7], (COLUMNS, FAR_COLUMN, RANK, RANK), (RANK * FAR_COLUMN) ** -0.5, 0.375, ((0, 32),), jnp.float32),
        "near_list": draw_near_list(jax.random.fold_in(splits[12], 71), 0),
        "far_list": draw_far_list(jax.random.fold_in(splits[12], 71), 0),
        "box_list": draw_box_list(jax.random.fold_in(splits[12], 71), 0),
        "column_list": draw_column_list(jax.random.fold_in(splits[12], 71), 0),
    }


topmost_level = lax.Precision.HIGHEST
matern_rate = math.sqrt(3.0) / 0.1

def matern_tiles(target_points, source_points):
    delta_x = target_points[:, None, 0, :, None] - source_points[:, :, 0, None, :]
    delta_y = target_points[:, None, 1, :, None] - source_points[:, :, 1, None, :]
    scaled = matern_rate * jnp.sqrt(delta_x * delta_x + delta_y * delta_y)
    return (1.0 + scaled) * jnp.exp(-scaled)

def near_field(target_points, source_points, source_values, present):
    kernel_tiles = matern_tiles(target_points, source_points) * present[:, :, None, None]
    return jnp.einsum('bkij,bkpj->bpi', kernel_tiles, source_values, precision=topmost_level)

def pick_rows(table, entries):
    present = entries >= 0
    chosen = table[jnp.where(present, entries, 0)]
    return chosen * present.astype(table.dtype)[:, :, None, None]

def reference(points, probes, basis, transfer_leaf, transfer_box, couple_leaf, couple_box, couple_column, near_list, far_list, box_list, column_list):
    cluster_points = points.reshape(2, CLUSTERS, LEAF).transpose(1, 0, 2)
    grouped_cluster_values = probes.reshape(PROBES, CLUSTERS, LEAF).transpose(1, 0, 2)
    skeleton_leaf = jnp.einsum('gyz,gzk->gyk', grouped_cluster_values, basis, precision=topmost_level)
    leaf_transfers = transfer_leaf.reshape(BOXES, LEAVES_DEV, RANK, RANK)
    skel_box = jnp.einsum('bcpr,bcrs->bps', skeleton_leaf.reshape(BOXES, LEAVES_DEV, PROBES, RANK), leaf_transfers, precision=topmost_level)
    box_term = jnp.einsum('bpr,brs->bps', skel_box, transfer_box, precision=topmost_level)
    skel_column = box_term.reshape(COLUMNS, N_SUB, PROBES, RANK).sum(axis=1)
    span_rows = 128

    def far_block(inputs):
        entries, couples = inputs
        return jnp.einsum('ckpr,ckrs->cps', pick_rows(skeleton_leaf, entries), couples, precision=topmost_level)
    far_leaf = lax.map(far_block, (far_list.reshape(CLUSTERS // span_rows, span_rows, FAR_LEAF), couple_leaf.reshape(CLUSTERS // span_rows, span_rows, FAR_LEAF, RANK, RANK))).reshape(CLUSTERS, PROBES, RANK)
    far_box = jnp.einsum('ckpr,ckrs->cps', pick_rows(skel_box, box_list), couple_box, precision=topmost_level)
    far_column = jnp.einsum('ckpr,ckrs->cps', pick_rows(skel_column, column_list), couple_column, precision=topmost_level)
    down_box = far_box + jnp.einsum('bps,brs->bpr', jnp.repeat(far_column, N_SUB, axis=0), transfer_box, precision=topmost_level)
    downward_leaf = far_leaf + jnp.einsum('bps,bcrs->bcpr', down_box, leaf_transfers, precision=topmost_level).reshape(CLUSTERS, PROBES, RANK)
    distant_values = jnp.einsum('wdq,wkq->wdk', downward_leaf, basis, precision=topmost_level)
    nearby_span = 16

    def near_block(inputs):
        target_list, entries = inputs
        present = entries >= 0
        safe = jnp.where(present, entries, 0)
        return near_field(target_list, cluster_points[safe], grouped_cluster_values[safe], present.astype(target_list.dtype))
    near_values = lax.map(near_block, (cluster_points.reshape(CLUSTERS // nearby_span, nearby_span, 2, LEAF), near_list.reshape(CLUSTERS // nearby_span, nearby_span, NEAR_COUNT))).reshape(CLUSTERS, PROBES, LEAF)
    return (distant_values + near_values).transpose(1, 0, 2).reshape(PROBES, POINT_TOTAL)
```

```python
import functools
import math

import jax
import jax.numpy as jnp
from jax import lax
from jax.experimental import pallas as pl
from jax.experimental.pallas import tpu as pltpu
from jax.sharding import PartitionSpec as P

NEAR_REACH = 8
FAR_REACH = 4
FEATURES = 16
GROUP = 8
FAR_STEP = 2

matern_rate = math.sqrt(3.0) / 0.1
coordinate_scale = matern_rate * math.log2(math.e)
ln2 = math.log(2.0)
tiny = 1e-20
f32 = jnp.float32
bf16 = jnp.bfloat16
vmem_bytes = 60 * 2**20
ring = ("leaf", "sub")


def halves(array):
    high = array.astype(bf16)
    return high, (array - high.astype(f32)).astype(bf16)


def stacked_halves(array):
    return jnp.concatenate(halves(array), axis=0)


def contract(left, right, dims):
    return lax.dot_general(left, right, (dims, ((), ())), preferred_element_type=f32)


def product3(left, right, dims=((1,), (0,))):
    rows = left.shape[0]
    high, low = halves(right)
    both = stacked_halves(left)
    wide = contract(both, high, dims)
    return wide[:rows] + wide[rows:] + contract(both[:rows], low, dims)


def skeleton_kernel(probes, basis, transfer_leaf, transfer_box, out):
    leaves, rank, leaf_size = basis.shape
    low_lanes = lax.broadcasted_iota(jnp.int32, (16, 2 * rank), 1) < rank

    def leaf_skeleton(c):
        both = stacked_halves(probes[:, c * leaf_size : (c + 1) * leaf_size])
        weights = stacked_halves(basis[c])
        wide = contract(both, weights, ((1,), (1,)))
        rolled = jnp.concatenate([wide[:16, rank:], wide[:16, :rank]], axis=1)
        return wide[:16] + wide[16:] + rolled

    box = jnp.zeros((16, rank), f32)
    for m in range(leaves // 2):
        even, odd = leaf_skeleton(2 * m), leaf_skeleton(2 * m + 1)
        odd = jnp.concatenate([odd[:, rank:], odd[:, :rank]], axis=1)
        pair = jnp.where(low_lanes, even, odd)
        out[m] = pair
        box += product3(pair, transfer_leaf[2 * m : 2 * m + 2].reshape(2 * rank, rank))
    term = product3(box, transfer_box[0])
    out[leaves // 2] = jnp.concatenate([box, term], axis=1)


def near_kernel(
    near, points, probes, left, right, out, values, source, target, total, item_c, item_s, item_w
):
    slots, leaves = near.shape
    leaf_size = target.shape[2]
    window = leaves + 2 * NEAR_REACH
    base = near[0, 0] - NEAR_REACH

    count = jnp.int32(0)
    for c in range(leaves):
        entries = [near[k, c] for k in range(slots)]
        for k in range(slots):
            new = entries[k] >= 0
            for j in range(k):
                new = new & (entries[j] != entries[k])
            times = jnp.float32(1.0)
            for j in range(k + 1, slots):
                times = times + jnp.where(entries[j] == entries[k], 1.0, 0.0)
            item_c[count] = c
            item_s[count] = entries[k] - base
            item_w[count] = times * ln2
            count = count + jnp.where(new, 1, 0)
    for u in range(GROUP):
        item_c[count + u] = 0
        item_s[count + u] = 0
        item_w[count + u] = 0.0

    ones = jnp.ones((3, leaf_size), f32)
    pad = jnp.zeros((2, leaf_size), f32)
    for w in range(window):
        own = NEAR_REACH <= w < NEAR_REACH + leaves
        if own:
            lanes = slice((w - NEAR_REACH) * leaf_size, (w - NEAR_REACH + 1) * leaf_size)
            place, value = points[:, lanes], probes[:, lanes]
        else:
            side = left if w < NEAR_REACH else right
            first = w if w < NEAR_REACH else w - NEAR_REACH - leaves
            lanes = slice(first * leaf_size, (first + 1) * leaf_size)
            place, value = side[16:18, lanes], side[0:16, lanes]
        values[w] = stacked_halves(value)
        scaled = (place - 0.5) * coordinate_scale
        first = scaled.astype(bf16).astype(f32)
        second = (scaled - first).astype(bf16).astype(f32)
        kept = first + second
        norm = kept[0:1] * kept[0:1] + kept[1:2] * kept[1:2]
        norm1 = norm.astype(bf16).astype(f32)
        rest = norm - norm1
        norm2 = rest.astype(bf16).astype(f32)
        norms = jnp.concatenate([norm1, norm2, rest - norm2], axis=0)
        rows = jnp.concatenate([first, second, first, second, norms, ones, pad], axis=0)
        source[w] = rows.T.astype(bf16)
        if own:
            target[w - NEAR_REACH] = jnp.concatenate(
                [-2.0 * first, -2.0 * first, -2.0 * second, -2.0 * second, ones, norms, pad], axis=0
            ).astype(bf16)
    total[...] = jnp.zeros_like(total)

    def tile(i):
        c, s, weight = item_c[i], item_s[i], item_w[i]
        squared = jnp.dot(source[s], target[c], preferred_element_type=f32)
        squared = jnp.maximum(squared, tiny)
        distance = squared * lax.rsqrt(squared)
        high, low = halves((distance + 1.0 / ln2) * jnp.exp2(-distance))
        both = values[s]
        wide = jnp.dot(both, high, preferred_element_type=f32)
        rest = jnp.dot(both[:16], low, preferred_element_type=f32)
        return c, (wide[:16] + wide[16:] + rest) * weight

    def group(t, carry):
        for c, term in [tile(t * GROUP + u) for u in range(GROUP)]:
            total[c] += term
        return carry

    lax.fori_loop(0, (count + GROUP - 1) // GROUP, group, 0)
    for c in range(leaves):
        out[:, c * leaf_size : (c + 1) * leaf_size] = total[c]


def fill_table(table, blocks, start):
    count, _, lanes = blocks.shape
    half = lanes // 2
    for m in range(count):
        block = blocks[m]
        swapped = jnp.concatenate([block[:, half:], block[:, :half]], axis=1)
        table[start + 2 * m] = stacked_halves(block)
        table[start + 2 * m + 1] = stacked_halves(swapped)


def picked(table, rows, low_lanes):
    pieces = []
    for k in range(0, len(rows) - 1, 2):
        pieces.append(jnp.where(low_lanes, table[rows[k]], table[rows[k + 1] ^ 1]))
    if len(rows) % 2:
        pieces.append(table[rows[-1]][:, : low_lanes.shape[1] // 2])
    return jnp.concatenate(pieces, axis=1)


def coupled(both, couples):
    count, rank, _ = couples.shape
    high, low = halves(couples.reshape(count * rank, rank))
    wide = jnp.dot(both, jnp.concatenate([high, low], axis=1), preferred_element_type=f32)
    return wide[:16, :rank] + wide[16:, :rank] + wide[:16, rank:]


def far_kernel(far, near, before, middle, after, couples, out, table):
    step = pl.program_id(0)
    per_step, slots, rank, _ = couples.shape
    leaves = far.shape[0]
    boxes = 2 * FAR_REACH + 1
    empty = boxes * leaves
    low_lanes = lax.broadcasted_iota(jnp.int32, (32, 2 * rank), 1) < rank

    @pl.when(step == 0)
    def _():
        for b in range(3):
            for place, blocks in ((b, before), (3 + b, middle), (6 + b, after)):
                fill_table(table, blocks.at[b, : leaves // 2], place * leaves)
        table[empty] = jnp.zeros_like(table[empty])
        table[empty + 1] = jnp.zeros_like(table[empty])

    base = near[0, 0] - FAR_REACH * leaves
    for u in range(per_step):
        c = step * per_step + u
        rows = [far[c, k] for k in range(slots)]
        rows = [jnp.where(row >= 0, row - base, empty) for row in rows]
        out[u] = coupled(picked(table, rows, low_lanes), couples[u])


def down_kernel(
    box_list,
    column_list,
    gathered,
    couple_box,
    couple_column,
    transfer_box,
    transfer_leaf,
    basis,
    far_leaf,
    near_values,
    out,
    table,
):
    leaves, rank, leaf_size = basis.shape
    boxes = gathered.shape[0]
    slots, column_slots = box_list.shape[1], column_list.shape[1]
    group_size = 4
    low_lanes = lax.broadcasted_iota(jnp.int32, (32, 2 * rank), 1) < rank

    def pick(row, present):
        block = gathered[jnp.where(present, row, 0)] * jnp.where(present, 1.0, 0.0)
        return block

    def swap(block):
        return jnp.concatenate([block[:, rank:], block[:, :rank]], axis=1)

    pieces = []
    for k in range(0, slots, 2):
        first = pick(box_list[0, k], box_list[0, k] >= 0)
        if k + 1 < slots:
            second = pick(box_list[0, k + 1], box_list[0, k + 1] >= 0)
            pieces.append(stacked_halves(jnp.where(low_lanes[:16], first, swap(second))))
        else:
            pieces.append(stacked_halves(first)[:, :rank])
    far_box = coupled(jnp.concatenate(pieces, axis=1), couple_box[0])

    columns = []
    for k in range(column_slots):
        row = column_list[0, k]
        start = jnp.where(row >= 0, row, 0) * group_size
        block = gathered[start]
        for j in range(1, group_size):
            block = block + gathered[start + j]
        columns.append(block * jnp.where(row >= 0, 1.0, 0.0))
    pieces = [
        stacked_halves(jnp.where(low_lanes[:16], swap(columns[k]), columns[k + 1]))
        for k in range(0, column_slots, 2)
    ]
    far_column = coupled(jnp.concatenate(pieces, axis=1), couple_column[0])
    down_box = far_box + product3(far_column, transfer_box[0], ((1,), (1,)))

    for c in range(leaves):
        down = far_leaf[c] + product3(down_box, transfer_leaf[c], ((1,), (1,)))
        lanes = slice(c * leaf_size, (c + 1) * leaf_size)
        out[:, lanes] = near_values[:, lanes] + product3(down, basis[c])


def whole(count):
    return [pl.BlockSpec(memory_space=pltpu.VMEM)] * count


def scalars(count):
    return [pl.BlockSpec(memory_space=pltpu.SMEM)] * count


params = pltpu.CompilerParams(vmem_limit_bytes=vmem_bytes)


def shifted(array, by):
    devices = lax.axis_size(ring)
    return lax.ppermute(array, ring, [(i, (i + by) % devices) for i in range(devices)])


def near_call(near_slots, points, probes, halo_left, halo_right):
    slots, leaves = near_slots.shape
    probe_count = probes.shape[0]
    leaf_size = probes.shape[1] // leaves
    window = leaves + 2 * NEAR_REACH
    items = leaves * slots + 2 * GROUP
    return pl.pallas_call(
        near_kernel,
        out_shape=jax.ShapeDtypeStruct(probes.shape, f32),
        in_specs=scalars(1) + whole(4),
        out_specs=pl.BlockSpec(memory_space=pltpu.VMEM),
        scratch_shapes=[
            pltpu.VMEM((window, 2 * probe_count, leaf_size), bf16),
            pltpu.VMEM((window, leaf_size, FEATURES), bf16),
            pltpu.VMEM((leaves, FEATURES, leaf_size), bf16),
            pltpu.VMEM((leaves, probe_count, leaf_size), f32),
        ]
        + [pltpu.SMEM((items,), dtype) for dtype in (jnp.int32, jnp.int32, f32)],
        compiler_params=params,
        cost_estimate=pl.CostEstimate(flops=20_000_000_000, bytes_accessed=2**22, transcendentals=0),
        name="near",
    )(near_slots, points, probes, halo_left, halo_right)


def per_device(
    points,
    probes,
    basis,
    transfer_leaf,
    transfer_box,
    couple_leaf,
    couple_box,
    couple_column,
    near_list,
    far_list,
    box_list,
    column_list,
):
    leaves, leaf_size, rank = basis.shape
    probe_count = probes.shape[0]
    reach = NEAR_REACH * leaf_size
    near_slots = near_list.T
    basis = basis.transpose(0, 2, 1)

    blocks = leaves // 2 + 1
    skeletons = pl.pallas_call(
        skeleton_kernel,
        out_shape=jax.ShapeDtypeStruct((blocks, probe_count, 2 * rank), f32),
        in_specs=whole(4),
        out_specs=pl.BlockSpec(memory_space=pltpu.VMEM),
        compiler_params=params,
        name="skeletons",
    )(probes, basis, transfer_leaf, transfer_box)

    stacked = jnp.concatenate([probes, points], axis=0)
    halo_left = shifted(stacked[:, -reach:], 1)
    halo_right = shifted(stacked[:, :reach], -1)

    middle = jnp.stack([shifted(skeletons, 1), skeletons, shifted(skeletons, -1)])
    before, after = shifted(middle, 3), shifted(middle, -3)

    sub = lax.axis_index("sub")
    window = jnp.concatenate([before[:, -1], middle[:, -1], after[:, -1]])
    column = lax.dynamic_slice_in_dim(window, FAR_REACH - sub, lax.axis_size("sub"), 0)
    gathered = lax.all_gather(column, "leaf", axis=0, tiled=True)

    near_values = near_call(near_slots, points, probes, halo_left, halo_right)

    boxes = 2 * FAR_REACH + 1
    three = pl.BlockSpec((3, blocks, probe_count, 2 * rank), lambda i: (0, 0, 0, 0))
    far_leaf = pl.pallas_call(
        far_kernel,
        grid=(leaves // FAR_STEP,),
        out_shape=jax.ShapeDtypeStruct((leaves, probe_count, rank), f32),
        in_specs=scalars(2)
        + [three] * 3
        + [pl.BlockSpec((FAR_STEP,) + couple_leaf.shape[1:], lambda i: (i, 0, 0, 0))],
        out_specs=pl.BlockSpec((FAR_STEP, probe_count, rank), lambda i: (i, 0, 0)),
        scratch_shapes=[pltpu.VMEM((boxes * leaves + 2, 2 * probe_count, 2 * rank), bf16)],
        compiler_params=params,
        cost_estimate=pl.CostEstimate(flops=5_000_000_000, bytes_accessed=2**25, transcendentals=0),
        name="far",
    )(far_list, near_slots, before, middle, after, couple_leaf)

    return pl.pallas_call(
        down_kernel,
        out_shape=jax.ShapeDtypeStruct(probes.shape, f32),
        in_specs=scalars(2) + whole(8),
        out_specs=pl.BlockSpec(memory_space=pltpu.VMEM),
        scratch_shapes=[pltpu.VMEM((8, 128), f32)],
        compiler_params=params,
        name="down",
    )(
        box_list,
        column_list,
        gathered,
        couple_box,
        couple_column,
        transfer_box,
        transfer_leaf,
        basis,
        far_leaf,
        near_values,
    )


def solution(mesh):
    placed = (
        P(None, ring),
        P(None, ring),
        P(ring, None, None),
        P(ring, None, None),
        P(ring, None, None),
        P(ring, None, None, None),
        P(ring, None, None, None),
        P("leaf", None, None, None),
        P(ring, None),
        P(ring, None),
        P(ring, None),
        P("leaf", None),
    )
    return jax.shard_map(
        per_device, mesh=mesh, in_specs=placed, out_specs=P(None, ring), check_vma=False
    )
```

```python
import functools
import math

import jax
import jax.numpy as jnp
from jax import lax
from jax.experimental import pallas as pl
from jax.experimental.pallas import tpu as pltpu
from jax.sharding import PartitionSpec as P

NEAR_REACH = 8
FAR_REACH = 4
FEATURES = 16
GROUP = 8
FAR_STEP = 2

matern_rate = math.sqrt(3.0) / 0.1
coordinate_scale = matern_rate * math.log2(math.e)
ln2 = math.log(2.0)
tiny = 1e-20
f32 = jnp.float32
bf16 = jnp.bfloat16
vmem_bytes = 60 * 2**20
ring = ("leaf", "sub")


def halves(array):
    high = array.astype(bf16)
    return high, (array - high.astype(f32)).astype(bf16)


def stacked_halves(array):
    return jnp.concatenate(halves(array), axis=0)


def contract(left, right, dims):
    return lax.dot_general(left, right, (dims, ((), ())), preferred_element_type=f32)


def product3(left, right, dims=((1,), (0,))):
    rows = left.shape[0]
    high, low = halves(right)
    both = stacked_halves(left)
    wide = contract(both, high, dims)
    return wide[:rows] + wide[rows:] + contract(both[:rows], low, dims)


def exchanged(block):
    half = block.shape[1] // 2
    return jnp.concatenate([block[:, half:], block[:, :half]], axis=1)


def skeleton_kernel(near, points, probes, basis, transfer_leaf, transfer_box, out, box_out, items):
    leaves, rank, leaf_size = basis.shape
    slots = near.shape[0]
    pairs = leaves // 2
    low_lanes = lax.broadcasted_iota(jnp.int32, (16, 2 * rank), 1) < rank

    leaf = lax.broadcasted_iota(jnp.int32, (1, leaves), 1)
    rows = [near[k : k + 1, :] for k in range(slots)]
    for k in range(slots):
        new = rows[k] >= 0
        times = jnp.ones_like(leaf)
        for j in range(k):
            new = new & (rows[j] != rows[k])
        for j in range(k + 1, slots):
            times = times + jnp.where(rows[j] == rows[k], 1, 0)
        place = rows[k] - rows[0] + leaf + NEAR_REACH
        items[k : k + 1, :] = jnp.where(new, leaf + place * 64 + times * 4096, 0)

    width = probes.shape[1]
    edge = NEAR_REACH * leaf_size
    for side, start in ((0, width - edge), (1, 0)):
        for j in range(edge // 128):
            lanes = slice(start + j * 128, start + (j + 1) * 128)
            out[side, pairs + j] = probes[:, lanes]
            out[side, pairs + edge // 128, j : j + 1, :] = points[0:1, lanes]
            out[side, pairs + edge // 128 + 1, j : j + 1, :] = points[1:2, lanes]

    def leaf_skeleton(c):
        both = stacked_halves(probes[:, c * leaf_size : (c + 1) * leaf_size])
        weights = stacked_halves(basis[c])
        wide = contract(both, weights, ((1,), (1,)))
        return wide[:16] + wide[16:] + exchanged(wide[:16])

    box = jnp.zeros((16, rank), f32)
    for m in range(pairs):
        pair = jnp.where(low_lanes, leaf_skeleton(2 * m), exchanged(leaf_skeleton(2 * m + 1)))
        out[0, m] = pair
        out[1, m] = pair
        box += product3(pair, transfer_leaf[2 * m : 2 * m + 2].reshape(2 * rank, rank))
    box_out[...] = jnp.concatenate([box, product3(box, transfer_box[0])], axis=1)


def near_kernel(
    items, points, probes, left, right, out, values, source, target, total, listed, *, groups
):
    slots, leaves = items.shape
    leaf_size = target.shape[2]
    pieces = leaf_size // 128
    pairs = leaves // 2
    edge_blocks = NEAR_REACH * pieces

    count = jnp.int32(0)
    for begin, end in groups:
        for c in range(begin, end):
            for k in range(slots):
                item = items[k, c]
                listed[count] = item
                count = count + jnp.where(item != 0, 1, 0)
    for u in range(GROUP):
        listed[count + u] = groups[0][0] + NEAR_REACH * 64

    ones = jnp.ones((3, leaf_size), f32)
    pad = jnp.zeros((2, leaf_size), f32)
    window = sorted({w for begin, end in groups for w in range(begin, end + 2 * NEAR_REACH)})
    for w in window:
        own = NEAR_REACH <= w < NEAR_REACH + leaves
        if own:
            lanes = slice((w - NEAR_REACH) * leaf_size, (w - NEAR_REACH + 1) * leaf_size)
            place, value = points[:, lanes], probes[:, lanes]
        else:
            side = left if w < NEAR_REACH else right
            first = (w if w < NEAR_REACH else w - NEAR_REACH - leaves) * pieces
            parts = range(first, first + pieces)
            value = jnp.concatenate([side[pairs + j] for j in parts], axis=1)
            place = jnp.concatenate(
                [
                    jnp.concatenate(
                        [side[pairs + edge_blocks + d, j : j + 1, :] for j in parts], axis=1
                    )
                    for d in range(2)
                ],
                axis=0,
            )
        values[w] = stacked_halves(value)
        scaled = (place - 0.5) * coordinate_scale
        first = scaled.astype(bf16).astype(f32)
        second = (scaled - first).astype(bf16).astype(f32)
        kept = first + second
        norm = kept[0:1] * kept[0:1] + kept[1:2] * kept[1:2]
        norm1 = norm.astype(bf16).astype(f32)
        rest = norm - norm1
        norm2 = rest.astype(bf16).astype(f32)
        norms = jnp.concatenate([norm1, norm2, rest - norm2], axis=0)
        rows = jnp.concatenate([first, second, first, second, norms, ones, pad], axis=0)
        source[w] = rows.T.astype(bf16)
        if own and any(begin <= w - NEAR_REACH < end for begin, end in groups):
            target[w - NEAR_REACH] = jnp.concatenate(
                [-2.0 * first, -2.0 * first, -2.0 * second, -2.0 * second, ones, norms, pad], axis=0
            ).astype(bf16)
    total[...] = jnp.zeros_like(total)

    def tile(i):
        item = listed[i]
        c, s, times = item & 63, (item >> 6) & 63, item >> 12
        squared = jnp.dot(source[s], target[c], preferred_element_type=f32)
        squared = jnp.maximum(squared, tiny)
        distance = squared * lax.rsqrt(squared)
        high, low = halves((distance + 1.0 / ln2) * jnp.exp2(-distance))
        both = values[s]
        wide = jnp.dot(both, high, preferred_element_type=f32)
        rest = jnp.dot(both[:16], low, preferred_element_type=f32)
        return c, (wide[:16] + wide[16:] + rest) * (times.astype(f32) * ln2)

    def group(t, carry):
        for c, term in [tile(t * GROUP + u) for u in range(GROUP)]:
            total[c] += term
        return carry

    lax.fori_loop(0, (count + GROUP - 1) // GROUP, group, 0)
    place = 0
    for begin, end in groups:
        for c in range(begin, end):
            out[:, place * leaf_size : (place + 1) * leaf_size] = total[c]
            place += 1


def fill_table(table, blocks, start):
    count, _, lanes = blocks.shape
    half = lanes // 2
    for m in range(count):
        block = blocks[m]
        swapped = jnp.concatenate([block[:, half:], block[:, :half]], axis=1)
        table[start + 2 * m] = stacked_halves(block)
        table[start + 2 * m + 1] = stacked_halves(swapped)


def picked(table, rows, low_lanes):
    pieces = []
    for k in range(0, len(rows) - 1, 2):
        pieces.append(jnp.where(low_lanes, table[rows[k]], table[rows[k + 1] ^ 1]))
    if len(rows) % 2:
        pieces.append(table[rows[-1]][:, : low_lanes.shape[1] // 2])
    return jnp.concatenate(pieces, axis=1)


def coupled_pairs(picks, couples):
    slots, rank, _ = couples.shape
    result = jnp.zeros((16, rank), f32)
    low_lanes = lax.broadcasted_iota(jnp.int32, (rank, 2 * rank), 1) < rank
    for start in range(0, slots, 8):
        pairs = (min(slots - start, 8) + 1) // 2
        highs, lows = [], []
        for m in range(pairs):
            even = couples[start + m]
            if start + pairs + m < slots:
                odd = couples[start + pairs + m]
            else:
                odd = jnp.zeros_like(even)
            high, low = halves(jnp.concatenate([even, odd], axis=1))
            highs.append(high)
            lows.append(low)
        right = jnp.concatenate(
            [jnp.concatenate(highs, axis=0), jnp.concatenate(lows, axis=0)], axis=1
        )
        left = jnp.concatenate(
            [picks(start, pairs), picks(start + pairs, pairs)], axis=0
        )
        wide = jnp.dot(left, right, preferred_element_type=f32)
        first = wide[:16, : 2 * rank] + wide[16:32, : 2 * rank] + wide[:16, 2 * rank :]
        second = wide[32:48, : 2 * rank] + wide[48:, : 2 * rank] + wide[32:48, 2 * rank :]
        result = result + first[:, :rank] + second[:, rank:]
    return result


def coupled(both, couples):
    count, rank, _ = couples.shape
    high, low = halves(couples.reshape(count * rank, rank))
    wide = jnp.dot(both, jnp.concatenate([high, low], axis=1), preferred_element_type=f32)
    return wide[:16, :rank] + wide[16:, :rank] + wide[:16, rank:]


def far_kernel(far, near, before, middle, after, couples, out, table):
    step = pl.program_id(0)
    per_step, slots, rank, _ = couples.shape
    leaves = far.shape[0]
    empty = (2 * FAR_REACH + 1) * leaves
    low_lanes = lax.broadcasted_iota(jnp.int32, (32, 2 * rank), 1) < rank

    @pl.when(step == 0)
    def _():
        for b in range(3):
            for place, blocks in ((b, before), (3 + b, middle), (6 + b, after)):
                fill_table(table, blocks.at[b], place * leaves)
        table[empty] = jnp.zeros_like(table[empty])
        table[empty + 1] = jnp.zeros_like(table[empty])

    base = near[0, 0] - FAR_REACH * leaves
    for u in range(per_step):
        c = step * per_step + u

        def picks(start, count):
            rows = [far[c, k] if k < slots else -1 for k in range(start, start + count)]
            rows = [jnp.where(row >= 0, row - base, empty) for row in rows]
            return picked(table, rows, low_lanes)

        out[u] = coupled_pairs(picks, couples[u])


def down_kernel(
    near,
    box_list,
    column_list,
    gathered,
    couple_box,
    couple_column,
    transfer_box,
    transfer_leaf,
    basis,
    far_leaf,
    near_inner,
    near_outer,
    out,
):
    leaves, rank, leaf_size = basis.shape
    slots, column_slots = box_list.shape[1], column_list.shape[1]
    group_size = 4
    low_lanes = lax.broadcasted_iota(jnp.int32, (32, 2 * rank), 1) < rank

    sub = (near[0, 0] // leaves) & (group_size - 1)

    def box_row(entry):
        entry = jnp.where(entry >= 0, entry, 0)
        return entry - (entry & (group_size - 1)) + ((entry - sub) & (group_size - 1))

    def pick(k):
        entry = box_list[0, k]
        return gathered[box_row(entry)] * jnp.where(entry >= 0, 1.0, 0.0)

    pieces = []
    for k in range(0, slots, 2):
        if k + 1 < slots:
            pieces.append(stacked_halves(jnp.where(low_lanes[:16], pick(k), exchanged(pick(k + 1)))))
        else:
            pieces.append(stacked_halves(pick(k))[:, :rank])
    far_box = coupled(jnp.concatenate(pieces, axis=1), couple_box[0])

    columns = []
    for k in range(column_slots):
        row = column_list[0, k]
        start = jnp.where(row >= 0, row, 0) * group_size
        block = gathered[start]
        for j in range(1, group_size):
            block = block + gathered[start + j]
        columns.append(block * jnp.where(row >= 0, 1.0, 0.0))
    pieces = [
        stacked_halves(jnp.where(low_lanes[:16], exchanged(columns[k]), columns[k + 1]))
        for k in range(0, column_slots, 2)
    ]
    far_column = coupled(jnp.concatenate(pieces, axis=1), couple_column[0])
    down_box = far_box + product3(far_column, transfer_box[0], ((1,), (1,)))

    for c in range(leaves):
        down = far_leaf[c] + product3(down_box, transfer_leaf[c], ((1,), (1,)))
        lanes = slice(c * leaf_size, (c + 1) * leaf_size)
        inner = NEAR_REACH <= c < leaves - NEAR_REACH
        place = c - NEAR_REACH if inner else c if c < NEAR_REACH else c - leaves + 2 * NEAR_REACH
        held = near_inner if inner else near_outer
        near_value = held[:, place * leaf_size : (place + 1) * leaf_size]
        out[:, lanes] = near_value + product3(down, basis[c])


def whole(count):
    return [pl.BlockSpec(memory_space=pltpu.VMEM)] * count


def scalars(count):
    return [pl.BlockSpec(memory_space=pltpu.SMEM)] * count


def params(mebibytes):
    return pltpu.CompilerParams(vmem_limit_bytes=mebibytes * 2**20)


def cost(flops):
    return pl.CostEstimate(flops=flops, bytes_accessed=2**20, transcendentals=0)


def shifted(array, axis, by):
    devices = lax.axis_size(axis)
    return lax.ppermute(array, axis, [(i, (i + by) % devices) for i in range(devices)])


def near_call(name, groups, items, points, probes, left, right):
    slots, leaves = items.shape
    probe_count = probes.shape[0]
    leaf_size = probes.shape[1] // leaves
    window = leaves + 2 * NEAR_REACH
    width = sum(end - begin for begin, end in groups) * leaf_size
    return pl.pallas_call(
        functools.partial(near_kernel, groups=groups),
        out_shape=jax.ShapeDtypeStruct((probe_count, width), f32),
        in_specs=scalars(1) + whole(4),
        out_specs=pl.BlockSpec(memory_space=pltpu.VMEM),
        scratch_shapes=[
            pltpu.VMEM((window, 2 * probe_count, leaf_size), bf16),
            pltpu.VMEM((window, leaf_size, FEATURES), bf16),
            pltpu.VMEM((leaves, FEATURES, leaf_size), bf16),
            pltpu.VMEM((leaves, probe_count, leaf_size), f32),
            pltpu.SMEM((leaves * slots + 2 * GROUP,), jnp.int32),
        ],
        compiler_params=params(14),
        cost_estimate=cost(10_000_000_000),
        name=name,
    )(items, points, probes, left, right)


def per_device(
    points,
    probes,
    basis,
    transfer_leaf,
    transfer_box,
    couple_leaf,
    couple_box,
    couple_column,
    near_list,
    far_list,
    box_list,
    column_list,
):
    leaves, leaf_size, rank = basis.shape
    probe_count = probes.shape[0]
    near_slots = near_list.T
    basis = basis.transpose(0, 2, 1)
    pairs = leaves // 2
    blocks = pairs + NEAR_REACH * leaf_size // 128 + 2

    bundles, box, items = pl.pallas_call(
        skeleton_kernel,
        out_shape=(
            jax.ShapeDtypeStruct((2, blocks, probe_count, 2 * rank), f32),
            jax.ShapeDtypeStruct((probe_count, 2 * rank), f32),
            jax.ShapeDtypeStruct(near_slots.shape, jnp.int32),
        ),
        in_specs=whole(6),
        out_specs=tuple(whole(3)),
        compiler_params=params(14),
        name="skeletons",
    )(near_slots, points, probes, basis, transfer_leaf, transfer_box)

    box_next, box_last = shifted(box, "sub", -1), shifted(box, "sub", 1)
    box_second = shifted(box_next, "sub", -1)
    column = jnp.stack([box, box_next, box_second, box_last])
    gathered = lax.all_gather(column, "leaf", axis=0, tiled=True)

    left, right = shifted(bundles[0], ring, 1), shifted(bundles[1], ring, -1)
    near_inner = near_call(
        "near_inner", ((NEAR_REACH, leaves - NEAR_REACH),), items, points, probes, box, box
    )
    middle = jnp.stack([left[:pairs], bundles[0, :pairs], right[:pairs]])
    before, after = shifted(middle, ring, 3), shifted(middle, ring, -3)
    near_outer = near_call(
        "near_outer",
        ((0, NEAR_REACH), (leaves - NEAR_REACH, leaves)),
        items,
        points,
        probes,
        left,
        right,
    )

    three = pl.BlockSpec(middle.shape, lambda i: (0, 0, 0, 0))
    far_leaf = pl.pallas_call(
        far_kernel,
        grid=(leaves // FAR_STEP,),
        out_shape=jax.ShapeDtypeStruct((leaves, probe_count, rank), f32),
        in_specs=scalars(2)
        + [three] * 3
        + [pl.BlockSpec((FAR_STEP,) + couple_leaf.shape[1:], lambda i: (i, 0, 0, 0))],
        out_specs=pl.BlockSpec((FAR_STEP, probe_count, rank), lambda i: (i, 0, 0)),
        scratch_shapes=[
            pltpu.VMEM(
                ((2 * FAR_REACH + 1) * leaves + 2, 2 * probe_count, 2 * rank), bf16
            )
        ],
        compiler_params=params(20),
        cost_estimate=cost(5_000_000_000),
        name="far",
    )(far_list, near_slots, before, middle, after, couple_leaf)

    return pl.pallas_call(
        down_kernel,
        out_shape=jax.ShapeDtypeStruct(probes.shape, f32),
        in_specs=scalars(3) + whole(9),
        out_specs=pl.BlockSpec(memory_space=pltpu.VMEM),
        compiler_params=params(14),
        name="down",
    )(
        near_slots,
        box_list,
        column_list,
        gathered,
        couple_box,
        couple_column,
        transfer_box,
        transfer_leaf,
        basis,
        far_leaf,
        near_inner,
        near_outer,
    )


def solution(mesh):
    placed = (
        P(None, ring),
        P(None, ring),
        P(ring, None, None),
        P(ring, None, None),
        P(ring, None, None),
        P(ring, None, None, None),
        P(ring, None, None, None),
        P("leaf", None, None, None),
        P(ring, None),
        P(ring, None),
        P(ring, None),
        P("leaf", None),
    )
    return jax.shard_map(
        per_device, mesh=mesh, in_specs=placed, out_specs=P(None, ring), check_vma=False
    )
```

```python
import functools
import math

import jax
import jax.numpy as jnp
from jax import lax
from jax.experimental import pallas as pl
from jax.experimental.pallas import tpu as pltpu
from jax.sharding import PartitionSpec as P

NEAR_REACH = 8
FAR_REACH = 4
FEATURES = 16
GROUP = 12
FAR_STEP = 2
CHUNKS = 4

matern_rate = math.sqrt(3.0) / 0.1
coordinate_scale = matern_rate * math.log2(math.e)
ln2 = math.log(2.0)
tiny = 1e-20
f32 = jnp.float32
bf16 = jnp.bfloat16
vmem_bytes = 60 * 2**20
ring = ("leaf", "sub")


def halves(array):
    high = array.astype(bf16)
    return high, (array - high.astype(f32)).astype(bf16)


def stacked_halves(array):
    return jnp.concatenate(halves(array), axis=0)


def contract(left, right, dims):
    return lax.dot_general(left, right, (dims, ((), ())), preferred_element_type=f32)


def product3(left, right, dims=((1,), (0,))):
    rows = left.shape[0]
    high, low = halves(right)
    both = stacked_halves(left)
    wide = contract(both, high, dims)
    return wide[:rows] + wide[rows:] + contract(both[:rows], low, dims)


def copies(pairs, semaphores):
    made = [
        pltpu.make_async_copy(source, held, semaphores.at[i])
        for i, (source, held) in enumerate(pairs)
    ]
    for copy in made:
        copy.start()
    return made


def parts(source, held):
    length = source.shape[0] // CHUNKS
    runs = [pl.ds(i * length, length) for i in range(CHUNKS)]
    return [(source.at[run], held.at[run]) for run in runs]


def exchanged(block):
    half = block.shape[1] // 2
    return jnp.concatenate([block[:, half:], block[:, :half]], axis=1)


def skeleton_kernel(
    near, points, probes_in, basis_in, transfer_in, transfer_box, out, box_out, items,
    probes, basis, transfer_leaf, semaphores,
):
    leaves, rank, leaf_size = basis.shape
    arriving = copies(
        [(probes_in, probes)] + parts(basis_in, basis) + parts(transfer_in, transfer_leaf),
        semaphores,
    )
    slots = near.shape[0]
    pairs = leaves // 2
    low_lanes = lax.broadcasted_iota(jnp.int32, (16, 2 * rank), 1) < rank

    leaf = lax.broadcasted_iota(jnp.int32, (1, leaves), 1)
    rows = [near[k : k + 1, :] for k in range(slots)]
    for k in range(slots):
        new = rows[k] >= 0
        times = jnp.ones_like(leaf)
        for j in range(k):
            new = new & (rows[j] != rows[k])
        for j in range(k + 1, slots):
            times = times + jnp.where(rows[j] == rows[k], 1, 0)
        place = rows[k] - rows[0] + leaf + NEAR_REACH
        items[k : k + 1, :] = jnp.where(new, leaf + place * 64 + times * 4096, 0)

    arriving[0].wait()
    width = probes.shape[1]
    edge = NEAR_REACH * leaf_size
    for side, start in ((0, width - edge), (1, 0)):
        for j in range(edge // 128):
            lanes = slice(start + j * 128, start + (j + 1) * 128)
            out[side, pairs + j] = probes[:, lanes]
            out[side, pairs + edge // 128, j : j + 1, :] = points[0:1, lanes]
            out[side, pairs + edge // 128 + 1, j : j + 1, :] = points[1:2, lanes]

    def leaf_skeleton(c):
        both = stacked_halves(probes[:, c * leaf_size : (c + 1) * leaf_size])
        weights = stacked_halves(basis[c])
        wide = contract(both, weights, ((1,), (1,)))
        return wide[:16] + wide[16:] + exchanged(wide[:16])

    box = jnp.zeros((16, rank), f32)
    for m in range(pairs):
        if m % (pairs // CHUNKS) == 0:
            arriving[1 + m // (pairs // CHUNKS)].wait()
            arriving[1 + CHUNKS + m // (pairs // CHUNKS)].wait()
        pair = jnp.where(low_lanes, leaf_skeleton(2 * m), exchanged(leaf_skeleton(2 * m + 1)))
        out[0, m] = pair
        out[1, m] = pair
        box += product3(pair, transfer_leaf[2 * m : 2 * m + 2].reshape(2 * rank, rank))
    box_out[0] = jnp.concatenate([box, product3(box, transfer_box[0])], axis=1)


def near_kernel(
    items, points, probes, left, right, out, values, source, target, total, listed, *, groups
):
    slots, leaves = items.shape
    leaf_size = target.shape[2]
    pieces = leaf_size // 128
    pairs = leaves // 2
    edge_blocks = NEAR_REACH * pieces

    count = jnp.int32(0)
    for begin, end in groups:
        for c in range(begin, end):
            for k in range(slots):
                item = items[k, c]
                listed[count] = item
                count = count + jnp.where(item != 0, 1, 0)
    for u in range(GROUP):
        listed[count + u] = groups[0][0] + NEAR_REACH * 64

    ones = jnp.ones((3, leaf_size), f32)
    pad = jnp.zeros((2, leaf_size), f32)
    window = sorted({w for begin, end in groups for w in range(begin, end + 2 * NEAR_REACH)})
    for w in window:
        own = NEAR_REACH <= w < NEAR_REACH + leaves
        if own:
            lanes = slice((w - NEAR_REACH) * leaf_size, (w - NEAR_REACH + 1) * leaf_size)
            place, value = points[:, lanes], probes[:, lanes]
        else:
            side = left if w < NEAR_REACH else right
            first = (w if w < NEAR_REACH else w - NEAR_REACH - leaves) * pieces
            parts = range(first, first + pieces)
            value = jnp.concatenate([side[pairs + j] for j in parts], axis=1)
            place = jnp.concatenate(
                [
                    jnp.concatenate(
                        [side[pairs + edge_blocks + d, j : j + 1, :] for j in parts], axis=1
                    )
                    for d in range(2)
                ],
                axis=0,
            )
        values[w] = stacked_halves(value)
        scaled = (place - 0.5) * coordinate_scale
        first = scaled.astype(bf16).astype(f32)
        second = (scaled - first).astype(bf16).astype(f32)
        kept = first + second
        norm = kept[0:1] * kept[0:1] + kept[1:2] * kept[1:2]
        norm1 = norm.astype(bf16).astype(f32)
        rest = norm - norm1
        norm2 = rest.astype(bf16).astype(f32)
        norms = jnp.concatenate([norm1, norm2, rest - norm2], axis=0)
        rows = jnp.concatenate([first, second, first, second, norms, ones, pad], axis=0)
        source[w] = rows.T.astype(bf16)
        if own and any(begin <= w - NEAR_REACH < end for begin, end in groups):
            target[w - NEAR_REACH] = jnp.concatenate(
                [-2.0 * first, -2.0 * first, -2.0 * second, -2.0 * second, ones, norms, pad], axis=0
            ).astype(bf16)
    total[...] = jnp.zeros_like(total)

    def tile(i):
        item = listed[i]
        c, s, times = item & 63, (item >> 6) & 63, item >> 12
        squared = jnp.dot(source[s], target[c], preferred_element_type=f32)
        squared = jnp.maximum(squared, tiny)
        distance = squared * lax.rsqrt(squared)
        high, low = halves((distance + 1.0 / ln2) * jnp.exp2(-distance))
        both = values[s]
        wide = jnp.dot(both, high, preferred_element_type=f32)
        rest = jnp.dot(both[:16], low, preferred_element_type=f32)
        return c, (wide[:16] + wide[16:] + rest) * (times.astype(f32) * ln2)

    def group(t, carry):
        for c, term in [tile(t * GROUP + u) for u in range(GROUP)]:
            total[c] += term
        return carry

    lax.fori_loop(0, (count + GROUP - 1) // GROUP, group, 0)
    place = 0
    for begin, end in groups:
        for c in range(begin, end):
            out[:, place * leaf_size : (place + 1) * leaf_size] = total[c]
            place += 1


def fill_table(table, blocks, start):
    count, _, lanes = blocks.shape
    half = lanes // 2
    for m in range(count):
        block = blocks[m]
        swapped = jnp.concatenate([block[:, half:], block[:, :half]], axis=1)
        table[start + 2 * m] = stacked_halves(block)
        table[start + 2 * m + 1] = stacked_halves(swapped)


def picked(table, rows, low_lanes):
    pieces = []
    for k in range(0, len(rows) - 1, 2):
        pieces.append(jnp.where(low_lanes, table[rows[k]], table[rows[k + 1] ^ 1]))
    if len(rows) % 2:
        pieces.append(table[rows[-1]][:, : low_lanes.shape[1] // 2])
    return jnp.concatenate(pieces, axis=1)


def coupled_pairs(picks, couples):
    slots, rank, _ = couples.shape
    result = jnp.zeros((16, rank), f32)
    low_lanes = lax.broadcasted_iota(jnp.int32, (rank, 2 * rank), 1) < rank
    for start in range(0, slots, 8):
        pairs = (min(slots - start, 8) + 1) // 2
        highs, lows = [], []
        for m in range(pairs):
            even = couples[start + m]
            if start + pairs + m < slots:
                odd = couples[start + pairs + m]
            else:
                odd = jnp.zeros_like(even)
            high, low = halves(jnp.concatenate([even, odd], axis=1))
            highs.append(high)
            lows.append(low)
        right = jnp.concatenate(
            [jnp.concatenate(highs, axis=0), jnp.concatenate(lows, axis=0)], axis=1
        )
        left = jnp.concatenate(
            [picks(start, pairs), picks(start + pairs, pairs)], axis=0
        )
        wide = jnp.dot(left, right, preferred_element_type=f32)
        first = wide[:16, : 2 * rank] + wide[16:32, : 2 * rank] + wide[:16, 2 * rank :]
        second = wide[32:48, : 2 * rank] + wide[48:, : 2 * rank] + wide[32:48, 2 * rank :]
        result = result + first[:, :rank] + second[:, rank:]
    return result


def coupled(both, couples):
    count, rank, _ = couples.shape
    high, low = halves(couples.reshape(count * rank, rank))
    wide = jnp.dot(both, jnp.concatenate([high, low], axis=1), preferred_element_type=f32)
    return wide[:16, :rank] + wide[16:, :rank] + wide[:16, rank:]


def outer_kernel(
    items, far, near, points, probes, left, right, before, middle, after, couples_in,
    out, far_out, values, source, target, total, listed, table, couples, semaphores, *, groups
):
    leaves, slots, rank, _ = couples.shape
    steps = leaves // FAR_STEP

    def arriving(step):
        run = pl.ds(step * FAR_STEP, FAR_STEP)
        return pltpu.make_async_copy(couples_in.at[run], couples.at[run], semaphores.at[step])

    def start(step, carry):
        arriving(step).start()
        return carry

    lax.fori_loop(0, steps, start, 0)
    near_kernel(
        items, points, probes, left, right, out, values, source, target, total, listed, groups=groups
    )

    empty = (2 * FAR_REACH + 1) * leaves
    low_lanes = lax.broadcasted_iota(jnp.int32, (32, 2 * rank), 1) < rank
    for b in range(3):
        for place, blocks in ((b, before), (3 + b, middle), (6 + b, after)):
            fill_table(table, blocks.at[b], place * leaves)
    table[empty] = jnp.zeros_like(table[empty])
    table[empty + 1] = jnp.zeros_like(table[empty])
    base = near[0, 0] - FAR_REACH * leaves

    def far_step(step, carry):
        arriving(step).wait()
        for u in range(FAR_STEP):
            c = step * FAR_STEP + u

            def picks(start, count):
                rows = [far[c, k] if k < slots else -1 for k in range(start, start + count)]
                rows = [jnp.where(row >= 0, row - base, empty) for row in rows]
                return picked(table, rows, low_lanes)

            far_out[c] = coupled_pairs(picks, couples.at[c])
        return carry

    lax.fori_loop(0, steps, far_step, 0)


def down_kernel(
    near, box_list, column_list, boxes0, boxes1, boxes2, boxes3, couple_box_in, couple_column_in,
    transfer_box_in, transfer_in, basis_in, far_in, inner_in, outer_in, out,
    gathered, couple_box, couple_column, transfer_box, transfer_leaf, basis, far_leaf,
    near_inner, near_outer, semaphores,
):
    leaves, rank, leaf_size = basis.shape
    slots, column_slots = box_list.shape[1], column_list.shape[1]
    low_lanes = lax.broadcasted_iota(jnp.int32, (32, 2 * rank), 1) < rank
    length = boxes0.shape[0]
    arriving = copies(
        [
            (boxes, gathered.at[pl.ds(i * length, length)])
            for i, boxes in enumerate((boxes0, boxes1, boxes2, boxes3))
        ]
        + [
            (couple_box_in, couple_box),
            (couple_column_in, couple_column),
            (transfer_box_in, transfer_box),
            (far_in, far_leaf),
            (inner_in, near_inner),
            (outer_in, near_outer),
        ]
        + parts(transfer_in, transfer_leaf)
        + parts(basis_in, basis),
        semaphores,
    )
    for copy in arriving[:7]:
        copy.wait()

    own = near[0, 0] // leaves

    def moved(entry, shift, bits):
        mask = (1 << bits) - 1
        return (((entry >> shift) - (own >> shift)) & mask) << shift

    def box_row(entry):
        entry = jnp.where(entry >= 0, entry, 0)
        return moved(entry, 0, 2) + moved(entry, 2, 1) + moved(entry, 3, 2) + moved(entry, 5, 2)

    def pick(k):
        entry = box_list[0, k]
        return gathered[box_row(entry)] * jnp.where(entry >= 0, 1.0, 0.0)

    pieces = []
    for k in range(0, slots, 2):
        if k + 1 < slots:
            pieces.append(stacked_halves(jnp.where(low_lanes[:16], pick(k), exchanged(pick(k + 1)))))
        else:
            pieces.append(stacked_halves(pick(k))[:, :rank])
    far_box = coupled(jnp.concatenate(pieces, axis=1), couple_box[0])

    columns = []
    for k in range(column_slots):
        row = column_list[0, k]
        start = box_row(row * 4) & ~3
        block = gathered[start]
        for j in range(1, 4):
            block = block + gathered[start + j]
        columns.append(block * jnp.where(row >= 0, 1.0, 0.0))
    pieces = [
        stacked_halves(jnp.where(low_lanes[:16], exchanged(columns[k]), columns[k + 1]))
        for k in range(0, column_slots, 2)
    ]
    far_column = coupled(jnp.concatenate(pieces, axis=1), couple_column[0])
    down_box = far_box + product3(far_column, transfer_box[0], ((1,), (1,)))

    for copy in arriving[7:10]:
        copy.wait()
    for c in range(leaves):
        if c % (leaves // CHUNKS) == 0:
            arriving[10 + c // (leaves // CHUNKS)].wait()
            arriving[10 + CHUNKS + c // (leaves // CHUNKS)].wait()
        down = far_leaf[c] + product3(down_box, transfer_leaf[c], ((1,), (1,)))
        lanes = slice(c * leaf_size, (c + 1) * leaf_size)
        inner = NEAR_REACH <= c < leaves - NEAR_REACH
        place = c - NEAR_REACH if inner else c if c < NEAR_REACH else c - leaves + 2 * NEAR_REACH
        held = near_inner if inner else near_outer
        near_value = held[:, place * leaf_size : (place + 1) * leaf_size]
        out[:, lanes] = near_value + product3(down, basis[c])


def whole(count):
    return [pl.BlockSpec(memory_space=pltpu.VMEM)] * count


def scalars(count):
    return [pl.BlockSpec(memory_space=pltpu.SMEM)] * count


params = pltpu.CompilerParams(vmem_limit_bytes=60 * 2**20)


def cost(flops):
    return pl.CostEstimate(flops=flops, bytes_accessed=2**20, transcendentals=0)


def shifted(array, axis, by):
    devices = lax.axis_size(axis)
    return lax.ppermute(array, axis, [(i, (i + by) % devices) for i in range(devices)])


def hbm(count):
    return [pl.BlockSpec(memory_space=pl.ANY)] * count


def near_scratch(items, probe_count, leaf_size):
    slots, leaves = items.shape
    window = leaves + 2 * NEAR_REACH
    return [
        pltpu.VMEM((window, 2 * probe_count, leaf_size), bf16),
        pltpu.VMEM((window, leaf_size, FEATURES), bf16),
        pltpu.VMEM((leaves, FEATURES, leaf_size), bf16),
        pltpu.VMEM((leaves, probe_count, leaf_size), f32),
        pltpu.SMEM((leaves * slots + 2 * GROUP,), jnp.int32),
    ]


def like(array):
    return pltpu.VMEM(array.shape, array.dtype)


def copy_semaphores(count):
    return pltpu.SemaphoreType.DMA((count,))


def moved_along(array, shift, bits, by):
    mask = (1 << bits) - 1

    def target(i):
        part = (i >> shift) & mask
        return i + ((((part - by) & mask) - part) << shift)

    return lax.ppermute(array, "leaf", [(i, target(i)) for i in range(lax.axis_size("leaf"))])


def per_device(
    points,
    probes,
    basis,
    transfer_leaf,
    transfer_box,
    couple_leaf,
    couple_box,
    couple_column,
    near_list,
    far_list,
    box_list,
    column_list,
):
    leaves, leaf_size, rank = basis.shape
    probe_count = probes.shape[0]
    near_slots = near_list.T
    basis = basis.transpose(0, 2, 1)
    pairs = leaves // 2
    blocks = pairs + NEAR_REACH * leaf_size // 128 + 2

    bundles, box, items = pl.pallas_call(
        skeleton_kernel,
        out_shape=(
            jax.ShapeDtypeStruct((2, blocks, probe_count, 2 * rank), f32),
            jax.ShapeDtypeStruct((1, probe_count, 2 * rank), f32),
            jax.ShapeDtypeStruct(near_slots.shape, jnp.int32),
        ),
        in_specs=whole(2) + hbm(3) + whole(1),
        out_specs=tuple(whole(3)),
        scratch_shapes=[like(probes), like(basis), like(transfer_leaf)]
        + [copy_semaphores(1 + 2 * CHUNKS)],
        compiler_params=params,
        name="skeletons",
    )(near_slots, points, probes, basis, transfer_leaf, transfer_box)

    box_next, box_last = shifted(box, "sub", -1), shifted(box, "sub", 1)
    left, right = shifted(bundles[0], ring, 1), shifted(bundles[1], ring, -1)
    box_second = shifted(box_next, "sub", -1)
    column = jnp.concatenate([box, box_next, box_second, box_last])
    both = jnp.concatenate([column, moved_along(column, 0, 1, 1)])
    along_y = [both] + [moved_along(both, 1, 2, by) for by in (1, 2, 3)]
    plane = jnp.concatenate(along_y)
    planes = [plane] + [moved_along(plane, 3, 2, by) for by in (1, 2, 3)]

    middle = jnp.stack([left[:pairs], bundles[0, :pairs], right[:pairs]])
    before, after = shifted(middle, ring, 3), shifted(middle, ring, -3)

    inner = ((NEAR_REACH, leaves - NEAR_REACH),)
    outer = ((0, NEAR_REACH), (leaves - NEAR_REACH, leaves))
    half = jax.ShapeDtypeStruct((probe_count, probes.shape[1] // 2), f32)
    near_inner = pl.pallas_call(
        functools.partial(near_kernel, groups=inner),
        out_shape=half,
        in_specs=scalars(1) + whole(4),
        out_specs=pl.BlockSpec(memory_space=pltpu.VMEM),
        scratch_shapes=near_scratch(items, probe_count, leaf_size),
        compiler_params=params,
        cost_estimate=cost(10_000_000_000),
        name="near_inner",
    )(items, points, probes, box, box)

    near_outer, far_leaf = pl.pallas_call(
        functools.partial(outer_kernel, groups=outer),
        out_shape=(half, jax.ShapeDtypeStruct((leaves, probe_count, rank), f32)),
        in_specs=scalars(3) + whole(7) + hbm(1),
        out_specs=tuple(whole(2)),
        scratch_shapes=near_scratch(items, probe_count, leaf_size)
        + [
            pltpu.VMEM(((2 * FAR_REACH + 1) * leaves + 2, 2 * probe_count, 2 * rank), bf16),
            like(couple_leaf),
            copy_semaphores(leaves // FAR_STEP),
        ],
        compiler_params=params,
        cost_estimate=cost(15_000_000_000),
        name="near_outer_far",
    )(items, far_list, near_slots, points, probes, left, right, before, middle, after, couple_leaf)

    gathered = pltpu.VMEM((4 * plane.shape[0],) + plane.shape[1:], f32)
    held = (couple_box, couple_column, transfer_box, transfer_leaf, basis, far_leaf)
    held += (near_inner, near_outer)
    return pl.pallas_call(
        down_kernel,
        out_shape=jax.ShapeDtypeStruct(probes.shape, f32),
        in_specs=scalars(3) + hbm(12),
        out_specs=pl.BlockSpec(memory_space=pltpu.VMEM),
        scratch_shapes=[gathered] + [like(array) for array in held]
        + [copy_semaphores(10 + 2 * CHUNKS)],
        compiler_params=params,
        name="down",
    )(near_slots, box_list, column_list, *planes, *held)


def solution(mesh):
    placed = (
        P(None, ring),
        P(None, ring),
        P(ring, None, None),
        P(ring, None, None),
        P(ring, None, None),
        P(ring, None, None, None),
        P(ring, None, None, None),
        P("leaf", None, None, None),
        P(ring, None),
        P(ring, None),
        P(ring, None),
        P("leaf", None),
    )
    return jax.shard_map(
        per_device, mesh=mesh, in_specs=placed, out_specs=P(None, ring), check_vma=False
    )
```

```python
import functools
import math

import jax
import jax.numpy as jnp
from jax import lax
from jax.experimental import pallas as pl
from jax.experimental.pallas import tpu as pltpu
from jax.sharding import PartitionSpec as P

NEAR_REACH = 8
FAR_REACH = 4
FEATURES = 16
GROUP = 12
FAR_STEP = 4
CHUNKS = 4

matern_rate = math.sqrt(3.0) / 0.1
coordinate_scale = matern_rate * math.log2(math.e)
ln2 = math.log(2.0)
tiny = 1e-20
f32 = jnp.float32
bf16 = jnp.bfloat16
vmem_bytes = 60 * 2**20
ring = ("leaf", "sub")


def halves(array):
    high = array.astype(bf16)
    return high, (array - high.astype(f32)).astype(bf16)


def stacked_halves(array):
    return jnp.concatenate(halves(array), axis=0)


def contract(left, right, dims):
    return lax.dot_general(left, right, (dims, ((), ())), preferred_element_type=f32)


def product3(left, right, dims=((1,), (0,))):
    rows = left.shape[0]
    high, low = halves(right)
    both = stacked_halves(left)
    wide = contract(both, high, dims)
    return wide[:rows] + wide[rows:] + contract(both[:rows], low, dims)


def copies(pairs, semaphores):
    made = [
        pltpu.make_async_copy(source, held, semaphores.at[i])
        for i, (source, held) in enumerate(pairs)
    ]
    for copy in made:
        copy.start()
    return made


def parts(source, held):
    length = source.shape[0] // CHUNKS
    runs = [pl.ds(i * length, length) for i in range(CHUNKS)]
    return [(source.at[run], held.at[run]) for run in runs]


def exchanged(block):
    half = block.shape[1] // 2
    return jnp.concatenate([block[:, half:], block[:, :half]], axis=1)


def skeleton_kernel(
    near, points, probes_in, basis_in, transfer_in, transfer_box, out, out_first, box_out, items,
    probes, basis, transfer_leaf, semaphores,
):
    leaves, rank, leaf_size = basis.shape
    arriving = copies(
        [(probes_in, probes)] + parts(basis_in, basis) + parts(transfer_in, transfer_leaf),
        semaphores,
    )
    slots = near.shape[0]
    pairs = leaves // 2
    low_lanes = lax.broadcasted_iota(jnp.int32, (16, 2 * rank), 1) < rank

    leaf = lax.broadcasted_iota(jnp.int32, (1, leaves), 1)
    rows = [near[k : k + 1, :] for k in range(slots)]
    for k in range(slots):
        new = rows[k] >= 0
        times = jnp.ones_like(leaf)
        for j in range(k):
            new = new & (rows[j] != rows[k])
        for j in range(k + 1, slots):
            times = times + jnp.where(rows[j] == rows[k], 1, 0)
        place = rows[k] - rows[0] + leaf + NEAR_REACH
        items[k : k + 1, :] = jnp.where(new, leaf + place * 64 + times * 4096, 0)

    arriving[0].wait()
    width = probes.shape[1]
    edge = NEAR_REACH * leaf_size
    for side, start in ((out, width - edge), (out_first, 0)):
        for j in range(edge // 128):
            lanes = slice(start + j * 128, start + (j + 1) * 128)
            side[pairs + j] = probes[:, lanes]
            side[pairs + edge // 128, j : j + 1, :] = points[0:1, lanes]
            side[pairs + edge // 128 + 1, j : j + 1, :] = points[1:2, lanes]

    def leaf_probes(c):
        return stacked_halves(probes[:, c * leaf_size : (c + 1) * leaf_size])

    def summed(wide):
        return wide[:16] + wide[16:] + exchanged(wide[:16])

    skeletons = []
    for m in range(pairs):
        if m % (pairs // CHUNKS) == 0:
            arriving[1 + m // (pairs // CHUNKS)].wait()
        left = jnp.concatenate([leaf_probes(2 * m), leaf_probes(2 * m + 1)], axis=0)
        right = jnp.concatenate([stacked_halves(basis[2 * m]), stacked_halves(basis[2 * m + 1])], axis=0)
        wide = contract(left, right, ((1,), (1,)))
        even, odd = summed(wide[:32, : 2 * rank]), summed(wide[32:, 2 * rank :])
        pair = jnp.where(low_lanes, even, exchanged(odd))
        out[m] = pair
        out_first[m] = pair
        skeletons.append(pair)
    for copy in arriving[1 + CHUNKS :]:
        copy.wait()
    high, low = halves(transfer_leaf[...].reshape(leaves * rank, rank))
    wide = jnp.dot(
        stacked_halves(jnp.concatenate(skeletons, axis=1)),
        jnp.concatenate([high, low], axis=1),
        preferred_element_type=f32,
    )
    box = summed(wide)[:, :rank]
    box_out[0] = jnp.concatenate([box, product3(box, transfer_box[0])], axis=1)


def near_kernel(
    items, points, probes, left, right, out, values, source, target, total, listed, *, groups
):
    slots, leaves = items.shape
    leaf_size = target.shape[2]
    pieces = leaf_size // 128
    pairs = leaves // 2
    edge_blocks = NEAR_REACH * pieces

    count = jnp.int32(0)
    for begin, end in groups:
        for c in range(begin, end):
            for k in range(slots):
                item = items[k, c]
                listed[count] = item
                count = count + jnp.where(item != 0, 1, 0)
    for u in range(GROUP):
        listed[count + u] = groups[0][0] + NEAR_REACH * 64

    ones = jnp.ones((3, leaf_size), f32)
    pad = jnp.zeros((2, leaf_size), f32)
    window = sorted({w for begin, end in groups for w in range(begin, end + 2 * NEAR_REACH)})
    for w in window:
        own = NEAR_REACH <= w < NEAR_REACH + leaves
        if own:
            lanes = slice((w - NEAR_REACH) * leaf_size, (w - NEAR_REACH + 1) * leaf_size)
            place, value = points[:, lanes], probes[:, lanes]
        else:
            side = left if w < NEAR_REACH else right
            first = (w if w < NEAR_REACH else w - NEAR_REACH - leaves) * pieces
            parts = range(first, first + pieces)
            value = jnp.concatenate([side[pairs + j] for j in parts], axis=1)
            place = jnp.concatenate(
                [
                    jnp.concatenate(
                        [side[pairs + edge_blocks + d, j : j + 1, :] for j in parts], axis=1
                    )
                    for d in range(2)
                ],
                axis=0,
            )
        values[w] = stacked_halves(value)
        scaled = (place - 0.5) * coordinate_scale
        first = scaled.astype(bf16).astype(f32)
        second = (scaled - first).astype(bf16).astype(f32)
        kept = first + second
        norm = kept[0:1] * kept[0:1] + kept[1:2] * kept[1:2]
        norm1 = norm.astype(bf16).astype(f32)
        rest = norm - norm1
        norm2 = rest.astype(bf16).astype(f32)
        norms = jnp.concatenate([norm1, norm2, rest - norm2], axis=0)
        rows = jnp.concatenate([first, second, first, second, norms, ones, pad], axis=0)
        source[w] = rows.T.astype(bf16)
        if own and any(begin <= w - NEAR_REACH < end for begin, end in groups):
            target[w - NEAR_REACH] = jnp.concatenate(
                [-2.0 * first, -2.0 * first, -2.0 * second, -2.0 * second, ones, norms, pad], axis=0
            ).astype(bf16)
    total[...] = jnp.zeros_like(total)

    def tile(i):
        item = listed[i]
        c, s, times = item & 63, (item >> 6) & 63, item >> 12
        squared = jnp.dot(source[s], target[c], preferred_element_type=f32)
        squared = jnp.maximum(squared, tiny)
        distance = squared * lax.rsqrt(squared)
        high, low = halves((distance + 1.0 / ln2) * jnp.exp2(-distance))
        both = values[s]
        wide = jnp.dot(both, high, preferred_element_type=f32)
        rest = jnp.dot(both[:16], low, preferred_element_type=f32)
        return c, (wide[:16] + wide[16:] + rest) * (times.astype(f32) * ln2)

    def group(t, carry):
        for c, term in [tile(t * GROUP + u) for u in range(GROUP)]:
            total[c] += term
        return carry

    lax.fori_loop(0, (count + GROUP - 1) // GROUP, group, 0)
    place = 0
    for begin, end in groups:
        for c in range(begin, end):
            out[:, place * leaf_size : (place + 1) * leaf_size] = total[c]
            place += 1


def fill_table(table, blocks, start):
    count, _, lanes = blocks.shape
    half = lanes // 2
    for m in range(count):
        block = blocks[m]
        swapped = jnp.concatenate([block[:, half:], block[:, :half]], axis=1)
        table[start + 2 * m] = stacked_halves(block)
        table[start + 2 * m + 1] = stacked_halves(swapped)


def picked(table, rows, low_lanes):
    pieces = []
    for k in range(0, len(rows) - 1, 2):
        pieces.append(jnp.where(low_lanes, table[rows[k]], table[rows[k + 1] ^ 1]))
    if len(rows) % 2:
        pieces.append(table[rows[-1]][:, : low_lanes.shape[1] // 2])
    return jnp.concatenate(pieces, axis=1)


def coupled_pairs(picks, couples):
    slots, rank, _ = couples.shape
    result = jnp.zeros((16, rank), f32)
    low_lanes = lax.broadcasted_iota(jnp.int32, (rank, 2 * rank), 1) < rank
    for start in range(0, slots, 8):
        pairs = (min(slots - start, 8) + 1) // 2
        highs, lows = [], []
        for m in range(pairs):
            even = couples[start + m]
            if start + pairs + m < slots:
                odd = couples[start + pairs + m]
            else:
                odd = jnp.zeros_like(even)
            high, low = halves(jnp.concatenate([even, odd], axis=1))
            highs.append(high)
            lows.append(low)
        right = jnp.concatenate(
            [jnp.concatenate(highs, axis=0), jnp.concatenate(lows, axis=0)], axis=1
        )
        left = jnp.concatenate(
            [picks(start, pairs), picks(start + pairs, pairs)], axis=0
        )
        wide = jnp.dot(left, right, preferred_element_type=f32)
        first = wide[:16, : 2 * rank] + wide[16:32, : 2 * rank] + wide[:16, 2 * rank :]
        second = wide[32:48, : 2 * rank] + wide[48:, : 2 * rank] + wide[32:48, 2 * rank :]
        result = result + first[:, :rank] + second[:, rank:]
    return result


def coupled(both, couples):
    count, rank, _ = couples.shape
    high, low = halves(couples.reshape(count * rank, rank))
    wide = jnp.dot(both, jnp.concatenate([high, low], axis=1), preferred_element_type=f32)
    return wide[:16, :rank] + wide[16:, :rank] + wide[:16, rank:]


def inner_kernel(
    items, points, probes, bundle, column, out, skeletons_out, column_out, *scratch, groups
):
    skeletons_out[...] = bundle[: skeletons_out.shape[0]]
    column_out[...] = column[...]
    near_kernel(items, points, probes, bundle, bundle, out, *scratch, groups=groups)


def far_kernel(
    far, near, before, middle, after, couples_in, out, table, couples, semaphores
):
    leaves, slots, rank, _ = couples.shape
    steps = leaves // FAR_STEP

    def arriving(step):
        run = pl.ds(step * FAR_STEP, FAR_STEP)
        return pltpu.make_async_copy(couples_in.at[run], couples.at[run], semaphores.at[step])

    def start(step, carry):
        arriving(step).start()
        return carry

    lax.fori_loop(0, steps, start, 0)
    empty = (2 * FAR_REACH + 1) * leaves
    low_lanes = lax.broadcasted_iota(jnp.int32, (32, 2 * rank), 1) < rank
    for b in range(3):
        for place, blocks in ((b, before), (3 + b, middle), (6 + b, after)):
            fill_table(table, blocks.at[b], place * leaves)
    table[empty] = jnp.zeros_like(table[empty])
    table[empty + 1] = jnp.zeros_like(table[empty])
    base = near[0, 0] - FAR_REACH * leaves

    def far_leaf(c):
        def picks(start, count):
            rows = [far[c, k] if k < slots else -1 for k in range(start, start + count)]
            rows = [jnp.where(row >= 0, row - base, empty) for row in rows]
            return picked(table, rows, low_lanes)

        return coupled_pairs(picks, couples.at[c])

    def far_step(step, carry):
        arriving(step).wait()
        for u in range(0, FAR_STEP, 2):
            c = step * FAR_STEP + u
            pair = jnp.concatenate([far_leaf(c), far_leaf(c + 1)], axis=1)
            out[(step * FAR_STEP + u) // 2] = pair
        return carry

    lax.fori_loop(0, steps, far_step, 0)


def down_kernel(
    near, box_list, column_list, boxes0, boxes1, boxes2, boxes3, couple_box_in, couple_column_in,
    transfer_box_in, transfer_in, basis_in, far_in, inner_in, outer_in, out,
    gathered, couple_box, couple_column, transfer_box, transfer_leaf, basis, far_leaf,
    near_inner, near_outer, semaphores,
):
    leaves, rank, leaf_size = basis.shape
    slots, column_slots = box_list.shape[1], column_list.shape[1]
    low_lanes = lax.broadcasted_iota(jnp.int32, (32, 2 * rank), 1) < rank
    length = boxes0.shape[0]
    arriving = copies(
        [
            (boxes, gathered.at[pl.ds(i * length, length)])
            for i, boxes in enumerate((boxes0, boxes1, boxes2, boxes3))
        ]
        + [
            (couple_box_in, couple_box),
            (couple_column_in, couple_column),
            (transfer_box_in, transfer_box),
            (far_in, far_leaf),
            (inner_in, near_inner),
            (outer_in, near_outer),
        ]
        + parts(transfer_in, transfer_leaf)
        + parts(basis_in, basis),
        semaphores,
    )
    for copy in arriving[:7]:
        copy.wait()

    own = near[0, 0] // leaves

    def moved(entry, shift, bits):
        mask = (1 << bits) - 1
        return (((entry >> shift) - (own >> shift)) & mask) << shift

    def box_row(entry):
        entry = jnp.where(entry >= 0, entry, 0)
        return moved(entry, 0, 2) + moved(entry, 2, 1) + moved(entry, 3, 2) + moved(entry, 5, 2)

    def pick(k):
        entry = box_list[0, k]
        return gathered[box_row(entry)] * jnp.where(entry >= 0, 1.0, 0.0)

    pieces = []
    for k in range(0, slots, 2):
        if k + 1 < slots:
            pieces.append(stacked_halves(jnp.where(low_lanes[:16], pick(k), exchanged(pick(k + 1)))))
        else:
            pieces.append(stacked_halves(pick(k))[:, :rank])
    far_box = coupled(jnp.concatenate(pieces, axis=1), couple_box[0])

    columns = []
    for k in range(column_slots):
        row = column_list[0, k]
        start = box_row(row * 4) & ~3
        block = gathered[start]
        for j in range(1, 4):
            block = block + gathered[start + j]
        columns.append(block * jnp.where(row >= 0, 1.0, 0.0))
    pieces = [
        stacked_halves(jnp.where(low_lanes[:16], exchanged(columns[k]), columns[k + 1]))
        for k in range(0, column_slots, 2)
    ]
    far_column = coupled(jnp.concatenate(pieces, axis=1), couple_column[0])
    down_box = far_box + product3(far_column, transfer_box[0], ((1,), (1,)))

    for copy in arriving[7 : 10 + CHUNKS]:
        copy.wait()
    high, low = halves(transfer_leaf[...].reshape(leaves * rank, rank))
    both = stacked_halves(down_box)
    wide = contract(both, high, ((1,), (1,)))
    from_box = wide[:16] + wide[16:] + contract(both[:16], low, ((1,), (1,)))

    lane = lax.broadcasted_iota(jnp.int32, (16, 4 * rank), 1)
    for m in range(leaves // 4):
        if m % (leaves // 4 // CHUNKS) == 0:
            arriving[10 + CHUNKS + m // (leaves // 4 // CHUNKS)].wait()
        down = from_box[:, m * 4 * rank : (m + 1) * 4 * rank]
        down = down + jnp.concatenate([far_leaf[2 * m], far_leaf[2 * m + 1]], axis=1)
        own_rows = [
            jnp.where((lane >= j * rank) & (lane < (j + 1) * rank), down, 0.0) for j in range(4)
        ]
        left = stacked_halves(jnp.concatenate(own_rows, axis=0))
        high, low = halves(basis[4 * m : 4 * m + 4].reshape(4 * rank, leaf_size))
        wide = jnp.dot(left, high, preferred_element_type=f32)
        rest = jnp.dot(left[:64], low, preferred_element_type=f32)
        result = wide[:64] + wide[64:] + rest
        for j in range(4):
            c = 4 * m + j
            inner = NEAR_REACH <= c < leaves - NEAR_REACH
            place = c - NEAR_REACH if inner else c if c < NEAR_REACH else c - leaves + 2 * NEAR_REACH
            held = near_inner if inner else near_outer
            near_value = held[:, place * leaf_size : (place + 1) * leaf_size]
            out[:, c * leaf_size : (c + 1) * leaf_size] = near_value + result[16 * j : 16 * j + 16]


def whole(count):
    return [pl.BlockSpec(memory_space=pltpu.VMEM)] * count


def scalars(count):
    return [pl.BlockSpec(memory_space=pltpu.SMEM)] * count


params = pltpu.CompilerParams(vmem_limit_bytes=60 * 2**20)


def cost(flops):
    return pl.CostEstimate(flops=flops, bytes_accessed=2**20, transcendentals=0)


def shifted(array, axis, by):
    devices = lax.axis_size(axis)
    return lax.ppermute(array, axis, [(i, (i + by) % devices) for i in range(devices)])


def hbm(count):
    return [pl.BlockSpec(memory_space=pl.ANY)] * count


def near_scratch(items, probe_count, leaf_size):
    slots, leaves = items.shape
    window = leaves + 2 * NEAR_REACH
    return [
        pltpu.VMEM((window, 2 * probe_count, leaf_size), bf16),
        pltpu.VMEM((window, leaf_size, FEATURES), bf16),
        pltpu.VMEM((leaves, FEATURES, leaf_size), bf16),
        pltpu.VMEM((leaves, probe_count, leaf_size), f32),
        pltpu.SMEM((leaves * slots + 2 * GROUP,), jnp.int32),
    ]


def like(array):
    return pltpu.VMEM(array.shape, array.dtype)


def copy_semaphores(count):
    return pltpu.SemaphoreType.DMA((count,))


def moved_along(array, shift, bits, by):
    mask = (1 << bits) - 1

    def target(i):
        part = (i >> shift) & mask
        return i + ((((part - by) & mask) - part) << shift)

    return lax.ppermute(array, "leaf", [(i, target(i)) for i in range(lax.axis_size("leaf"))])


def per_device(
    points,
    probes,
    basis,
    transfer_leaf,
    transfer_box,
    couple_leaf,
    couple_box,
    couple_column,
    near_list,
    far_list,
    box_list,
    column_list,
):
    leaves, leaf_size, rank = basis.shape
    probe_count = probes.shape[0]
    near_slots = near_list.T
    basis = basis.transpose(0, 2, 1)
    pairs = leaves // 2
    blocks = pairs + NEAR_REACH * leaf_size // 128 + 2

    edges = jax.ShapeDtypeStruct((blocks, probe_count, 2 * rank), f32)
    bundle_last, bundle_first, box, items = pl.pallas_call(
        skeleton_kernel,
        out_shape=(
            edges,
            edges,
            jax.ShapeDtypeStruct((1, probe_count, 2 * rank), f32),
            jax.ShapeDtypeStruct(near_slots.shape, jnp.int32),
        ),
        in_specs=whole(2) + hbm(3) + whole(1),
        out_specs=tuple(whole(4)),
        scratch_shapes=[like(probes), like(basis), like(transfer_leaf)]
        + [copy_semaphores(1 + 2 * CHUNKS)],
        compiler_params=params,
        name="skeletons",
    )(near_slots, points, probes, basis, transfer_leaf, transfer_box)

    column = jnp.concatenate([box] + [shifted(box, "sub", -by) for by in (1, 2, 3)])
    left, right = shifted(bundle_last, ring, 1), shifted(bundle_first, ring, -1)
    other_core = moved_along(column, 0, 1, 1)

    inner = ((NEAR_REACH, leaves - NEAR_REACH),)
    outer = ((0, NEAR_REACH), (leaves - NEAR_REACH, leaves))
    half = jax.ShapeDtypeStruct((probe_count, probes.shape[1] // 2), f32)
    near_inner, skeletons, column = pl.pallas_call(
        functools.partial(inner_kernel, groups=inner),
        out_shape=(
            half,
            jax.ShapeDtypeStruct((pairs, probe_count, 2 * rank), f32),
            jax.ShapeDtypeStruct(column.shape, f32),
        ),
        in_specs=scalars(1) + whole(4),
        out_specs=tuple(whole(3)),
        scratch_shapes=near_scratch(items, probe_count, leaf_size),
        compiler_params=params,
        cost_estimate=cost(10_000_000_000),
        name="near_inner",
    )(items, points, probes, bundle_last, column)

    both = jnp.concatenate([column, other_core])
    middle = jnp.stack([left[:pairs], skeletons, right[:pairs]])
    plane = jnp.concatenate([both] + [moved_along(both, 1, 2, by) for by in (1, 2, 3)])
    before, after = shifted(middle, ring, 3), shifted(middle, ring, -3)
    planes = [plane] + [moved_along(plane, 3, 2, by) for by in (1, 2, 3)]

    near_outer = pl.pallas_call(
        functools.partial(near_kernel, groups=outer),
        out_shape=half,
        in_specs=scalars(1) + whole(4),
        out_specs=pl.BlockSpec(memory_space=pltpu.VMEM),
        scratch_shapes=near_scratch(items, probe_count, leaf_size),
        compiler_params=params,
        cost_estimate=cost(10_000_000_000),
        name="near_outer",
    )(items, points, probes, left, right)

    far_leaf = pl.pallas_call(
        far_kernel,
        out_shape=jax.ShapeDtypeStruct((pairs, probe_count, 2 * rank), f32),
        in_specs=scalars(2) + whole(3) + hbm(1),
        out_specs=pl.BlockSpec(memory_space=pltpu.VMEM),
        scratch_shapes=[
            pltpu.VMEM(((2 * FAR_REACH + 1) * leaves + 2, 2 * probe_count, 2 * rank), bf16),
            like(couple_leaf),
            copy_semaphores(leaves // FAR_STEP),
        ],
        compiler_params=params,
        cost_estimate=cost(8_000_000_000),
        name="far",
    )(far_list, near_slots, before, middle, after, couple_leaf)

    gathered = pltpu.VMEM((4 * plane.shape[0],) + plane.shape[1:], f32)
    held = (couple_box, couple_column, transfer_box, transfer_leaf, basis, far_leaf)
    held += (near_inner, near_outer)
    return pl.pallas_call(
        down_kernel,
        out_shape=jax.ShapeDtypeStruct(probes.shape, f32),
        in_specs=scalars(3) + hbm(12),
        out_specs=pl.BlockSpec(memory_space=pltpu.VMEM),
        scratch_shapes=[gathered] + [like(array) for array in held]
        + [copy_semaphores(10 + 2 * CHUNKS)],
        compiler_params=params,
        name="down",
    )(near_slots, box_list, column_list, *planes, *held)


def solution(mesh):
    placed = (
        P(None, ring),
        P(None, ring),
        P(ring, None, None),
        P(ring, None, None),
        P(ring, None, None),
        P(ring, None, None, None),
        P(ring, None, None, None),
        P("leaf", None, None, None),
        P(ring, None),
        P(ring, None),
        P(ring, None),
        P("leaf", None),
    )
    return jax.shard_map(
        per_device, mesh=mesh, in_specs=placed, out_specs=P(None, ring), check_vma=False
    )
```

```python
import functools
import math

import jax
import jax.numpy as jnp
from jax import lax
from jax.experimental import pallas as pl
from jax.experimental.pallas import tpu as pltpu
from jax.sharding import PartitionSpec as P

NEAR_REACH = 8
FAR_REACH = 4
FEATURES = 16
GROUP = 12
TAIL_GROUP = 4
FAR_STEP = 2
CHUNKS = 4

matern_rate = math.sqrt(3.0) / 0.1
coordinate_scale = matern_rate * math.log2(math.e)
ln2 = math.log(2.0)
tiny = 1e-20
f32 = jnp.float32
bf16 = jnp.bfloat16
vmem_bytes = 60 * 2**20
ring = ("leaf", "sub")


def halves(array):
    high = array.astype(bf16)
    return high, (array - high.astype(f32)).astype(bf16)


def stacked_halves(array):
    return jnp.concatenate(halves(array), axis=0)


def contract(left, right, dims):
    return lax.dot_general(left, right, (dims, ((), ())), preferred_element_type=f32)


def product3(left, right, dims=((1,), (0,))):
    rows = left.shape[0]
    high, low = halves(right)
    both = stacked_halves(left)
    wide = contract(both, high, dims)
    return wide[:rows] + wide[rows:] + contract(both[:rows], low, dims)


def copies(pairs, semaphores):
    made = [
        pltpu.make_async_copy(source, held, semaphores.at[i])
        for i, (source, held) in enumerate(pairs)
    ]
    for copy in made:
        copy.start()
    return made


def parts(source, held):
    length = source.shape[0] // CHUNKS
    runs = [pl.ds(i * length, length) for i in range(CHUNKS)]
    return [(source.at[run], held.at[run]) for run in runs]


def exchanged(block):
    half = block.shape[1] // 2
    return jnp.concatenate([block[:, half:], block[:, :half]], axis=1)


def skeleton_kernel(
    near, points, probes_in, basis_in, transfer_in, transfer_box, out, out_first, items,
    probes, basis, transfer_leaf, semaphores,
):
    leaves, rank, leaf_size = basis.shape
    arriving = copies(
        [(probes_in, probes)] + parts(basis_in, basis) + parts(transfer_in, transfer_leaf),
        semaphores,
    )
    slots = near.shape[0]
    pairs = leaves // 2
    low_lanes = lax.broadcasted_iota(jnp.int32, (16, 2 * rank), 1) < rank

    leaf = lax.broadcasted_iota(jnp.int32, (1, leaves), 1)
    rows = [near[k : k + 1, :] for k in range(slots)]
    for k in range(slots):
        new = rows[k] >= 0
        times = jnp.ones_like(leaf)
        for j in range(k):
            new = new & (rows[j] != rows[k])
        for j in range(k + 1, slots):
            times = times + jnp.where(rows[j] == rows[k], 1, 0)
        place = rows[k] - rows[0] + leaf + NEAR_REACH
        items[k : k + 1, :] = jnp.where(new, leaf + place * 64 + times * 4096, 0)

    arriving[0].wait()
    width = probes.shape[1]
    edge = NEAR_REACH * leaf_size
    for side, start in ((out, width - edge), (out_first, 0)):
        for j in range(edge // 128):
            lanes = slice(start + j * 128, start + (j + 1) * 128)
            side[pairs + 1 + j] = probes[:, lanes]
            side[pairs + 1 + edge // 128, j : j + 1, :] = points[0:1, lanes]
            side[pairs + 2 + edge // 128, j : j + 1, :] = points[1:2, lanes]

    def leaf_probes(c):
        return stacked_halves(probes[:, c * leaf_size : (c + 1) * leaf_size])

    def summed(wide):
        return wide[:16] + wide[16:] + exchanged(wide[:16])

    skeletons = []
    for m in range(pairs):
        if m % (pairs // CHUNKS) == 0:
            arriving[1 + m // (pairs // CHUNKS)].wait()
        left = jnp.concatenate([leaf_probes(2 * m), leaf_probes(2 * m + 1)], axis=0)
        right = jnp.concatenate([stacked_halves(basis[2 * m]), stacked_halves(basis[2 * m + 1])], axis=0)
        wide = contract(left, right, ((1,), (1,)))
        even, odd = summed(wide[:32, : 2 * rank]), summed(wide[32:, 2 * rank :])
        pair = jnp.where(low_lanes, even, exchanged(odd))
        out[m] = pair
        out_first[m] = pair
        skeletons.append(pair)
    for copy in arriving[1 + CHUNKS :]:
        copy.wait()
    high, low = halves(transfer_leaf[...].reshape(leaves * rank, rank))
    wide = jnp.dot(
        stacked_halves(jnp.concatenate(skeletons, axis=1)),
        jnp.concatenate([high, low], axis=1),
        preferred_element_type=f32,
    )
    box = summed(wide)[:, :rank]
    block = jnp.concatenate([box, product3(box, transfer_box[0])], axis=1)
    out[pairs] = block
    out_first[pairs] = block


def near_kernel(
    items, points, probes, side, carried, out, carried_out,
    values, source, target, total, listed, semaphore, *, begin, end
):
    slots, leaves = items.shape
    leaf_size = target.shape[2]
    pieces = leaf_size // 128
    pairs = leaves // 2
    edge_blocks = NEAR_REACH * pieces
    if len(carried.shape) == 4:
        handed_on = carried.at[:, pairs]
    else:
        handed_on = carried.at[pl.ds(0, carried_out.shape[0])]
    handing = pltpu.make_async_copy(handed_on, carried_out, semaphore.at[0])
    handing.start()

    count = jnp.int32(0)
    for c in range(begin, end):
        for k in range(slots):
            item = items[k, c]
            listed[count] = item
            count = count + jnp.where(item != 0, 1, 0)
    for u in range(TAIL_GROUP):
        listed[count + u] = begin + (begin + NEAR_REACH) * 64

    ones = jnp.ones((3, leaf_size), f32)
    pad = jnp.zeros((2, leaf_size), f32)
    for w in range(begin, end + 2 * NEAR_REACH):
        own = NEAR_REACH <= w < NEAR_REACH + leaves
        if own:
            lanes = slice((w - NEAR_REACH) * leaf_size, (w - NEAR_REACH + 1) * leaf_size)
            place, value = points[:, lanes], probes[:, lanes]
        else:
            first = (w if w < NEAR_REACH else w - NEAR_REACH - leaves) * pieces
            parts = range(first, first + pieces)
            value = jnp.concatenate([side[pairs + 1 + j] for j in parts], axis=1)
            place = jnp.concatenate(
                [
                    jnp.concatenate(
                        [side[pairs + 1 + edge_blocks + d, j : j + 1, :] for j in parts], axis=1
                    )
                    for d in range(2)
                ],
                axis=0,
            )
        values[w] = stacked_halves(value)
        scaled = (place - 0.5) * coordinate_scale
        first = scaled.astype(bf16).astype(f32)
        second = (scaled - first).astype(bf16).astype(f32)
        kept = first + second
        norm = kept[0:1] * kept[0:1] + kept[1:2] * kept[1:2]
        norm1 = norm.astype(bf16).astype(f32)
        rest = norm - norm1
        norm2 = rest.astype(bf16).astype(f32)
        norms = jnp.concatenate([norm1, norm2, rest - norm2], axis=0)
        rows = jnp.concatenate([first, second, first, second, norms, ones, pad], axis=0)
        source[w] = rows.T.astype(bf16)
        if begin <= w - NEAR_REACH < end:
            target[w - NEAR_REACH] = jnp.concatenate(
                [-2.0 * first, -2.0 * first, -2.0 * second, -2.0 * second, ones, norms, pad], axis=0
            ).astype(bf16)
    total[...] = jnp.zeros_like(total)

    def tile(i):
        item = listed[i]
        c, s, times = item & 63, (item >> 6) & 63, item >> 12
        squared = jnp.dot(source[s], target[c], preferred_element_type=f32)
        squared = jnp.maximum(squared, tiny)
        distance = squared * lax.rsqrt(squared)
        high, low = halves((distance + 1.0 / ln2) * jnp.exp2(-distance))
        both = values[s]
        wide = jnp.dot(both, high, preferred_element_type=f32)
        rest = jnp.dot(both[:16], low, preferred_element_type=f32)
        return c, (wide[:16] + wide[16:] + rest) * (times.astype(f32) * ln2)

    def group(size, first):
        def step(t, carry):
            for c, term in [tile(first + t * size + u) for u in range(size)]:
                total[c] += term
            return carry

        return step

    full = count // GROUP
    lax.fori_loop(0, full, group(GROUP, 0), 0)
    rest = count - full * GROUP
    lax.fori_loop(0, (rest + TAIL_GROUP - 1) // TAIL_GROUP, group(TAIL_GROUP, full * GROUP), 0)
    for c in range(begin, end):
        out[:, (c - begin) * leaf_size : (c - begin + 1) * leaf_size] = total[c]
    handing.wait()


def fill_table(table, blocks, start):
    count, _, lanes = blocks.shape
    half = lanes // 2
    for m in range(count):
        block = blocks[m]
        swapped = jnp.concatenate([block[:, half:], block[:, :half]], axis=1)
        table[start + 2 * m] = stacked_halves(block)
        table[start + 2 * m + 1] = stacked_halves(swapped)


def picked(table, rows, low_lanes):
    pieces = []
    for k in range(0, len(rows) - 1, 2):
        pieces.append(jnp.where(low_lanes, table[rows[k]], table[rows[k + 1] ^ 1]))
    if len(rows) % 2:
        pieces.append(table[rows[-1]][:, : low_lanes.shape[1] // 2])
    return jnp.concatenate(pieces, axis=1)


def coupled_pairs(picks, couples):
    slots, rank, _ = couples.shape
    result = jnp.zeros((16, rank), f32)
    low_lanes = lax.broadcasted_iota(jnp.int32, (rank, 2 * rank), 1) < rank
    for start in range(0, slots, 8):
        pairs = (min(slots - start, 8) + 1) // 2
        highs, lows = [], []
        for m in range(pairs):
            even = couples[start + m]
            if start + pairs + m < slots:
                odd = couples[start + pairs + m]
            else:
                odd = jnp.zeros_like(even)
            high, low = halves(jnp.concatenate([even, odd], axis=1))
            highs.append(high)
            lows.append(low)
        right = jnp.concatenate(
            [jnp.concatenate(highs, axis=0), jnp.concatenate(lows, axis=0)], axis=1
        )
        left = jnp.concatenate(
            [picks(start, pairs), picks(start + pairs, pairs)], axis=0
        )
        wide = jnp.dot(left, right, preferred_element_type=f32)
        first = wide[:16, : 2 * rank] + wide[16:32, : 2 * rank] + wide[:16, 2 * rank :]
        second = wide[32:48, : 2 * rank] + wide[48:, : 2 * rank] + wide[32:48, 2 * rank :]
        result = result + first[:, :rank] + second[:, rank:]
    return result


def coupled(both, couples):
    count, rank, _ = couples.shape
    high, low = halves(couples.reshape(count * rank, rank))
    wide = jnp.dot(both, jnp.concatenate([high, low], axis=1), preferred_element_type=f32)
    return wide[:16, :rank] + wide[16:, :rank] + wide[:16, rank:]


def far_kernel(far, near, before, middle, after, couples, after_this, out, table):
    step = pl.program_id(0)
    per_step, slots, rank, _ = couples.shape
    leaves = far.shape[0]
    pairs = leaves // 2
    empty = (2 * FAR_REACH + 1) * leaves
    low_lanes = lax.broadcasted_iota(jnp.int32, (32, 2 * rank), 1) < rank

    @pl.when(step == 0)
    def _():
        for b in range(3):
            for place, blocks in ((b, before), (3 + b, middle), (6 + b, after)):
                fill_table(table, blocks.at[b, :pairs], place * leaves)
        table[empty] = jnp.zeros_like(table[empty])
        table[empty + 1] = jnp.zeros_like(table[empty])

    base = near[0, 0] - FAR_REACH * leaves

    def far_leaf(u):
        c = step * per_step + u

        def picks(start, count):
            rows = [far[c, k] if k < slots else -1 for k in range(start, start + count)]
            rows = [jnp.where(row >= 0, row - base, empty) for row in rows]
            return picked(table, rows, low_lanes)

        return coupled_pairs(picks, couples.at[u])

    for u in range(0, per_step, 2):
        out[u // 2] = jnp.concatenate([far_leaf(u), far_leaf(u + 1)], axis=1)


def down_kernel(
    near, box_list, column_list, boxes0, boxes1, boxes2, boxes3, couple_box_in, couple_column_in,
    transfer_box_in, far_in, near0_in, near1_in, near2_in, near3_in, transfer_in, basis_in, out,
    gathered, couple_box, couple_column, transfer_box, far_leaf, near0, near1, near2, near3,
    transfer_leaf, basis, semaphores,
):
    leaves, rank, leaf_size = basis.shape
    slots, column_slots = box_list.shape[1], column_list.shape[1]
    boxes = gathered.shape[0]
    low_lanes = lax.broadcasted_iota(jnp.int32, (32, 2 * rank), 1) < rank
    runs, place = [], 0
    for part in (boxes0, boxes1, boxes2, boxes3):
        runs.append((part, gathered.at[pl.ds(place, part.shape[0])]))
        place += part.shape[0]
    arriving = copies(
        runs
        + [
            (couple_box_in, couple_box),
            (couple_column_in, couple_column),
            (transfer_box_in, transfer_box),
            (far_in, far_leaf),
            (near0_in, near0),
            (near1_in, near1),
            (near2_in, near2),
            (near3_in, near3),
        ]
        + parts(transfer_in, transfer_leaf)
        + parts(basis_in, basis),
        semaphores,
    )
    later = 12 + CHUNKS
    for copy in arriving[:7]:
        copy.wait()

    first = near[0, 0] // leaves - boxes0.shape[0] - boxes1.shape[0] // 2

    def box_row(entry):
        return (jnp.where(entry >= 0, entry, 0) - first) & (boxes - 1)

    def pick(k):
        entry = box_list[0, k]
        return gathered[box_row(entry)] * jnp.where(entry >= 0, 1.0, 0.0)

    pieces = []
    for k in range(0, slots, 2):
        if k + 1 < slots:
            pieces.append(stacked_halves(jnp.where(low_lanes[:16], pick(k), exchanged(pick(k + 1)))))
        else:
            pieces.append(stacked_halves(pick(k))[:, :rank])
    far_box = coupled(jnp.concatenate(pieces, axis=1), couple_box[0])

    columns = []
    for k in range(column_slots):
        row = column_list[0, k]
        block = gathered[box_row(row * 4)]
        for j in range(1, 4):
            block = block + gathered[box_row(row * 4 + j)]
        columns.append(block * jnp.where(row >= 0, 1.0, 0.0))
    pieces = [
        stacked_halves(jnp.where(low_lanes[:16], exchanged(columns[k]), columns[k + 1]))
        for k in range(0, column_slots, 2)
    ]
    far_column = coupled(jnp.concatenate(pieces, axis=1), couple_column[0])
    down_box = far_box + product3(far_column, transfer_box[0], ((1,), (1,)))

    for copy in arriving[7:later]:
        copy.wait()
    high, low = halves(transfer_leaf[...].reshape(leaves * rank, rank))
    both = stacked_halves(down_box)
    wide = contract(both, high, ((1,), (1,)))
    from_box = wide[:16] + wide[16:] + contract(both[:16], low, ((1,), (1,)))

    lane = lax.broadcasted_iota(jnp.int32, (16, 4 * rank), 1)
    for m in range(leaves // 4):
        if m % (leaves // 4 // CHUNKS) == 0:
            arriving[later + m // (leaves // 4 // CHUNKS)].wait()
        down = from_box[:, m * 4 * rank : (m + 1) * 4 * rank]
        down = down + jnp.concatenate([far_leaf[2 * m], far_leaf[2 * m + 1]], axis=1)
        own_rows = [
            jnp.where((lane >= j * rank) & (lane < (j + 1) * rank), down, 0.0) for j in range(4)
        ]
        left = stacked_halves(jnp.concatenate(own_rows, axis=0))
        high, low = halves(basis[4 * m : 4 * m + 4].reshape(4 * rank, leaf_size))
        wide = jnp.dot(left, high, preferred_element_type=f32)
        rest = jnp.dot(left[:64], low, preferred_element_type=f32)
        result = wide[:64] + wide[64:] + rest
        for j in range(4):
            c = 4 * m + j
            held = (near0, near1, near2, near3)[c // NEAR_REACH]
            place = c % NEAR_REACH
            near_value = held[:, place * leaf_size : (place + 1) * leaf_size]
            out[:, c * leaf_size : (c + 1) * leaf_size] = near_value + result[16 * j : 16 * j + 16]


def whole(count):
    return [pl.BlockSpec(memory_space=pltpu.VMEM)] * count


def scalars(count):
    return [pl.BlockSpec(memory_space=pltpu.SMEM)] * count


params = pltpu.CompilerParams(vmem_limit_bytes=60 * 2**20)


def cost(flops):
    return pl.CostEstimate(flops=flops, bytes_accessed=2**20, transcendentals=0)


def shifted(array, axis, by):
    devices = lax.axis_size(axis)
    return lax.ppermute(array, axis, [(i, (i + by) % devices) for i in range(devices)])


def hbm(count):
    return [pl.BlockSpec(memory_space=pl.ANY)] * count


def like(array):
    return pltpu.VMEM(array.shape, array.dtype)


def copy_semaphores(count):
    return pltpu.SemaphoreType.DMA((count,))


def near_call(name, begin, items, points, probes, side, carried):
    slots, leaves = items.shape
    probe_count = probes.shape[0]
    leaf_size = probes.shape[1] // leaves
    window = leaves + 2 * NEAR_REACH
    if carried.ndim == 4:
        handed_on = (carried.shape[0],) + carried.shape[2:]
    else:
        handed_on = (min(carried.shape[0], 27),) + carried.shape[1:]
    if name == "near_first":
        handed_on = (leaves // 2 + 1,) + carried.shape[1:]
    return pl.pallas_call(
        functools.partial(near_kernel, begin=begin, end=begin + NEAR_REACH),
        out_shape=(
            jax.ShapeDtypeStruct((probe_count, NEAR_REACH * leaf_size), f32),
            jax.ShapeDtypeStruct(handed_on, f32),
        ),
        in_specs=scalars(1) + whole(3) + hbm(1),
        out_specs=tuple(whole(1) + hbm(1)),
        scratch_shapes=[
            pltpu.VMEM((window, 2 * probe_count, leaf_size), bf16),
            pltpu.VMEM((window, leaf_size, FEATURES), bf16),
            pltpu.VMEM((leaves, FEATURES, leaf_size), bf16),
            pltpu.VMEM((leaves, probe_count, leaf_size), f32),
            pltpu.SMEM((leaves * slots + 2 * GROUP,), jnp.int32),
            copy_semaphores(1),
        ],
        compiler_params=params,
        cost_estimate=cost(10_000_000_000),
        name=name,
    )(items, points, probes, side, carried)


def per_device(
    points,
    probes,
    basis,
    transfer_leaf,
    transfer_box,
    couple_leaf,
    couple_box,
    couple_column,
    near_list,
    far_list,
    box_list,
    column_list,
):
    leaves, leaf_size, rank = basis.shape
    probe_count = probes.shape[0]
    near_slots = near_list.T
    basis = basis.transpose(0, 2, 1)
    pairs = leaves // 2
    blocks = pairs + 1 + NEAR_REACH * leaf_size // 128 + 2

    edges = jax.ShapeDtypeStruct((blocks, probe_count, 2 * rank), f32)
    bundle_last, bundle_first, items = pl.pallas_call(
        skeleton_kernel,
        out_shape=(edges, edges, jax.ShapeDtypeStruct(near_slots.shape, jnp.int32)),
        in_specs=whole(2) + hbm(3) + whole(1),
        out_specs=tuple(whole(3)),
        scratch_shapes=[like(probes), like(basis), like(transfer_leaf)]
        + [copy_semaphores(1 + 2 * CHUNKS)],
        compiler_params=params,
        name="skeletons",
    )(near_slots, points, probes, basis, transfer_leaf, transfer_box)

    near_leaves = functools.partial(near_call, items=items, points=points, probes=probes)
    left, right = shifted(bundle_last, ring, 1), shifted(bundle_first, ring, -1)
    near1, own = near_leaves("near_first", NEAR_REACH, side=bundle_first, carried=bundle_last)

    middle = jnp.stack([left[: pairs + 1], own, right[: pairs + 1]])
    before, after = shifted(middle, ring, 3), shifted(middle, ring, -3)
    near2, three = near_leaves("near_second", 2 * NEAR_REACH, side=bundle_first, carried=middle)

    nine = jnp.concatenate([before[:, pairs], three, after[:, pairs]])
    nine_before, nine_after = shifted(nine, ring, 9), shifted(nine, ring, -9)
    near0, nine = near_leaves("near_third", 0, side=left, carried=nine)

    more = jnp.concatenate([nine_before, nine, nine_after])
    more_before, more_after = shifted(more, ring, 27), shifted(more, ring, -27)
    near3, more = near_leaves("near_fourth", leaves - NEAR_REACH, side=right, carried=more)

    count = lax.axis_size(ring)
    missing = (count - 3 * more.shape[0] - more.shape[0]) // 2
    inner = jnp.concatenate([more_before[-missing:], more, more_after[:missing]])
    opposite = shifted(inner, ring, count // 2)

    window = pl.BlockSpec(middle.shape, lambda i: (0, 0, 0, 0))
    far_leaf = pl.pallas_call(
        far_kernel,
        grid=(leaves // FAR_STEP,),
        out_shape=jax.ShapeDtypeStruct((pairs, probe_count, 2 * rank), f32),
        in_specs=scalars(2)
        + [window] * 3
        + [pl.BlockSpec((FAR_STEP,) + couple_leaf.shape[1:], lambda i: (i, 0, 0, 0))]
        + hbm(1),
        out_specs=pl.BlockSpec((FAR_STEP // 2, probe_count, 2 * rank), lambda i: (i, 0, 0)),
        scratch_shapes=[
            pltpu.VMEM(((2 * FAR_REACH + 1) * leaves + 2, 2 * probe_count, 2 * rank), bf16)
        ],
        compiler_params=params,
        cost_estimate=cost(8_000_000_000),
        name="far",
    )(far_list, near_slots, before, middle, after, couple_leaf, inner)

    held = (couple_box, couple_column, transfer_box, far_leaf, near0, near1, near2, near3)
    held += (transfer_leaf, basis)
    return pl.pallas_call(
        down_kernel,
        out_shape=jax.ShapeDtypeStruct(probes.shape, f32),
        in_specs=scalars(3) + hbm(14),
        out_specs=pl.BlockSpec(memory_space=pltpu.VMEM),
        scratch_shapes=[pltpu.VMEM((count, probe_count, 2 * rank), f32)]
        + [like(array) for array in held]
        + [copy_semaphores(12 + 2 * CHUNKS)],
        compiler_params=params,
        name="down",
    )(near_slots, box_list, column_list, more_before, more, more_after, opposite, *held)


def solution(mesh):
    placed = (
        P(None, ring),
        P(None, ring),
        P(ring, None, None),
        P(ring, None, None),
        P(ring, None, None),
        P(ring, None, None, None),
        P(ring, None, None, None),
        P("leaf", None, None, None),
        P(ring, None),
        P(ring, None),
        P(ring, None),
        P("leaf", None),
    )
    return jax.shard_map(
        per_device, mesh=mesh, in_specs=placed, out_specs=P(None, ring), check_vma=False
    )
```

```python
import functools
import math

import jax
import jax.numpy as jnp
from jax import lax
from jax.experimental import pallas as pl
from jax.experimental.pallas import tpu as pltpu
from jax.sharding import PartitionSpec as P

NEAR_REACH = 8
FAR_REACH = 4
FEATURES = 16
GROUP = 12
TAIL_GROUP = 4
FAR_STEP = 2
CHUNKS = 4

matern_rate = math.sqrt(3.0) / 0.1
coordinate_scale = matern_rate * math.log2(math.e)
ln2 = math.log(2.0)
tiny = 1e-20
f32 = jnp.float32
bf16 = jnp.bfloat16
vmem_bytes = 60 * 2**20
ring = ("leaf", "sub")


def halves(array):
    high = array.astype(bf16)
    return high, (array - high.astype(f32)).astype(bf16)


def stacked_halves(array):
    return jnp.concatenate(halves(array), axis=0)


def contract(left, right, dims):
    return lax.dot_general(left, right, (dims, ((), ())), preferred_element_type=f32)


def product3(left, right, dims=((1,), (0,))):
    rows = left.shape[0]
    high, low = halves(right)
    both = stacked_halves(left)
    wide = contract(both, high, dims)
    return wide[:rows] + wide[rows:] + contract(both[:rows], low, dims)


def copies(pairs, semaphores):
    made = [
        pltpu.make_async_copy(source, held, semaphores.at[i])
        for i, (source, held) in enumerate(pairs)
    ]
    for copy in made:
        copy.start()
    return made


def parts(source, held):
    length = source.shape[0] // CHUNKS
    runs = [pl.ds(i * length, length) for i in range(CHUNKS)]
    return [(source.at[run], held.at[run]) for run in runs]


def exchanged(block):
    half = block.shape[1] // 2
    return jnp.concatenate([block[:, half:], block[:, :half]], axis=1)


def skeleton_kernel(
    near, points, probes_in, basis_in, transfer_in, transfer_box, out, out_first, items,
    probes, basis, transfer_leaf, semaphores,
):
    leaves, rank, leaf_size = basis.shape
    arriving = copies(
        [(probes_in, probes)] + parts(basis_in, basis) + parts(transfer_in, transfer_leaf),
        semaphores,
    )
    slots = near.shape[0]
    pairs = leaves // 2
    low_lanes = lax.broadcasted_iota(jnp.int32, (16, 2 * rank), 1) < rank

    leaf = lax.broadcasted_iota(jnp.int32, (1, leaves), 1)
    rows = [near[k : k + 1, :] for k in range(slots)]
    for k in range(slots):
        new = rows[k] >= 0
        times = jnp.ones_like(leaf)
        for j in range(k):
            new = new & (rows[j] != rows[k])
        for j in range(k + 1, slots):
            times = times + jnp.where(rows[j] == rows[k], 1, 0)
        place = rows[k] - rows[0] + leaf + NEAR_REACH
        items[k : k + 1, :] = jnp.where(new, leaf + place * 64 + times * 4096, 0)

    arriving[0].wait()
    width = probes.shape[1]
    edge = NEAR_REACH * leaf_size
    for side, start in ((out, width - edge), (out_first, 0)):
        for j in range(edge // 128):
            lanes = slice(start + j * 128, start + (j + 1) * 128)
            side[pairs + 1 + j] = probes[:, lanes]
            side[pairs + 1 + edge // 128, j : j + 1, :] = points[0:1, lanes]
            side[pairs + 2 + edge // 128, j : j + 1, :] = points[1:2, lanes]

    def leaf_probes(c):
        return stacked_halves(probes[:, c * leaf_size : (c + 1) * leaf_size])

    def summed(wide):
        return wide[:16] + wide[16:] + exchanged(wide[:16])

    skeletons = []
    for m in range(pairs):
        if m % (pairs // CHUNKS) == 0:
            arriving[1 + m // (pairs // CHUNKS)].wait()
        left = jnp.concatenate([leaf_probes(2 * m), leaf_probes(2 * m + 1)], axis=0)
        right = jnp.concatenate([stacked_halves(basis[2 * m]), stacked_halves(basis[2 * m + 1])], axis=0)
        wide = contract(left, right, ((1,), (1,)))
        even, odd = summed(wide[:32, : 2 * rank]), summed(wide[32:, 2 * rank :])
        pair = jnp.where(low_lanes, even, exchanged(odd))
        out[m] = pair
        out_first[m] = pair
        skeletons.append(pair)
    for copy in arriving[1 + CHUNKS :]:
        copy.wait()
    high, low = halves(transfer_leaf[...].reshape(leaves * rank, rank))
    wide = jnp.dot(
        stacked_halves(jnp.concatenate(skeletons, axis=1)),
        jnp.concatenate([high, low], axis=1),
        preferred_element_type=f32,
    )
    box = summed(wide)[:, :rank]
    block = jnp.concatenate([box, product3(box, transfer_box[0])], axis=1)
    out[pairs] = block
    out_first[pairs] = block


def near_kernel(
    items, points, probes, side, carried, out, carried_out,
    values, source, target, total, listed, *, begin, end
):
    slots, leaves = items.shape
    leaf_size = target.shape[2]
    pieces = leaf_size // 128
    pairs = leaves // 2
    edge_blocks = NEAR_REACH * pieces
    for i in range(carried_out.shape[0]):
        carried_out[i] = carried[i, pairs] if len(carried.shape) == 4 else carried[i]

    count = jnp.int32(0)
    for c in range(begin, end):
        for k in range(slots):
            item = items[k, c]
            listed[count] = item
            count = count + jnp.where(item != 0, 1, 0)
    for u in range(TAIL_GROUP):
        listed[count + u] = begin + (begin + NEAR_REACH) * 64

    ones = jnp.ones((3, leaf_size), f32)
    pad = jnp.zeros((2, leaf_size), f32)
    for w in range(begin, end + 2 * NEAR_REACH):
        own = NEAR_REACH <= w < NEAR_REACH + leaves
        if own:
            lanes = slice((w - NEAR_REACH) * leaf_size, (w - NEAR_REACH + 1) * leaf_size)
            place, value = points[:, lanes], probes[:, lanes]
        else:
            first = (w if w < NEAR_REACH else w - NEAR_REACH - leaves) * pieces
            parts = range(first, first + pieces)
            value = jnp.concatenate([side[pairs + 1 + j] for j in parts], axis=1)
            place = jnp.concatenate(
                [
                    jnp.concatenate(
                        [side[pairs + 1 + edge_blocks + d, j : j + 1, :] for j in parts], axis=1
                    )
                    for d in range(2)
                ],
                axis=0,
            )
        values[w] = stacked_halves(value)
        scaled = (place - 0.5) * coordinate_scale
        first = scaled.astype(bf16).astype(f32)
        second = (scaled - first).astype(bf16).astype(f32)
        kept = first + second
        norm = kept[0:1] * kept[0:1] + kept[1:2] * kept[1:2]
        norm1 = norm.astype(bf16).astype(f32)
        rest = norm - norm1
        norm2 = rest.astype(bf16).astype(f32)
        norms = jnp.concatenate([norm1, norm2, rest - norm2], axis=0)
        rows = jnp.concatenate([first, second, first, second, norms, ones, pad], axis=0)
        source[w] = rows.T.astype(bf16)
        if begin <= w - NEAR_REACH < end:
            target[w - NEAR_REACH] = jnp.concatenate(
                [-2.0 * first, -2.0 * first, -2.0 * second, -2.0 * second, ones, norms, pad], axis=0
            ).astype(bf16)
    total[...] = jnp.zeros_like(total)

    def tile(i):
        item = listed[i]
        c, s, times = item & 63, (item >> 6) & 63, item >> 12
        squared = jnp.dot(source[s], target[c], preferred_element_type=f32)
        squared = jnp.maximum(squared, tiny)
        distance = squared * lax.rsqrt(squared)
        high, low = halves((distance + 1.0 / ln2) * jnp.exp2(-distance))
        both = values[s]
        wide = jnp.dot(both, high, preferred_element_type=f32)
        rest = jnp.dot(both[:16], low, preferred_element_type=f32)
        return c, (wide[:16] + wide[16:] + rest) * (times.astype(f32) * ln2)

    def group(size, first):
        def step(t, carry):
            for c, term in [tile(first + t * size + u) for u in range(size)]:
                total[c] += term
            return carry

        return step

    full = count // GROUP
    lax.fori_loop(0, full, group(GROUP, 0), 0)
    rest = count - full * GROUP
    lax.fori_loop(0, (rest + TAIL_GROUP - 1) // TAIL_GROUP, group(TAIL_GROUP, full * GROUP), 0)
    for c in range(begin, end):
        out[:, (c - begin) * leaf_size : (c - begin + 1) * leaf_size] = total[c]


def fill_table(table, blocks, start):
    count, _, lanes = blocks.shape
    half = lanes // 2
    for m in range(count):
        block = blocks[m]
        swapped = jnp.concatenate([block[:, half:], block[:, :half]], axis=1)
        table[start + 2 * m] = stacked_halves(block)
        table[start + 2 * m + 1] = stacked_halves(swapped)


def picked(table, rows, low_lanes):
    pieces = []
    for k in range(0, len(rows) - 1, 2):
        pieces.append(jnp.where(low_lanes, table[rows[k]], table[rows[k + 1] ^ 1]))
    if len(rows) % 2:
        pieces.append(table[rows[-1]][:, : low_lanes.shape[1] // 2])
    return jnp.concatenate(pieces, axis=1)


def coupled_pairs(picks, couples):
    slots, rank, _ = couples.shape
    result = jnp.zeros((16, rank), f32)
    low_lanes = lax.broadcasted_iota(jnp.int32, (rank, 2 * rank), 1) < rank
    for start in range(0, slots, 8):
        pairs = (min(slots - start, 8) + 1) // 2
        highs, lows = [], []
        for m in range(pairs):
            even = couples[start + m]
            if start + pairs + m < slots:
                odd = couples[start + pairs + m]
            else:
                odd = jnp.zeros_like(even)
            high, low = halves(jnp.concatenate([even, odd], axis=1))
            highs.append(high)
            lows.append(low)
        right = jnp.concatenate(
            [jnp.concatenate(highs, axis=0), jnp.concatenate(lows, axis=0)], axis=1
        )
        left = jnp.concatenate(
            [picks(start, pairs), picks(start + pairs, pairs)], axis=0
        )
        wide = jnp.dot(left, right, preferred_element_type=f32)
        first = wide[:16, : 2 * rank] + wide[16:32, : 2 * rank] + wide[:16, 2 * rank :]
        second = wide[32:48, : 2 * rank] + wide[48:, : 2 * rank] + wide[32:48, 2 * rank :]
        result = result + first[:, :rank] + second[:, rank:]
    return result


def coupled(both, couples):
    count, rank, _ = couples.shape
    high, low = halves(couples.reshape(count * rank, rank))
    wide = jnp.dot(both, jnp.concatenate([high, low], axis=1), preferred_element_type=f32)
    return wide[:16, :rank] + wide[16:, :rank] + wide[:16, rank:]


def far_kernel(far, near, before, middle, after, couples, after_this, out, table):
    step = pl.program_id(0)
    per_step, slots, rank, _ = couples.shape
    leaves = far.shape[0]
    pairs = leaves // 2
    empty = (2 * FAR_REACH + 1) * leaves
    low_lanes = lax.broadcasted_iota(jnp.int32, (32, 2 * rank), 1) < rank

    @pl.when(step == 0)
    def _():
        for b in range(3):
            for place, blocks in ((b, before), (3 + b, middle), (6 + b, after)):
                fill_table(table, blocks.at[b, :pairs], place * leaves)
        table[empty] = jnp.zeros_like(table[empty])
        table[empty + 1] = jnp.zeros_like(table[empty])

    base = near[0, 0] - FAR_REACH * leaves

    def far_leaf(u):
        c = step * per_step + u

        def picks(start, count):
            rows = [far[c, k] if k < slots else -1 for k in range(start, start + count)]
            rows = [jnp.where(row >= 0, row - base, empty) for row in rows]
            return picked(table, rows, low_lanes)

        return coupled_pairs(picks, couples.at[u])

    for u in range(0, per_step, 2):
        out[u // 2] = jnp.concatenate([far_leaf(u), far_leaf(u + 1)], axis=1)


def down_kernel(
    near, box_list, column_list, boxes0, boxes1, boxes2, boxes3, couple_box_in, couple_column_in,
    transfer_box_in, far_in, near0_in, near1_in, near2_in, near3_in, transfer_in, basis_in, out,
    gathered, couple_box, couple_column, transfer_box, far_leaf, near0, near1, near2, near3,
    transfer_leaf, basis, semaphores,
):
    leaves, rank, leaf_size = basis.shape
    slots, column_slots = box_list.shape[1], column_list.shape[1]
    boxes = gathered.shape[0]
    low_lanes = lax.broadcasted_iota(jnp.int32, (32, 2 * rank), 1) < rank
    runs, place = [], 0
    for part in (boxes0, boxes1, boxes2, boxes3):
        runs.append((part, gathered.at[pl.ds(place, part.shape[0])]))
        place += part.shape[0]
    arriving = copies(
        runs
        + [
            (couple_box_in, couple_box),
            (couple_column_in, couple_column),
            (transfer_box_in, transfer_box),
            (far_in, far_leaf),
            (near0_in, near0),
            (near1_in, near1),
            (near2_in, near2),
            (near3_in, near3),
        ]
        + parts(transfer_in, transfer_leaf)
        + parts(basis_in, basis),
        semaphores,
    )
    later = 12 + CHUNKS
    for copy in arriving[:7]:
        copy.wait()

    first = near[0, 0] // leaves - boxes0.shape[0] - boxes1.shape[0] // 2

    def box_row(entry):
        return (jnp.where(entry >= 0, entry, 0) - first) & (boxes - 1)

    def pick(k):
        entry = box_list[0, k]
        return gathered[box_row(entry)] * jnp.where(entry >= 0, 1.0, 0.0)

    pieces = []
    for k in range(0, slots, 2):
        if k + 1 < slots:
            pieces.append(stacked_halves(jnp.where(low_lanes[:16], pick(k), exchanged(pick(k + 1)))))
        else:
            pieces.append(stacked_halves(pick(k))[:, :rank])
    far_box = coupled(jnp.concatenate(pieces, axis=1), couple_box[0])

    columns = []
    for k in range(column_slots):
        row = column_list[0, k]
        block = gathered[box_row(row * 4)]
        for j in range(1, 4):
            block = block + gathered[box_row(row * 4 + j)]
        columns.append(block * jnp.where(row >= 0, 1.0, 0.0))
    pieces = [
        stacked_halves(jnp.where(low_lanes[:16], exchanged(columns[k]), columns[k + 1]))
        for k in range(0, column_slots, 2)
    ]
    far_column = coupled(jnp.concatenate(pieces, axis=1), couple_column[0])
    down_box = far_box + product3(far_column, transfer_box[0], ((1,), (1,)))

    for copy in arriving[7:later]:
        copy.wait()
    high, low = halves(transfer_leaf[...].reshape(leaves * rank, rank))
    both = stacked_halves(down_box)
    wide = contract(both, high, ((1,), (1,)))
    from_box = wide[:16] + wide[16:] + contract(both[:16], low, ((1,), (1,)))

    lane = lax.broadcasted_iota(jnp.int32, (16, 4 * rank), 1)
    for m in range(leaves // 4):
        if m % (leaves // 4 // CHUNKS) == 0:
            arriving[later + m // (leaves // 4 // CHUNKS)].wait()
        down = from_box[:, m * 4 * rank : (m + 1) * 4 * rank]
        down = down + jnp.concatenate([far_leaf[2 * m], far_leaf[2 * m + 1]], axis=1)
        own_rows = [
            jnp.where((lane >= j * rank) & (lane < (j + 1) * rank), down, 0.0) for j in range(4)
        ]
        left = stacked_halves(jnp.concatenate(own_rows, axis=0))
        high, low = halves(basis[4 * m : 4 * m + 4].reshape(4 * rank, leaf_size))
        wide = jnp.dot(left, high, preferred_element_type=f32)
        rest = jnp.dot(left[:64], low, preferred_element_type=f32)
        result = wide[:64] + wide[64:] + rest
        for j in range(4):
            c = 4 * m + j
            held = (near0, near1, near2, near3)[c // NEAR_REACH]
            place = c % NEAR_REACH
            near_value = held[:, place * leaf_size : (place + 1) * leaf_size]
            out[:, c * leaf_size : (c + 1) * leaf_size] = near_value + result[16 * j : 16 * j + 16]


def whole(count):
    return [pl.BlockSpec(memory_space=pltpu.VMEM)] * count


def scalars(count):
    return [pl.BlockSpec(memory_space=pltpu.SMEM)] * count


def params(mebibytes):
    return pltpu.CompilerParams(vmem_limit_bytes=mebibytes * 2**20)


def cost(flops):
    return pl.CostEstimate(flops=flops, bytes_accessed=2**20, transcendentals=0)


def shifted(array, axis, by):
    devices = lax.axis_size(axis)
    return lax.ppermute(array, axis, [(i, (i + by) % devices) for i in range(devices)])


def hbm(count):
    return [pl.BlockSpec(memory_space=pl.ANY)] * count


def like(array):
    return pltpu.VMEM(array.shape, array.dtype)


def copy_semaphores(count):
    return pltpu.SemaphoreType.DMA((count,))


def near_call(name, begin, items, points, probes, side, carried):
    slots, leaves = items.shape
    probe_count = probes.shape[0]
    leaf_size = probes.shape[1] // leaves
    window = leaves + 2 * NEAR_REACH
    if carried.ndim == 4:
        handed_on = (carried.shape[0],) + carried.shape[2:]
    else:
        handed_on = (min(carried.shape[0], 27),) + carried.shape[1:]
    if name == "near_first":
        handed_on = (leaves // 2 + 1,) + carried.shape[1:]
    return pl.pallas_call(
        functools.partial(near_kernel, begin=begin, end=begin + NEAR_REACH),
        out_shape=(
            jax.ShapeDtypeStruct((probe_count, NEAR_REACH * leaf_size), f32),
            jax.ShapeDtypeStruct(handed_on, f32),
        ),
        in_specs=scalars(1) + whole(4),
        out_specs=tuple(whole(2)),
        scratch_shapes=[
            pltpu.VMEM((window, 2 * probe_count, leaf_size), bf16),
            pltpu.VMEM((window, leaf_size, FEATURES), bf16),
            pltpu.VMEM((leaves, FEATURES, leaf_size), bf16),
            pltpu.VMEM((leaves, probe_count, leaf_size), f32),
            pltpu.SMEM((leaves * slots + 2 * GROUP,), jnp.int32),
        ],
        compiler_params=params(16),
        cost_estimate=cost(10_000_000_000),
        name=name,
    )(items, points, probes, side, carried)


def per_device(
    points,
    probes,
    basis,
    transfer_leaf,
    transfer_box,
    couple_leaf,
    couple_box,
    couple_column,
    near_list,
    far_list,
    box_list,
    column_list,
):
    leaves, leaf_size, rank = basis.shape
    probe_count = probes.shape[0]
    near_slots = near_list.T
    basis = basis.transpose(0, 2, 1)
    pairs = leaves // 2
    blocks = pairs + 1 + NEAR_REACH * leaf_size // 128 + 2

    edges = jax.ShapeDtypeStruct((blocks, probe_count, 2 * rank), f32)
    bundle_last, bundle_first, items = pl.pallas_call(
        skeleton_kernel,
        out_shape=(edges, edges, jax.ShapeDtypeStruct(near_slots.shape, jnp.int32)),
        in_specs=whole(2) + hbm(3) + whole(1),
        out_specs=tuple(whole(3)),
        scratch_shapes=[like(probes), like(basis), like(transfer_leaf)]
        + [copy_semaphores(1 + 2 * CHUNKS)],
        compiler_params=params(60),
        name="skeletons",
    )(near_slots, points, probes, basis, transfer_leaf, transfer_box)

    near_leaves = functools.partial(near_call, items=items, points=points, probes=probes)
    left, right = shifted(bundle_last, ring, 1), shifted(bundle_first, ring, -1)
    near1, own = near_leaves("near_first", NEAR_REACH, side=bundle_first, carried=bundle_last)

    middle = jnp.stack([left[: pairs + 1], own, right[: pairs + 1]])
    before, after = shifted(middle, ring, 3), shifted(middle, ring, -3)
    near2, three = near_leaves("near_second", 2 * NEAR_REACH, side=bundle_first, carried=middle)

    nine = jnp.concatenate([before[:, pairs], three, after[:, pairs]])
    nine_before, nine_after = shifted(nine, ring, 9), shifted(nine, ring, -9)
    near0, nine = near_leaves("near_third", 0, side=left, carried=nine)

    more = jnp.concatenate([nine_before, nine, nine_after])
    more_before, more_after = shifted(more, ring, 27), shifted(more, ring, -27)
    near3, more = near_leaves("near_fourth", leaves - NEAR_REACH, side=right, carried=more)

    count = lax.axis_size(ring)
    missing = (count - 3 * more.shape[0] - more.shape[0]) // 2
    inner = jnp.concatenate([more_before[-missing:], more, more_after[:missing]])
    opposite = shifted(inner, ring, count // 2)

    window = pl.BlockSpec(middle.shape, lambda i: (0, 0, 0, 0))
    far_leaf = pl.pallas_call(
        far_kernel,
        grid=(leaves // FAR_STEP,),
        out_shape=jax.ShapeDtypeStruct((pairs, probe_count, 2 * rank), f32),
        in_specs=scalars(2)
        + [window] * 3
        + [pl.BlockSpec((FAR_STEP,) + couple_leaf.shape[1:], lambda i: (i, 0, 0, 0))]
        + hbm(1),
        out_specs=pl.BlockSpec((FAR_STEP // 2, probe_count, 2 * rank), lambda i: (i, 0, 0)),
        scratch_shapes=[
            pltpu.VMEM(((2 * FAR_REACH + 1) * leaves + 2, 2 * probe_count, 2 * rank), bf16)
        ],
        compiler_params=params(20),
        cost_estimate=cost(8_000_000_000),
        name="far",
    )(far_list, near_slots, before, middle, after, couple_leaf, inner)

    held = (couple_box, couple_column, transfer_box, far_leaf, near0, near1, near2, near3)
    held += (transfer_leaf, basis)
    return pl.pallas_call(
        down_kernel,
        out_shape=jax.ShapeDtypeStruct(probes.shape, f32),
        in_specs=scalars(3) + hbm(14),
        out_specs=pl.BlockSpec(memory_space=pltpu.VMEM),
        scratch_shapes=[pltpu.VMEM((count, probe_count, 2 * rank), f32)]
        + [like(array) for array in held]
        + [copy_semaphores(12 + 2 * CHUNKS)],
        compiler_params=params(40),
        name="down",
    )(near_slots, box_list, column_list, more_before, more, more_after, opposite, *held)


def solution(mesh):
    placed = (
        P(None, ring),
        P(None, ring),
        P(ring, None, None),
        P(ring, None, None),
        P(ring, None, None),
        P(ring, None, None, None),
        P(ring, None, None, None),
        P("leaf", None, None, None),
        P(ring, None),
        P(ring, None),
        P(ring, None),
        P("leaf", None),
    )
    return jax.shard_map(
        per_device, mesh=mesh, in_specs=placed, out_specs=P(None, ring), check_vma=False
    )
```

```python
import functools
import math

import jax
import jax.numpy as jnp
from jax import lax
from jax.experimental import pallas as pl
from jax.experimental.pallas import tpu as pltpu
from jax.sharding import PartitionSpec as P

NEAR_REACH = 8
FAR_REACH = 4
FEATURES = 16
GROUP = 12
TAIL_GROUP = 4
FAR_STEP = 2
CHUNKS = 4

matern_rate = math.sqrt(3.0) / 0.1
coordinate_scale = matern_rate * math.log2(math.e)
ln2 = math.log(2.0)
tiny = 1e-20
f32 = jnp.float32
bf16 = jnp.bfloat16
vmem_bytes = 60 * 2**20
ring = ("leaf", "sub")


def halves(array):
    high = array.astype(bf16)
    return high, (array - high.astype(f32)).astype(bf16)


def stacked_halves(array):
    return jnp.concatenate(halves(array), axis=0)


def contract(left, right, dims):
    return lax.dot_general(left, right, (dims, ((), ())), preferred_element_type=f32)


def product3(left, right, dims=((1,), (0,))):
    rows = left.shape[0]
    high, low = halves(right)
    both = stacked_halves(left)
    wide = contract(both, high, dims)
    return wide[:rows] + wide[rows:] + contract(both[:rows], low, dims)


def copies(pairs, semaphores):
    made = [
        pltpu.make_async_copy(source, held, semaphores.at[i])
        for i, (source, held) in enumerate(pairs)
    ]
    for copy in made:
        copy.start()
    return made


def parts(source, held):
    length = source.shape[0] // CHUNKS
    runs = [pl.ds(i * length, length) for i in range(CHUNKS)]
    return [(source.at[run], held.at[run]) for run in runs]


def exchanged(block):
    half = block.shape[1] // 2
    return jnp.concatenate([block[:, half:], block[:, :half]], axis=1)


def skeleton_kernel(
    near, points, probes_in, basis_in, transfer_in, transfer_box, out, out_first, sent, items,
    probes, basis, transfer_leaf, semaphores,
):
    leaves, rank, leaf_size = basis.shape
    arriving = copies(
        [(probes_in, probes)] + parts(basis_in, basis) + parts(transfer_in, transfer_leaf),
        semaphores,
    )
    slots = near.shape[0]
    pairs = leaves // 2
    low_lanes = lax.broadcasted_iota(jnp.int32, (16, 2 * rank), 1) < rank

    leaf = lax.broadcasted_iota(jnp.int32, (1, leaves), 1)
    rows = [near[k : k + 1, :] for k in range(slots)]
    for k in range(slots):
        new = rows[k] >= 0
        times = jnp.ones_like(leaf)
        for j in range(k):
            new = new & (rows[j] != rows[k])
        for j in range(k + 1, slots):
            times = times + jnp.where(rows[j] == rows[k], 1, 0)
        place = rows[k] - rows[0] + leaf + NEAR_REACH
        items[k : k + 1, :] = jnp.where(new, leaf + place * 64 + times * 4096, 0)

    arriving[0].wait()
    width = probes.shape[1]
    edge = NEAR_REACH * leaf_size
    for side, start in ((out, width - edge), (out_first, 0)):
        for j in range(edge // 128):
            lanes = slice(start + j * 128, start + (j + 1) * 128)
            side[pairs + j] = probes[:, lanes]
            side[pairs + edge // 128, j : j + 1, :] = points[0:1, lanes]
            side[pairs + 1 + edge // 128, j : j + 1, :] = points[1:2, lanes]

    def leaf_probes(c):
        return stacked_halves(probes[:, c * leaf_size : (c + 1) * leaf_size])

    def summed(wide):
        return wide[:16] + wide[16:] + exchanged(wide[:16])

    skeletons = []
    for m in range(pairs):
        if m % (pairs // CHUNKS) == 0:
            arriving[1 + m // (pairs // CHUNKS)].wait()
        left = jnp.concatenate([leaf_probes(2 * m), leaf_probes(2 * m + 1)], axis=0)
        right = jnp.concatenate([stacked_halves(basis[2 * m]), stacked_halves(basis[2 * m + 1])], axis=0)
        wide = contract(left, right, ((1,), (1,)))
        even, odd = summed(wide[:32, : 2 * rank]), summed(wide[32:, 2 * rank :])
        pair = jnp.where(low_lanes, even, exchanged(odd))
        out[m] = pair
        out_first[m] = pair
        skeletons.append(pair)
    for copy in arriving[1 + CHUNKS :]:
        copy.wait()
    high, low = halves(transfer_leaf[...].reshape(leaves * rank, rank))
    wide = jnp.dot(
        stacked_halves(jnp.concatenate(skeletons, axis=1)),
        jnp.concatenate([high, low], axis=1),
        preferred_element_type=f32,
    )
    box = summed(wide)[:, :rank]
    block = jnp.concatenate([box, product3(box, transfer_box[0])], axis=1)
    for i in range(sent.shape[0]):
        sent[i] = block


def near_kernel(
    items, points, probes, left, right, out, values, source, target, total, listed
):
    slots, leaves = items.shape
    leaf_size = target.shape[2]
    pieces = leaf_size // 128
    pairs = leaves // 2
    edge_blocks = NEAR_REACH * pieces

    count = jnp.int32(0)
    for c in range(leaves):
        for k in range(slots):
            item = items[k, c]
            listed[count] = item
            count = count + jnp.where(item != 0, 1, 0)
    for u in range(TAIL_GROUP):
        listed[count + u] = NEAR_REACH * 64

    ones = jnp.ones((3, leaf_size), f32)
    pad = jnp.zeros((2, leaf_size), f32)
    for w in range(leaves + 2 * NEAR_REACH):
        own = NEAR_REACH <= w < NEAR_REACH + leaves
        if own:
            lanes = slice((w - NEAR_REACH) * leaf_size, (w - NEAR_REACH + 1) * leaf_size)
            place, value = points[:, lanes], probes[:, lanes]
        else:
            side = left if w < NEAR_REACH else right
            first = (w if w < NEAR_REACH else w - NEAR_REACH - leaves) * pieces
            runs = range(first, first + pieces)
            value = jnp.concatenate([side[pairs + j] for j in runs], axis=1)
            place = jnp.concatenate(
                [
                    jnp.concatenate(
                        [side[pairs + edge_blocks + d, j : j + 1, :] for j in runs], axis=1
                    )
                    for d in range(2)
                ],
                axis=0,
            )
        values[w] = stacked_halves(value)
        scaled = (place - 0.5) * coordinate_scale
        first = scaled.astype(bf16).astype(f32)
        second = (scaled - first).astype(bf16).astype(f32)
        kept = first + second
        norm = kept[0:1] * kept[0:1] + kept[1:2] * kept[1:2]
        norm1 = norm.astype(bf16).astype(f32)
        rest = norm - norm1
        norm2 = rest.astype(bf16).astype(f32)
        norms = jnp.concatenate([norm1, norm2, rest - norm2], axis=0)
        rows = jnp.concatenate([first, second, first, second, norms, ones, pad], axis=0)
        source[w] = rows.T.astype(bf16)
        if own:
            target[w - NEAR_REACH] = jnp.concatenate(
                [-2.0 * first, -2.0 * first, -2.0 * second, -2.0 * second, ones, norms, pad], axis=0
            ).astype(bf16)
    total[...] = jnp.zeros_like(total)

    def tile(i):
        item = listed[i]
        c, s, times = item & 63, (item >> 6) & 63, item >> 12
        squared = jnp.dot(source[s], target[c], preferred_element_type=f32)
        squared = jnp.maximum(squared, tiny)
        distance = squared * lax.rsqrt(squared)
        high, low = halves((distance + 1.0 / ln2) * jnp.exp2(-distance))
        both = values[s]
        wide = jnp.dot(both, high, preferred_element_type=f32)
        rest = jnp.dot(both[:16], low, preferred_element_type=f32)
        return c, (wide[:16] + wide[16:] + rest) * (times.astype(f32) * ln2)

    def group(size, first):
        def step(t, carry):
            for c, term in [tile(first + t * size + u) for u in range(size)]:
                total[c] += term
            return carry

        return step

    full = count // GROUP
    lax.fori_loop(0, full, group(GROUP, 0), 0)
    rest = count - full * GROUP
    lax.fori_loop(0, (rest + TAIL_GROUP - 1) // TAIL_GROUP, group(TAIL_GROUP, full * GROUP), 0)
    for c in range(leaves):
        out[:, c * leaf_size : (c + 1) * leaf_size] = total[c]


def fill_table(table, blocks, start):
    count, _, lanes = blocks.shape
    half = lanes // 2
    for m in range(count):
        block = blocks[m]
        swapped = jnp.concatenate([block[:, half:], block[:, :half]], axis=1)
        table[start + 2 * m] = stacked_halves(block)
        table[start + 2 * m + 1] = stacked_halves(swapped)


def picked(table, rows, low_lanes):
    pieces = []
    for k in range(0, len(rows) - 1, 2):
        pieces.append(jnp.where(low_lanes, table[rows[k]], table[rows[k + 1] ^ 1]))
    if len(rows) % 2:
        pieces.append(table[rows[-1]][:, : low_lanes.shape[1] // 2])
    return jnp.concatenate(pieces, axis=1)


def coupled_pairs(picks, couples):
    slots, rank, _ = couples.shape
    result = jnp.zeros((16, rank), f32)
    low_lanes = lax.broadcasted_iota(jnp.int32, (rank, 2 * rank), 1) < rank
    for start in range(0, slots, 8):
        pairs = (min(slots - start, 8) + 1) // 2
        highs, lows = [], []
        for m in range(pairs):
            even = couples[start + m]
            if start + pairs + m < slots:
                odd = couples[start + pairs + m]
            else:
                odd = jnp.zeros_like(even)
            high, low = halves(jnp.concatenate([even, odd], axis=1))
            highs.append(high)
            lows.append(low)
        right = jnp.concatenate(
            [jnp.concatenate(highs, axis=0), jnp.concatenate(lows, axis=0)], axis=1
        )
        left = jnp.concatenate(
            [picks(start, pairs), picks(start + pairs, pairs)], axis=0
        )
        wide = jnp.dot(left, right, preferred_element_type=f32)
        first = wide[:16, : 2 * rank] + wide[16:32, : 2 * rank] + wide[:16, 2 * rank :]
        second = wide[32:48, : 2 * rank] + wide[48:, : 2 * rank] + wide[32:48, 2 * rank :]
        result = result + first[:, :rank] + second[:, rank:]
    return result


def coupled(both, couples):
    count, rank, _ = couples.shape
    high, low = halves(couples.reshape(count * rank, rank))
    wide = jnp.dot(both, jnp.concatenate([high, low], axis=1), preferred_element_type=f32)
    return wide[:16, :rank] + wide[16:, :rank] + wide[:16, rank:]


def far_kernel(far, near, before, middle, after, couples, out, table):
    step = pl.program_id(0)
    per_step, slots, rank, _ = couples.shape
    leaves = far.shape[0]
    empty = (2 * FAR_REACH + 1) * leaves
    low_lanes = lax.broadcasted_iota(jnp.int32, (32, 2 * rank), 1) < rank

    @pl.when(step == 0)
    def _():
        for b in range(3):
            for place, blocks in ((b, before), (3 + b, middle), (6 + b, after)):
                fill_table(table, blocks.at[b], place * leaves)
        table[empty] = jnp.zeros_like(table[empty])
        table[empty + 1] = jnp.zeros_like(table[empty])

    base = near[0, 0] - FAR_REACH * leaves

    def far_leaf(u):
        c = step * per_step + u

        def picks(start, count):
            rows = [far[c, k] if k < slots else -1 for k in range(start, start + count)]
            rows = [jnp.where(row >= 0, row - base, empty) for row in rows]
            return picked(table, rows, low_lanes)

        return coupled_pairs(picks, couples.at[u])

    for u in range(0, per_step, 2):
        out[u // 2] = jnp.concatenate([far_leaf(u), far_leaf(u + 1)], axis=1)


def down_kernel(
    box_list, column_list, boxes_in, couple_box_in, couple_column_in,
    transfer_box_in, far_in, near_in, transfer_in, basis_in, out,
    gathered, couple_box, couple_column, transfer_box, far_leaf, near, transfer_leaf, basis,
    semaphores,
):
    leaves, rank, leaf_size = basis.shape
    slots, column_slots = box_list.shape[1], column_list.shape[1]
    low_lanes = lax.broadcasted_iota(jnp.int32, (32, 2 * rank), 1) < rank
    arriving = copies(
        [
            (boxes_in, gathered),
            (couple_box_in, couple_box),
            (couple_column_in, couple_column),
            (transfer_box_in, transfer_box),
            (far_in, far_leaf),
            (near_in, near),
        ]
        + parts(transfer_in, transfer_leaf)
        + parts(basis_in, basis),
        semaphores,
    )
    later = 6 + CHUNKS
    for copy in arriving[:4]:
        copy.wait()

    def box_row(entry):
        return jnp.where(entry >= 0, entry, 0)

    def pick(k):
        entry = box_list[0, k]
        return gathered[box_row(entry)] * jnp.where(entry >= 0, 1.0, 0.0)

    pieces = []
    for k in range(0, slots, 2):
        if k + 1 < slots:
            pieces.append(stacked_halves(jnp.where(low_lanes[:16], pick(k), exchanged(pick(k + 1)))))
        else:
            pieces.append(stacked_halves(pick(k))[:, :rank])
    far_box = coupled(jnp.concatenate(pieces, axis=1), couple_box[0])

    columns = []
    for k in range(column_slots):
        row = column_list[0, k]
        block = gathered[box_row(row * 4)]
        for j in range(1, 4):
            block = block + gathered[box_row(row * 4 + j)]
        columns.append(block * jnp.where(row >= 0, 1.0, 0.0))
    pieces = [
        stacked_halves(jnp.where(low_lanes[:16], exchanged(columns[k]), columns[k + 1]))
        for k in range(0, column_slots, 2)
    ]
    far_column = coupled(jnp.concatenate(pieces, axis=1), couple_column[0])
    down_box = far_box + product3(far_column, transfer_box[0], ((1,), (1,)))

    for copy in arriving[4:later]:
        copy.wait()
    high, low = halves(transfer_leaf[...].reshape(leaves * rank, rank))
    both = stacked_halves(down_box)
    wide = contract(both, high, ((1,), (1,)))
    from_box = wide[:16] + wide[16:] + contract(both[:16], low, ((1,), (1,)))

    lane = lax.broadcasted_iota(jnp.int32, (16, 4 * rank), 1)
    for m in range(leaves // 4):
        if m % (leaves // 4 // CHUNKS) == 0:
            arriving[later + m // (leaves // 4 // CHUNKS)].wait()
        down = from_box[:, m * 4 * rank : (m + 1) * 4 * rank]
        down = down + jnp.concatenate([far_leaf[2 * m], far_leaf[2 * m + 1]], axis=1)
        own_rows = [
            jnp.where((lane >= j * rank) & (lane < (j + 1) * rank), down, 0.0) for j in range(4)
        ]
        left = stacked_halves(jnp.concatenate(own_rows, axis=0))
        high, low = halves(basis[4 * m : 4 * m + 4].reshape(4 * rank, leaf_size))
        wide = jnp.dot(left, high, preferred_element_type=f32)
        rest = jnp.dot(left[:64], low, preferred_element_type=f32)
        result = wide[:64] + wide[64:] + rest
        for j in range(4):
            c = 4 * m + j
            lanes = slice(c * leaf_size, (c + 1) * leaf_size)
            out[:, lanes] = near[:, lanes] + result[16 * j : 16 * j + 16]


def whole(count):
    return [pl.BlockSpec(memory_space=pltpu.VMEM)] * count


def scalars(count):
    return [pl.BlockSpec(memory_space=pltpu.SMEM)] * count


def params(mebibytes):
    return pltpu.CompilerParams(vmem_limit_bytes=mebibytes * 2**20)


def cost(flops):
    return pl.CostEstimate(flops=flops, bytes_accessed=2**20, transcendentals=0)


def shifted(array, axis, by):
    devices = lax.axis_size(axis)
    return lax.ppermute(array, axis, [(i, (i + by) % devices) for i in range(devices)])


def hbm(count):
    return [pl.BlockSpec(memory_space=pl.ANY)] * count


def like(array):
    return pltpu.VMEM(array.shape, array.dtype)


def copy_semaphores(count):
    return pltpu.SemaphoreType.DMA((count,))


def per_device(
    points,
    probes,
    basis,
    transfer_leaf,
    transfer_box,
    couple_leaf,
    couple_box,
    couple_column,
    near_list,
    far_list,
    box_list,
    column_list,
):
    leaves, leaf_size, rank = basis.shape
    probe_count = probes.shape[0]
    near_slots = near_list.T
    basis = basis.transpose(0, 2, 1)
    pairs = leaves // 2
    blocks = pairs + NEAR_REACH * leaf_size // 128 + 2
    devices = lax.axis_size(ring)

    edges = jax.ShapeDtypeStruct((blocks, probe_count, 2 * rank), f32)
    bundle_last, bundle_first, sent, items = pl.pallas_call(
        skeleton_kernel,
        out_shape=(
            edges,
            edges,
            jax.ShapeDtypeStruct((devices, probe_count, 2 * rank), f32),
            jax.ShapeDtypeStruct(near_slots.shape, jnp.int32),
        ),
        in_specs=whole(2) + hbm(3) + whole(1),
        out_specs=tuple(whole(4)),
        scratch_shapes=[like(probes), like(basis), like(transfer_leaf)]
        + [copy_semaphores(1 + 2 * CHUNKS)],
        compiler_params=params(60),
        name="skeletons",
    )(near_slots, points, probes, basis, transfer_leaf, transfer_box)

    left, right = shifted(bundle_last, ring, 1), shifted(bundle_first, ring, -1)
    boxes = lax.all_to_all(sent, ring, 0, 0, tiled=True)
    middle = jnp.stack([left[:pairs], bundle_last[:pairs], right[:pairs]])
    before, after = shifted(middle, ring, 3), shifted(middle, ring, -3)

    window = leaves + 2 * NEAR_REACH
    near_values = pl.pallas_call(
        near_kernel,
        out_shape=jax.ShapeDtypeStruct(probes.shape, f32),
        in_specs=scalars(1) + whole(4),
        out_specs=pl.BlockSpec(memory_space=pltpu.VMEM),
        scratch_shapes=[
            pltpu.VMEM((window, 2 * probe_count, leaf_size), bf16),
            pltpu.VMEM((window, leaf_size, FEATURES), bf16),
            pltpu.VMEM((leaves, FEATURES, leaf_size), bf16),
            pltpu.VMEM((leaves, probe_count, leaf_size), f32),
            pltpu.SMEM((leaves * near_slots.shape[0] + 2 * GROUP,), jnp.int32),
        ],
        compiler_params=params(16),
        cost_estimate=cost(20_000_000_000),
        name="near",
    )(items, points, probes, left, right)

    blocks3 = pl.BlockSpec(middle.shape, lambda i: (0, 0, 0, 0))
    far_leaf = pl.pallas_call(
        far_kernel,
        grid=(leaves // FAR_STEP,),
        out_shape=jax.ShapeDtypeStruct((pairs, probe_count, 2 * rank), f32),
        in_specs=scalars(2)
        + [blocks3] * 3
        + [pl.BlockSpec((FAR_STEP,) + couple_leaf.shape[1:], lambda i: (i, 0, 0, 0))],
        out_specs=pl.BlockSpec((FAR_STEP // 2, probe_count, 2 * rank), lambda i: (i, 0, 0)),
        scratch_shapes=[
            pltpu.VMEM(((2 * FAR_REACH + 1) * leaves + 2, 2 * probe_count, 2 * rank), bf16)
        ],
        compiler_params=params(20),
        cost_estimate=cost(8_000_000_000),
        name="far",
    )(far_list, near_slots, before, middle, after, couple_leaf)

    held = (boxes, couple_box, couple_column, transfer_box, far_leaf, near_values)
    held += (transfer_leaf, basis)
    return pl.pallas_call(
        down_kernel,
        out_shape=jax.ShapeDtypeStruct(probes.shape, f32),
        in_specs=scalars(2) + hbm(8),
        out_specs=pl.BlockSpec(memory_space=pltpu.VMEM),
        scratch_shapes=[like(array) for array in held] + [copy_semaphores(6 + 2 * CHUNKS)],
        compiler_params=params(40),
        name="down",
    )(box_list, column_list, *held)


def solution(mesh):
    placed = (
        P(None, ring),
        P(None, ring),
        P(ring, None, None),
        P(ring, None, None),
        P(ring, None, None),
        P(ring, None, None, None),
        P(ring, None, None, None),
        P("leaf", None, None, None),
        P(ring, None),
        P(ring, None),
        P(ring, None),
        P("leaf", None),
    )
    return jax.shard_map(
        per_device, mesh=mesh, in_specs=placed, out_specs=P(None, ring), check_vma=False
    )
```

```python
import functools
import math

import jax
import jax.numpy as jnp
from jax import lax
from jax.experimental import pallas as pl
from jax.experimental.pallas import tpu as pltpu
from jax.sharding import PartitionSpec as P

NEAR_REACH = 8
FAR_REACH = 4
FEATURES = 16
GROUP = 12
TAIL_GROUP = 4
FAR_STEP = 8
CHUNKS = 4

matern_rate = math.sqrt(3.0) / 0.1
coordinate_scale = matern_rate * math.log2(math.e)
ln2 = math.log(2.0)
tiny = 1e-20
f32 = jnp.float32
bf16 = jnp.bfloat16
vmem_bytes = 60 * 2**20
ring = ("leaf", "sub")


def halves(array):
    high = array.astype(bf16)
    return high, (array - high.astype(f32)).astype(bf16)


def stacked_halves(array):
    return jnp.concatenate(halves(array), axis=0)


def contract(left, right, dims):
    return lax.dot_general(left, right, (dims, ((), ())), preferred_element_type=f32)


def product3(left, right, dims=((1,), (0,))):
    rows = left.shape[0]
    high, low = halves(right)
    both = stacked_halves(left)
    wide = contract(both, high, dims)
    return wide[:rows] + wide[rows:] + contract(both[:rows], low, dims)


def copies(pairs, semaphores):
    made = [
        pltpu.make_async_copy(source, held, semaphores.at[i])
        for i, (source, held) in enumerate(pairs)
    ]
    for copy in made:
        copy.start()
    return made


def parts(source, held):
    length = source.shape[0] // CHUNKS
    runs = [pl.ds(i * length, length) for i in range(CHUNKS)]
    return [(source.at[run], held.at[run]) for run in runs]


def exchanged(block):
    half = block.shape[1] // 2
    return jnp.concatenate([block[:, half:], block[:, :half]], axis=1)


def skeleton_kernel(
    near, far, points, probes_in, basis_in, transfer_in, transfer_box, out, out_first, sent, items,
    probes, basis, transfer_leaf, semaphores,
):
    leaves, rank, leaf_size = basis.shape
    arriving = copies(
        [(probes_in, probes)] + parts(basis_in, basis) + parts(transfer_in, transfer_leaf),
        semaphores,
    )
    slots = near.shape[0]
    pairs = leaves // 2
    low_lanes = lax.broadcasted_iota(jnp.int32, (16, 2 * rank), 1) < rank

    leaf = lax.broadcasted_iota(jnp.int32, (1, leaves), 1)
    rows = [near[k : k + 1, :] for k in range(slots)]
    for k in range(slots):
        new = rows[k] >= 0
        times = jnp.ones_like(leaf)
        for j in range(k):
            new = new & (rows[j] != rows[k])
        for j in range(k + 1, slots):
            times = times + jnp.where(rows[j] == rows[k], 1, 0)
        place = rows[k] - rows[0] + leaf + NEAR_REACH
        items[k : k + 1, 0:leaves] = jnp.where(new, leaf + place * 64 + times * 4096, 0)
    empty = (2 * FAR_REACH + 1) * leaves
    place = far[...] - (near[0:1, 0:1] - FAR_REACH * leaves)
    items[slots : slots + leaves, 0 : far.shape[1]] = jnp.where(far[...] >= 0, place, empty)

    arriving[0].wait()
    width = probes.shape[1]
    edge = NEAR_REACH * leaf_size
    for side, start in ((out, width - edge), (out_first, 0)):
        for j in range(edge // 128):
            lanes = slice(start + j * 128, start + (j + 1) * 128)
            side[pairs + j] = probes[:, lanes]
            side[pairs + edge // 128, j : j + 1, :] = points[0:1, lanes]
            side[pairs + 1 + edge // 128, j : j + 1, :] = points[1:2, lanes]

    def leaf_probes(c):
        return stacked_halves(probes[:, c * leaf_size : (c + 1) * leaf_size])

    def summed(wide):
        return wide[:16] + wide[16:] + exchanged(wide[:16])

    skeletons = []
    for m in range(pairs):
        if m % (pairs // CHUNKS) == 0:
            arriving[1 + m // (pairs // CHUNKS)].wait()
        left = jnp.concatenate([leaf_probes(2 * m), leaf_probes(2 * m + 1)], axis=0)
        right = jnp.concatenate([stacked_halves(basis[2 * m]), stacked_halves(basis[2 * m + 1])], axis=0)
        wide = contract(left, right, ((1,), (1,)))
        even, odd = summed(wide[:32, : 2 * rank]), summed(wide[32:, 2 * rank :])
        pair = jnp.where(low_lanes, even, exchanged(odd))
        out[m] = pair
        out_first[m] = pair
        skeletons.append(pair)
    for copy in arriving[1 + CHUNKS :]:
        copy.wait()
    high, low = halves(transfer_leaf[...].reshape(leaves * rank, rank))
    wide = jnp.dot(
        stacked_halves(jnp.concatenate(skeletons, axis=1)),
        jnp.concatenate([high, low], axis=1),
        preferred_element_type=f32,
    )
    box = summed(wide)[:, :rank]
    block = jnp.concatenate([box, product3(box, transfer_box[0])], axis=1)
    for i in range(sent.shape[0]):
        sent[i] = block


def near_field(
    items, points, probes, left, right, out, values, source, target, total, listed, arriving
):
    leaves, _, leaf_size = target.shape
    slots = items.shape[0] - leaves
    pieces = leaf_size // 128
    pairs = leaves // 2
    edge_blocks = NEAR_REACH * pieces

    count = jnp.int32(0)
    for c in range(leaves):
        for k in range(slots):
            item = items[k, c]
            listed[count] = item
            count = count + jnp.where(item != 0, 1, 0)
    for u in range(TAIL_GROUP):
        listed[count + u] = NEAR_REACH * 64

    for copy in arriving:
        copy.wait()
    ones = jnp.ones((3, leaf_size), f32)
    pad = jnp.zeros((2, leaf_size), f32)
    for w in range(leaves + 2 * NEAR_REACH):
        own = NEAR_REACH <= w < NEAR_REACH + leaves
        if own:
            lanes = slice((w - NEAR_REACH) * leaf_size, (w - NEAR_REACH + 1) * leaf_size)
            place, value = points[:, lanes], probes[:, lanes]
        else:
            side = left if w < NEAR_REACH else right
            first = (w if w < NEAR_REACH else w - NEAR_REACH - leaves) * pieces
            runs = range(first, first + pieces)
            value = jnp.concatenate([side[pairs + j] for j in runs], axis=1)
            place = jnp.concatenate(
                [
                    jnp.concatenate(
                        [side[pairs + edge_blocks + d, j : j + 1, :] for j in runs], axis=1
                    )
                    for d in range(2)
                ],
                axis=0,
            )
        values[w] = stacked_halves(value)
        scaled = (place - 0.5) * coordinate_scale
        first = scaled.astype(bf16).astype(f32)
        second = (scaled - first).astype(bf16).astype(f32)
        kept = first + second
        norm = kept[0:1] * kept[0:1] + kept[1:2] * kept[1:2]
        norm1 = norm.astype(bf16).astype(f32)
        rest = norm - norm1
        norm2 = rest.astype(bf16).astype(f32)
        norms = jnp.concatenate([norm1, norm2, rest - norm2], axis=0)
        rows = jnp.concatenate([first, second, first, second, norms, ones, pad], axis=0)
        source[w] = rows.T.astype(bf16)
        if own:
            target[w - NEAR_REACH] = jnp.concatenate(
                [-2.0 * first, -2.0 * first, -2.0 * second, -2.0 * second, ones, norms, pad], axis=0
            ).astype(bf16)
    total[...] = jnp.zeros_like(total)

    def tile(i):
        item = listed[i]
        c, s, times = item & 63, (item >> 6) & 63, item >> 12
        squared = jnp.dot(source[s], target[c], preferred_element_type=f32)
        squared = jnp.maximum(squared, tiny)
        distance = squared * lax.rsqrt(squared)
        high, low = halves((distance + 1.0 / ln2) * jnp.exp2(-distance))
        both = values[s]
        wide = jnp.dot(both, high, preferred_element_type=f32)
        rest = jnp.dot(both[:16], low, preferred_element_type=f32)
        return c, (wide[:16] + wide[16:] + rest) * (times.astype(f32) * ln2)

    def group(size, first):
        def step(t, carry):
            for c, term in [tile(first + t * size + u) for u in range(size)]:
                total[c] += term
            return carry

        return step

    full = count // GROUP
    lax.fori_loop(0, full, group(GROUP, 0), 0)
    rest = count - full * GROUP
    lax.fori_loop(0, (rest + TAIL_GROUP - 1) // TAIL_GROUP, group(TAIL_GROUP, full * GROUP), 0)
    for c in range(leaves):
        out[:, c * leaf_size : (c + 1) * leaf_size] = total[c]


def fill_table(table, blocks, start):
    count, _, lanes = blocks.shape
    half = lanes // 2
    for m in range(count):
        block = blocks[m]
        swapped = jnp.concatenate([block[:, half:], block[:, :half]], axis=1)
        table[start + 2 * m] = stacked_halves(block)
        table[start + 2 * m + 1] = stacked_halves(swapped)


def picked(table, rows, low_lanes):
    pieces = []
    for k in range(0, len(rows) - 1, 2):
        pieces.append(jnp.where(low_lanes, table[rows[k]], table[rows[k + 1] ^ 1]))
    if len(rows) % 2:
        pieces.append(table[rows[-1]][:, : low_lanes.shape[1] // 2])
    return jnp.concatenate(pieces, axis=1)


def coupled_pairs(picks, couples):
    slots, rank, _ = couples.shape
    result = jnp.zeros((16, rank), f32)
    low_lanes = lax.broadcasted_iota(jnp.int32, (rank, 2 * rank), 1) < rank
    for start in range(0, slots, 8):
        pairs = (min(slots - start, 8) + 1) // 2
        highs, lows = [], []
        for m in range(pairs):
            even = couples[start + m]
            if start + pairs + m < slots:
                odd = couples[start + pairs + m]
            else:
                odd = jnp.zeros_like(even)
            high, low = halves(jnp.concatenate([even, odd], axis=1))
            highs.append(high)
            lows.append(low)
        right = jnp.concatenate(
            [jnp.concatenate(highs, axis=0), jnp.concatenate(lows, axis=0)], axis=1
        )
        left = jnp.concatenate(
            [picks(start, pairs), picks(start + pairs, pairs)], axis=0
        )
        wide = jnp.dot(left, right, preferred_element_type=f32)
        first = wide[:16, : 2 * rank] + wide[16:32, : 2 * rank] + wide[:16, 2 * rank :]
        second = wide[32:48, : 2 * rank] + wide[48:, : 2 * rank] + wide[32:48, 2 * rank :]
        result = result + first[:, :rank] + second[:, rank:]
    return result


def coupled(both, couples):
    count, rank, _ = couples.shape
    high, low = halves(couples.reshape(count * rank, rank))
    wide = jnp.dot(both, jnp.concatenate([high, low], axis=1), preferred_element_type=f32)
    return wide[:16, :rank] + wide[16:, :rank] + wide[:16, rank:]


def field_kernel(
    items, points_in, probes_in, left, right, before, middle, after, couples_in, out,
    far_out, points, probes, values, source, target, total, listed, table, couples, semaphores,
    held_semaphores,
):
    leaves, slots, rank, _ = couples.shape
    steps = leaves // FAR_STEP

    held = copies([(points_in, points), (probes_in, probes)], held_semaphores)

    def arriving(step):
        run = pl.ds(step * FAR_STEP, FAR_STEP)
        return pltpu.make_async_copy(couples_in.at[run], couples.at[run], semaphores.at[step])

    def start(step, carry):
        arriving(step).start()
        return carry

    lax.fori_loop(0, steps, start, 0)
    near_field(
        items, points, probes, left, right, out, values, source, target, total, listed, held
    )

    empty = (2 * FAR_REACH + 1) * leaves
    low_lanes = lax.broadcasted_iota(jnp.int32, (32, 2 * rank), 1) < rank
    for b in range(3):
        for place, blocks in ((b, before), (3 + b, middle), (6 + b, after)):
            fill_table(table, blocks.at[b], place * leaves)
    table[empty] = jnp.zeros_like(table[empty])
    table[empty + 1] = jnp.zeros_like(table[empty])
    first_row = items.shape[0] - leaves

    def far_leaf(c):
        def picks(start, count):
            listed_here = range(start, start + count)
            rows = [items[first_row + c, k] if k < slots else empty for k in listed_here]
            return picked(table, rows, low_lanes)

        return coupled_pairs(picks, couples.at[c])

    def far_step(step, carry):
        arriving(step).wait()
        for u in range(0, FAR_STEP, 2):
            c = step * FAR_STEP + u
            far_out[c // 2] = jnp.concatenate([far_leaf(c), far_leaf(c + 1)], axis=1)
        return carry

    lax.fori_loop(0, steps, far_step, 0)


def down_kernel(
    box_list, column_list, boxes_in, couple_box_in, couple_column_in,
    transfer_box_in, far_in, near_in, transfer_in, basis_in, out,
    gathered, couple_box, couple_column, transfer_box, far_leaf, near, transfer_leaf, basis,
    semaphores,
):
    leaves, rank, leaf_size = basis.shape
    slots, column_slots = box_list.shape[1], column_list.shape[1]
    low_lanes = lax.broadcasted_iota(jnp.int32, (32, 2 * rank), 1) < rank
    arriving = copies(
        [
            (boxes_in, gathered),
            (couple_box_in, couple_box),
            (couple_column_in, couple_column),
            (transfer_box_in, transfer_box),
            (far_in, far_leaf),
            (near_in, near),
        ]
        + parts(transfer_in, transfer_leaf)
        + parts(basis_in, basis),
        semaphores,
    )
    later = 6 + CHUNKS
    for copy in arriving[:4]:
        copy.wait()

    def box_row(entry):
        return jnp.where(entry >= 0, entry, 0)

    def pick(k):
        entry = box_list[0, k]
        return gathered[box_row(entry)] * jnp.where(entry >= 0, 1.0, 0.0)

    pieces = []
    for k in range(0, slots, 2):
        if k + 1 < slots:
            pieces.append(stacked_halves(jnp.where(low_lanes[:16], pick(k), exchanged(pick(k + 1)))))
        else:
            pieces.append(stacked_halves(pick(k))[:, :rank])
    far_box = coupled(jnp.concatenate(pieces, axis=1), couple_box[0])

    columns = []
    for k in range(column_slots):
        row = column_list[0, k]
        block = gathered[box_row(row * 4)]
        for j in range(1, 4):
            block = block + gathered[box_row(row * 4 + j)]
        columns.append(block * jnp.where(row >= 0, 1.0, 0.0))
    pieces = [
        stacked_halves(jnp.where(low_lanes[:16], exchanged(columns[k]), columns[k + 1]))
        for k in range(0, column_slots, 2)
    ]
    far_column = coupled(jnp.concatenate(pieces, axis=1), couple_column[0])
    down_box = far_box + product3(far_column, transfer_box[0], ((1,), (1,)))

    for copy in arriving[4:later]:
        copy.wait()
    high, low = halves(transfer_leaf[...].reshape(leaves * rank, rank))
    both = stacked_halves(down_box)
    wide = contract(both, high, ((1,), (1,)))
    from_box = wide[:16] + wide[16:] + contract(both[:16], low, ((1,), (1,)))

    lane = lax.broadcasted_iota(jnp.int32, (16, 4 * rank), 1)
    for m in range(leaves // 4):
        if m % (leaves // 4 // CHUNKS) == 0:
            arriving[later + m // (leaves // 4 // CHUNKS)].wait()
        down = from_box[:, m * 4 * rank : (m + 1) * 4 * rank]
        down = down + jnp.concatenate([far_leaf[2 * m], far_leaf[2 * m + 1]], axis=1)
        own_rows = [
            jnp.where((lane >= j * rank) & (lane < (j + 1) * rank), down, 0.0) for j in range(4)
        ]
        left = stacked_halves(jnp.concatenate(own_rows, axis=0))
        high, low = halves(basis[4 * m : 4 * m + 4].reshape(4 * rank, leaf_size))
        wide = jnp.dot(left, high, preferred_element_type=f32)
        rest = jnp.dot(left[:64], low, preferred_element_type=f32)
        result = wide[:64] + wide[64:] + rest
        for j in range(4):
            c = 4 * m + j
            lanes = slice(c * leaf_size, (c + 1) * leaf_size)
            out[:, lanes] = near[:, lanes] + result[16 * j : 16 * j + 16]


def whole(count):
    return [pl.BlockSpec(memory_space=pltpu.VMEM)] * count


def scalars(count):
    return [pl.BlockSpec(memory_space=pltpu.SMEM)] * count


def params(mebibytes):
    return pltpu.CompilerParams(vmem_limit_bytes=mebibytes * 2**20)


def cost(flops):
    return pl.CostEstimate(flops=flops, bytes_accessed=2**20, transcendentals=0)


def shifted(array, axis, by):
    devices = lax.axis_size(axis)
    return lax.ppermute(array, axis, [(i, (i + by) % devices) for i in range(devices)])


def hbm(count):
    return [pl.BlockSpec(memory_space=pl.ANY)] * count


def like(array):
    return pltpu.VMEM(array.shape, array.dtype)


def copy_semaphores(count):
    return pltpu.SemaphoreType.DMA((count,))


def per_device(
    points,
    probes,
    basis,
    transfer_leaf,
    transfer_box,
    couple_leaf,
    couple_box,
    couple_column,
    near_list,
    far_list,
    box_list,
    column_list,
):
    leaves, leaf_size, rank = basis.shape
    probe_count = probes.shape[0]
    near_slots = near_list.T
    basis = basis.transpose(0, 2, 1)
    pairs = leaves // 2
    blocks = pairs + NEAR_REACH * leaf_size // 128 + 2
    devices = lax.axis_size(ring)

    edges = jax.ShapeDtypeStruct((blocks, probe_count, 2 * rank), f32)
    bundle_last, bundle_first, sent, items = pl.pallas_call(
        skeleton_kernel,
        out_shape=(
            edges,
            edges,
            jax.ShapeDtypeStruct((devices, probe_count, 2 * rank), f32),
            jax.ShapeDtypeStruct((near_slots.shape[0] + leaves, 128), jnp.int32),
        ),
        in_specs=whole(3) + hbm(3) + whole(1),
        out_specs=tuple(whole(4)),
        scratch_shapes=[like(probes), like(basis), like(transfer_leaf)]
        + [copy_semaphores(1 + 2 * CHUNKS)],
        compiler_params=params(60),
        name="skeletons",
    )(near_slots, far_list, points, probes, basis, transfer_leaf, transfer_box)

    left, right = shifted(bundle_last, ring, 1), shifted(bundle_first, ring, -1)
    sent, left, right = lax.optimization_barrier((sent, left, right))
    boxes = lax.all_to_all(sent, ring, 0, 0, tiled=True)
    middle = jnp.stack([left[:pairs], bundle_last[:pairs], right[:pairs]])
    before, after = shifted(middle, ring, 3), shifted(middle, ring, -3)

    window = leaves + 2 * NEAR_REACH
    near_values, far_leaf = pl.pallas_call(
        field_kernel,
        out_shape=(
            jax.ShapeDtypeStruct(probes.shape, f32),
            jax.ShapeDtypeStruct((pairs, probe_count, 2 * rank), f32),
        ),
        in_specs=scalars(1) + hbm(2) + whole(5) + hbm(1),
        out_specs=tuple(whole(2)),
        scratch_shapes=[
            like(points),
            like(probes),
            pltpu.VMEM((window, 2 * probe_count, leaf_size), bf16),
            pltpu.VMEM((window, leaf_size, FEATURES), bf16),
            pltpu.VMEM((leaves, FEATURES, leaf_size), bf16),
            pltpu.VMEM((leaves, probe_count, leaf_size), f32),
            pltpu.SMEM((leaves * near_slots.shape[0] + 2 * GROUP,), jnp.int32),
            pltpu.VMEM(((2 * FAR_REACH + 1) * leaves + 2, 2 * probe_count, 2 * rank), bf16),
            like(couple_leaf),
            copy_semaphores(leaves // FAR_STEP),
            copy_semaphores(2),
        ],
        compiler_params=params(60),
        cost_estimate=cost(30_000_000_000),
        name="near_far",
    )(items, points, probes, left, right, before, middle, after, couple_leaf)

    held = (boxes, couple_box, couple_column, transfer_box, far_leaf, near_values)
    held += (transfer_leaf, basis)
    return pl.pallas_call(
        down_kernel,
        out_shape=jax.ShapeDtypeStruct(probes.shape, f32),
        in_specs=scalars(2) + hbm(8),
        out_specs=pl.BlockSpec(memory_space=pltpu.VMEM),
        scratch_shapes=[like(array) for array in held] + [copy_semaphores(6 + 2 * CHUNKS)],
        compiler_params=params(60),
        name="down",
    )(box_list, column_list, *held)


def solution(mesh):
    placed = (
        P(None, ring),
        P(None, ring),
        P(ring, None, None),
        P(ring, None, None),
        P(ring, None, None),
        P(ring, None, None, None),
        P(ring, None, None, None),
        P("leaf", None, None, None),
        P(ring, None),
        P(ring, None),
        P(ring, None),
        P("leaf", None),
    )
    return jax.shard_map(
        per_device, mesh=mesh, in_specs=placed, out_specs=P(None, ring), check_vma=False
    )
```

```python
import functools
import math

import jax
import jax.numpy as jnp
from jax import lax
from jax.experimental import pallas as pl
from jax.experimental.pallas import tpu as pltpu
from jax.sharding import PartitionSpec as P

NEAR_REACH = 8
FAR_REACH = 4
FEATURES = 16
GROUP = 12
TAIL_GROUP = 4
FAR_STEP = 4
CHUNKS = 4

matern_rate = math.sqrt(3.0) / 0.1
coordinate_scale = matern_rate * math.log2(math.e)
ln2 = math.log(2.0)
tiny = 1e-20
f32 = jnp.float32
bf16 = jnp.bfloat16
vmem_bytes = 60 * 2**20
ring = ("leaf", "sub")


def halves(array):
    high = array.astype(bf16)
    return high, (array - high.astype(f32)).astype(bf16)


def stacked_halves(array):
    return jnp.concatenate(halves(array), axis=0)


def contract(left, right, dims):
    return lax.dot_general(left, right, (dims, ((), ())), preferred_element_type=f32)


def product3(left, right, dims=((1,), (0,))):
    rows = left.shape[0]
    high, low = halves(right)
    both = stacked_halves(left)
    wide = contract(both, high, dims)
    return wide[:rows] + wide[rows:] + contract(both[:rows], low, dims)


def copies(pairs, semaphores):
    made = [
        pltpu.make_async_copy(source, held, semaphores.at[i])
        for i, (source, held) in enumerate(pairs)
    ]
    for copy in made:
        copy.start()
    return made


def parts(source, held):
    length = source.shape[0] // CHUNKS
    runs = [pl.ds(i * length, length) for i in range(CHUNKS)]
    return [(source.at[run], held.at[run]) for run in runs]


def exchanged(block):
    half = block.shape[1] // 2
    return jnp.concatenate([block[:, half:], block[:, :half]], axis=1)


def skeleton_kernel(
    near, far, points, probes_in, basis_in, transfer_in, transfer_box, out, out_first, sent, items,
    probes, basis, transfer_leaf, semaphores,
):
    leaves, rank, leaf_size = basis.shape
    arriving = copies(
        [(probes_in, probes)] + parts(basis_in, basis) + parts(transfer_in, transfer_leaf),
        semaphores,
    )
    slots = near.shape[0]
    pairs = leaves // 2
    low_lanes = lax.broadcasted_iota(jnp.int32, (16, 2 * rank), 1) < rank

    leaf = lax.broadcasted_iota(jnp.int32, (1, leaves), 1)
    rows = [near[k : k + 1, :] for k in range(slots)]
    for k in range(slots):
        new = rows[k] >= 0
        times = jnp.ones_like(leaf)
        for j in range(k):
            new = new & (rows[j] != rows[k])
        for j in range(k + 1, slots):
            times = times + jnp.where(rows[j] == rows[k], 1, 0)
        place = rows[k] - rows[0] + leaf + NEAR_REACH
        items[k : k + 1, 0:leaves] = jnp.where(new, leaf + place * 64 + times * 4096, 0)
    empty = (2 * FAR_REACH + 1) * leaves
    place = far[...] - (near[0:1, 0:1] - FAR_REACH * leaves)
    items[slots : slots + leaves, 0 : far.shape[1]] = jnp.where(far[...] >= 0, place, empty)

    arriving[0].wait()
    width = probes.shape[1]
    edge = NEAR_REACH * leaf_size
    for side, start in ((out, width - edge), (out_first, 0)):
        for j in range(edge // 128):
            lanes = slice(start + j * 128, start + (j + 1) * 128)
            side[pairs + j] = probes[:, lanes]
            side[pairs + edge // 128, j : j + 1, :] = points[0:1, lanes]
            side[pairs + 1 + edge // 128, j : j + 1, :] = points[1:2, lanes]

    def leaf_probes(c):
        return stacked_halves(probes[:, c * leaf_size : (c + 1) * leaf_size])

    def summed(wide):
        return wide[:16] + wide[16:] + exchanged(wide[:16])

    skeletons = []
    for m in range(pairs):
        if m % (pairs // CHUNKS) == 0:
            arriving[1 + m // (pairs // CHUNKS)].wait()
        left = jnp.concatenate([leaf_probes(2 * m), leaf_probes(2 * m + 1)], axis=0)
        right = jnp.concatenate([stacked_halves(basis[2 * m]), stacked_halves(basis[2 * m + 1])], axis=0)
        wide = contract(left, right, ((1,), (1,)))
        even, odd = summed(wide[:32, : 2 * rank]), summed(wide[32:, 2 * rank :])
        pair = jnp.where(low_lanes, even, exchanged(odd))
        out[m] = pair
        out_first[m] = pair
        skeletons.append(pair)
    for copy in arriving[1 + CHUNKS :]:
        copy.wait()
    high, low = halves(transfer_leaf[...].reshape(leaves * rank, rank))
    wide = jnp.dot(
        stacked_halves(jnp.concatenate(skeletons, axis=1)),
        jnp.concatenate([high, low], axis=1),
        preferred_element_type=f32,
    )
    box = summed(wide)[:, :rank]
    block = jnp.concatenate([box, product3(box, transfer_box[0])], axis=1)
    for i in range(sent.shape[0]):
        sent[i] = block


def near_field(
    items, points, probes, left, right, out, values, source, target, total, listed, arriving, groups
):
    leaves, _, leaf_size = target.shape
    slots = items.shape[0] - leaves
    pieces = leaf_size // 128
    pairs = leaves // 2
    edge_blocks = NEAR_REACH * pieces

    count = jnp.int32(0)
    served = [c for begin, end in groups for c in range(begin, end)]
    for c in served:
        for k in range(slots):
            item = items[k, c]
            listed[count] = item
            count = count + jnp.where(item != 0, 1, 0)
    for u in range(TAIL_GROUP):
        listed[count + u] = served[0] + (served[0] + NEAR_REACH) * 64

    for copy in arriving:
        copy.wait()
    ones = jnp.ones((3, leaf_size), f32)
    pad = jnp.zeros((2, leaf_size), f32)
    window = {c + j for c in served for j in range(2 * NEAR_REACH + 1)}
    for w in sorted(window):
        own = NEAR_REACH <= w < NEAR_REACH + leaves
        if own:
            lanes = slice((w - NEAR_REACH) * leaf_size, (w - NEAR_REACH + 1) * leaf_size)
            place, value = points[:, lanes], probes[:, lanes]
        else:
            side = left if w < NEAR_REACH else right
            first = (w if w < NEAR_REACH else w - NEAR_REACH - leaves) * pieces
            runs = range(first, first + pieces)
            value = jnp.concatenate([side[pairs + j] for j in runs], axis=1)
            place = jnp.concatenate(
                [
                    jnp.concatenate(
                        [side[pairs + edge_blocks + d, j : j + 1, :] for j in runs], axis=1
                    )
                    for d in range(2)
                ],
                axis=0,
            )
        values[w] = stacked_halves(value)
        scaled = (place - 0.5) * coordinate_scale
        first = scaled.astype(bf16).astype(f32)
        second = (scaled - first).astype(bf16).astype(f32)
        kept = first + second
        norm = kept[0:1] * kept[0:1] + kept[1:2] * kept[1:2]
        norm1 = norm.astype(bf16).astype(f32)
        rest = norm - norm1
        norm2 = rest.astype(bf16).astype(f32)
        norms = jnp.concatenate([norm1, norm2, rest - norm2], axis=0)
        rows = jnp.concatenate([first, second, first, second, norms, ones, pad], axis=0)
        source[w] = rows.T.astype(bf16)
        if w - NEAR_REACH in served:
            target[w - NEAR_REACH] = jnp.concatenate(
                [-2.0 * first, -2.0 * first, -2.0 * second, -2.0 * second, ones, norms, pad], axis=0
            ).astype(bf16)
    total[...] = jnp.zeros_like(total)

    def tile(i):
        item = listed[i]
        c, s, times = item & 63, (item >> 6) & 63, item >> 12
        squared = jnp.dot(source[s], target[c], preferred_element_type=f32)
        squared = jnp.maximum(squared, tiny)
        distance = squared * lax.rsqrt(squared)
        high, low = halves((distance + 1.0 / ln2) * jnp.exp2(-distance))
        both = values[s]
        wide = jnp.dot(both, high, preferred_element_type=f32)
        rest = jnp.dot(both[:16], low, preferred_element_type=f32)
        return c, (wide[:16] + wide[16:] + rest) * (times.astype(f32) * ln2)

    def group(size, first):
        def step(t, carry):
            for c, term in [tile(first + t * size + u) for u in range(size)]:
                total[c] += term
            return carry

        return step

    full = count // GROUP
    lax.fori_loop(0, full, group(GROUP, 0), 0)
    rest = count - full * GROUP
    lax.fori_loop(0, (rest + TAIL_GROUP - 1) // TAIL_GROUP, group(TAIL_GROUP, full * GROUP), 0)
    for place, c in enumerate(served):
        out[:, place * leaf_size : (place + 1) * leaf_size] = total[c]


def fill_table(table, blocks, start):
    count, _, lanes = blocks.shape
    half = lanes // 2
    for m in range(count):
        block = blocks[m]
        swapped = jnp.concatenate([block[:, half:], block[:, :half]], axis=1)
        table[start + 2 * m] = stacked_halves(block)
        table[start + 2 * m + 1] = stacked_halves(swapped)


def picked(table, rows, low_lanes):
    pieces = []
    for k in range(0, len(rows) - 1, 2):
        pieces.append(jnp.where(low_lanes, table[rows[k]], table[rows[k + 1] ^ 1]))
    if len(rows) % 2:
        pieces.append(table[rows[-1]][:, : low_lanes.shape[1] // 2])
    return jnp.concatenate(pieces, axis=1)


def coupled_pairs(picks, couples):
    slots, rank, _ = couples.shape
    result = jnp.zeros((16, rank), f32)
    low_lanes = lax.broadcasted_iota(jnp.int32, (rank, 2 * rank), 1) < rank
    for start in range(0, slots, 8):
        pairs = (min(slots - start, 8) + 1) // 2
        highs, lows = [], []
        for m in range(pairs):
            even = couples[start + m]
            if start + pairs + m < slots:
                odd = couples[start + pairs + m]
            else:
                odd = jnp.zeros_like(even)
            high, low = halves(jnp.concatenate([even, odd], axis=1))
            highs.append(high)
            lows.append(low)
        right = jnp.concatenate(
            [jnp.concatenate(highs, axis=0), jnp.concatenate(lows, axis=0)], axis=1
        )
        left = jnp.concatenate(
            [picks(start, pairs), picks(start + pairs, pairs)], axis=0
        )
        wide = jnp.dot(left, right, preferred_element_type=f32)
        first = wide[:16, : 2 * rank] + wide[16:32, : 2 * rank] + wide[:16, 2 * rank :]
        second = wide[32:48, : 2 * rank] + wide[48:, : 2 * rank] + wide[32:48, 2 * rank :]
        result = result + first[:, :rank] + second[:, rank:]
    return result


def coupled(both, couples):
    count, rank, _ = couples.shape
    high, low = halves(couples.reshape(count * rank, rank))
    wide = jnp.dot(both, jnp.concatenate([high, low], axis=1), preferred_element_type=f32)
    return wide[:16, :rank] + wide[16:, :rank] + wide[:16, rank:]


def inner_kernel(
    items, points_in, probes_in, out,
    points, probes, values, source, target, total, listed, held_semaphores, *, groups
):
    held = copies([(points_in, points), (probes_in, probes)], held_semaphores)
    near_field(
        items, points, probes, None, None, out, values, source, target, total, listed, held, groups
    )


def field_kernel(
    items, points_in, probes_in, left, right, before, middle, after, couples_in, out,
    far_out, points, probes, values, source, target, total, listed, held_semaphores, table, couples,
    semaphores, *, groups
):
    leaves, slots, rank, _ = couples.shape
    steps = leaves // FAR_STEP

    held = copies([(points_in, points), (probes_in, probes)], held_semaphores)

    def arriving(step):
        run = pl.ds(step * FAR_STEP, FAR_STEP)
        return pltpu.make_async_copy(couples_in.at[run], couples.at[run], semaphores.at[step])

    def start(step, carry):
        arriving(step).start()
        return carry

    lax.fori_loop(0, steps, start, 0)
    near_field(
        items, points, probes, left, right, out, values, source, target, total, listed, held, groups
    )

    empty = (2 * FAR_REACH + 1) * leaves
    low_lanes = lax.broadcasted_iota(jnp.int32, (32, 2 * rank), 1) < rank
    for b in range(3):
        for place, blocks in ((b, before), (3 + b, middle), (6 + b, after)):
            fill_table(table, blocks.at[b], place * leaves)
    table[empty] = jnp.zeros_like(table[empty])
    table[empty + 1] = jnp.zeros_like(table[empty])
    first_row = items.shape[0] - leaves

    def far_leaf(c):
        def picks(start, count):
            listed_here = range(start, start + count)
            rows = [items[first_row + c, k] if k < slots else empty for k in listed_here]
            return picked(table, rows, low_lanes)

        return coupled_pairs(picks, couples.at[c])

    def far_step(step, carry):
        arriving(step).wait()
        for u in range(0, FAR_STEP, 2):
            c = step * FAR_STEP + u
            far_out[c // 2] = jnp.concatenate([far_leaf(c), far_leaf(c + 1)], axis=1)
        return carry

    lax.fori_loop(0, steps, far_step, 0)


def down_kernel(
    box_list, column_list, boxes_in, couple_box_in, couple_column_in,
    transfer_box_in, far_in, inner_in, outer_in, transfer_in, basis_in, out,
    gathered, couple_box, couple_column, transfer_box, far_leaf, inner, outer, transfer_leaf, basis,
    semaphores,
):
    leaves, rank, leaf_size = basis.shape
    slots, column_slots = box_list.shape[1], column_list.shape[1]
    low_lanes = lax.broadcasted_iota(jnp.int32, (32, 2 * rank), 1) < rank
    arriving = copies(
        [
            (boxes_in, gathered),
            (couple_box_in, couple_box),
            (couple_column_in, couple_column),
            (transfer_box_in, transfer_box),
            (far_in, far_leaf),
            (inner_in, inner),
            (outer_in, outer),
        ]
        + parts(transfer_in, transfer_leaf)
        + parts(basis_in, basis),
        semaphores,
    )
    later = 7 + CHUNKS
    for copy in arriving[:4]:
        copy.wait()

    def box_row(entry):
        return jnp.where(entry >= 0, entry, 0)

    def pick(k):
        entry = box_list[0, k]
        return gathered[box_row(entry)] * jnp.where(entry >= 0, 1.0, 0.0)

    pieces = []
    for k in range(0, slots, 2):
        if k + 1 < slots:
            pieces.append(stacked_halves(jnp.where(low_lanes[:16], pick(k), exchanged(pick(k + 1)))))
        else:
            pieces.append(stacked_halves(pick(k))[:, :rank])
    far_box = coupled(jnp.concatenate(pieces, axis=1), couple_box[0])

    columns = []
    for k in range(column_slots):
        row = column_list[0, k]
        block = gathered[box_row(row * 4)]
        for j in range(1, 4):
            block = block + gathered[box_row(row * 4 + j)]
        columns.append(block * jnp.where(row >= 0, 1.0, 0.0))
    pieces = [
        stacked_halves(jnp.where(low_lanes[:16], exchanged(columns[k]), columns[k + 1]))
        for k in range(0, column_slots, 2)
    ]
    far_column = coupled(jnp.concatenate(pieces, axis=1), couple_column[0])
    down_box = far_box + product3(far_column, transfer_box[0], ((1,), (1,)))

    for copy in arriving[4:later]:
        copy.wait()
    high, low = halves(transfer_leaf[...].reshape(leaves * rank, rank))
    both = stacked_halves(down_box)
    wide = contract(both, high, ((1,), (1,)))
    from_box = wide[:16] + wide[16:] + contract(both[:16], low, ((1,), (1,)))

    lane = lax.broadcasted_iota(jnp.int32, (16, 4 * rank), 1)
    for m in range(leaves // 4):
        if m % (leaves // 4 // CHUNKS) == 0:
            arriving[later + m // (leaves // 4 // CHUNKS)].wait()
        down = from_box[:, m * 4 * rank : (m + 1) * 4 * rank]
        down = down + jnp.concatenate([far_leaf[2 * m], far_leaf[2 * m + 1]], axis=1)
        own_rows = [
            jnp.where((lane >= j * rank) & (lane < (j + 1) * rank), down, 0.0) for j in range(4)
        ]
        left = stacked_halves(jnp.concatenate(own_rows, axis=0))
        high, low = halves(basis[4 * m : 4 * m + 4].reshape(4 * rank, leaf_size))
        wide = jnp.dot(left, high, preferred_element_type=f32)
        rest = jnp.dot(left[:64], low, preferred_element_type=f32)
        result = wide[:64] + wide[64:] + rest
        for j in range(4):
            c = 4 * m + j
            held, place = outer, c if c < NEAR_REACH else c - leaves + 2 * NEAR_REACH
            if NEAR_REACH <= c < leaves - NEAR_REACH:
                held, place = inner, c - NEAR_REACH
            near_value = held[:, place * leaf_size : (place + 1) * leaf_size]
            lanes = slice(c * leaf_size, (c + 1) * leaf_size)
            out[:, lanes] = near_value + result[16 * j : 16 * j + 16]


def whole(count):
    return [pl.BlockSpec(memory_space=pltpu.VMEM)] * count


def scalars(count):
    return [pl.BlockSpec(memory_space=pltpu.SMEM)] * count


def params(mebibytes):
    return pltpu.CompilerParams(vmem_limit_bytes=mebibytes * 2**20)


def cost(flops):
    return pl.CostEstimate(flops=flops, bytes_accessed=2**20, transcendentals=0)


def shifted(array, axis, by):
    devices = lax.axis_size(axis)
    return lax.ppermute(array, axis, [(i, (i + by) % devices) for i in range(devices)])


def hbm(count):
    return [pl.BlockSpec(memory_space=pl.ANY)] * count


def like(array):
    return pltpu.VMEM(array.shape, array.dtype)


def copy_semaphores(count):
    return pltpu.SemaphoreType.DMA((count,))


def per_device(
    points,
    probes,
    basis,
    transfer_leaf,
    transfer_box,
    couple_leaf,
    couple_box,
    couple_column,
    near_list,
    far_list,
    box_list,
    column_list,
):
    leaves, leaf_size, rank = basis.shape
    probe_count = probes.shape[0]
    near_slots = near_list.T
    basis = basis.transpose(0, 2, 1)
    pairs = leaves // 2
    blocks = pairs + NEAR_REACH * leaf_size // 128 + 2
    devices = lax.axis_size(ring)

    edges = jax.ShapeDtypeStruct((blocks, probe_count, 2 * rank), f32)
    bundle_last, bundle_first, sent, items = pl.pallas_call(
        skeleton_kernel,
        out_shape=(
            edges,
            edges,
            jax.ShapeDtypeStruct((devices, probe_count, 2 * rank), f32),
            jax.ShapeDtypeStruct((near_slots.shape[0] + leaves, 128), jnp.int32),
        ),
        in_specs=whole(3) + hbm(3) + whole(1),
        out_specs=tuple(whole(4)),
        scratch_shapes=[like(probes), like(basis), like(transfer_leaf)]
        + [copy_semaphores(1 + 2 * CHUNKS)],
        compiler_params=params(60),
        name="skeletons",
    )(near_slots, far_list, points, probes, basis, transfer_leaf, transfer_box)

    left, right = shifted(bundle_last, ring, 1), shifted(bundle_first, ring, -1)

    window = leaves + 2 * NEAR_REACH
    near_scratch = [
        like(points),
        like(probes),
        pltpu.VMEM((window, 2 * probe_count, leaf_size), bf16),
        pltpu.VMEM((window, leaf_size, FEATURES), bf16),
        pltpu.VMEM((leaves, FEATURES, leaf_size), bf16),
        pltpu.VMEM((leaves, probe_count, leaf_size), f32),
        pltpu.SMEM((leaves * near_slots.shape[0] + 2 * GROUP,), jnp.int32),
        copy_semaphores(2),
    ]
    inner = ((NEAR_REACH, leaves - NEAR_REACH),)
    outer = ((0, NEAR_REACH), (leaves - NEAR_REACH, leaves))
    half = jax.ShapeDtypeStruct((probe_count, probes.shape[1] // 2), f32)
    near_inner = pl.pallas_call(
        functools.partial(inner_kernel, groups=inner),
        out_shape=half,
        in_specs=scalars(1) + hbm(2),
        out_specs=pl.BlockSpec(memory_space=pltpu.VMEM),
        scratch_shapes=near_scratch,
        compiler_params=params(60),
        cost_estimate=cost(10_000_000_000),
        name="near_inner",
    )(items, points, probes)

    sent, left, right, near_inner = lax.optimization_barrier((sent, left, right, near_inner))
    middle = jnp.stack([left[:pairs], bundle_last[:pairs], right[:pairs]])
    before, after = shifted(middle, ring, 3), shifted(middle, ring, -3)
    boxes = lax.all_to_all(sent, ring, 0, 0, tiled=True)

    near_outer, far_leaf = pl.pallas_call(
        functools.partial(field_kernel, groups=outer),
        out_shape=(half, jax.ShapeDtypeStruct((pairs, probe_count, 2 * rank), f32)),
        in_specs=scalars(1) + hbm(2) + whole(5) + hbm(1),
        out_specs=tuple(whole(2)),
        scratch_shapes=near_scratch
        + [
            pltpu.VMEM(((2 * FAR_REACH + 1) * leaves + 2, 2 * probe_count, 2 * rank), bf16),
            like(couple_leaf),
            copy_semaphores(leaves // FAR_STEP),
        ],
        compiler_params=params(60),
        cost_estimate=cost(20_000_000_000),
        name="near_far",
    )(items, points, probes, left, right, before, middle, after, couple_leaf)

    held = (boxes, couple_box, couple_column, transfer_box, far_leaf, near_inner, near_outer)
    held += (transfer_leaf, basis)
    return pl.pallas_call(
        down_kernel,
        out_shape=jax.ShapeDtypeStruct(probes.shape, f32),
        in_specs=scalars(2) + hbm(9),
        out_specs=pl.BlockSpec(memory_space=pltpu.VMEM),
        scratch_shapes=[like(array) for array in held] + [copy_semaphores(7 + 2 * CHUNKS)],
        compiler_params=params(60),
        name="down",
    )(box_list, column_list, *held)


def solution(mesh):
    placed = (
        P(None, ring),
        P(None, ring),
        P(ring, None, None),
        P(ring, None, None),
        P(ring, None, None),
        P(ring, None, None, None),
        P(ring, None, None, None),
        P("leaf", None, None, None),
        P(ring, None),
        P(ring, None),
        P(ring, None),
        P("leaf", None),
    )
    return jax.shard_map(
        per_device, mesh=mesh, in_specs=placed, out_specs=P(None, ring), check_vma=False
    )
```

```python
import functools
import math

import jax
import jax.numpy as jnp
from jax import lax
from jax.experimental import pallas as pl
from jax.experimental.pallas import tpu as pltpu
from jax.sharding import PartitionSpec as P

NEAR_REACH = 8
FAR_REACH = 4
FEATURES = 16
GROUP = 16
TAIL_GROUP = 4
FAR_STEP = 4
CHUNKS = 4

matern_rate = math.sqrt(3.0) / 0.1
coordinate_scale = matern_rate * math.log2(math.e)
ln2 = math.log(2.0)
tiny = 1e-20
f32 = jnp.float32
bf16 = jnp.bfloat16
vmem_bytes = 60 * 2**20
ring = ("leaf", "sub")


def halves(array):
    high = array.astype(bf16)
    return high, (array - high.astype(f32)).astype(bf16)


def stacked_halves(array):
    return jnp.concatenate(halves(array), axis=0)


def contract(left, right, dims):
    return lax.dot_general(left, right, (dims, ((), ())), preferred_element_type=f32)


def product3(left, right, dims=((1,), (0,))):
    rows = left.shape[0]
    high, low = halves(right)
    both = stacked_halves(left)
    wide = contract(both, high, dims)
    return wide[:rows] + wide[rows:] + contract(both[:rows], low, dims)


def copies(pairs, semaphores):
    made = [
        pltpu.make_async_copy(source, held, semaphores.at[i])
        for i, (source, held) in enumerate(pairs)
    ]
    for copy in made:
        copy.start()
    return made


def parts(source, held):
    length = source.shape[0] // CHUNKS
    runs = [pl.ds(i * length, length) for i in range(CHUNKS)]
    return [(source.at[run], held.at[run]) for run in runs]


def exchanged(block):
    half = block.shape[1] // 2
    return jnp.concatenate([block[:, half:], block[:, :half]], axis=1)


def skeleton_kernel(
    near, far, points, probes_in, basis_in, transfer_in, transfer_box, out, out_first, own, box_out, items,
    probes, basis, transfer_leaf, semaphores,
):
    leaves, rank, leaf_size = basis.shape
    arriving = copies(
        [(probes_in, probes)] + parts(basis_in, basis) + parts(transfer_in, transfer_leaf),
        semaphores,
    )
    slots = near.shape[0]
    pairs = leaves // 2
    low_lanes = lax.broadcasted_iota(jnp.int32, (16, 2 * rank), 1) < rank

    leaf = lax.broadcasted_iota(jnp.int32, (1, leaves), 1)
    rows = [near[k : k + 1, :] for k in range(slots)]
    for k in range(slots):
        new = rows[k] >= 0
        times = jnp.ones_like(leaf)
        for j in range(k):
            new = new & (rows[j] != rows[k])
        for j in range(k + 1, slots):
            times = times + jnp.where(rows[j] == rows[k], 1, 0)
        place = rows[k] - rows[0] + leaf + NEAR_REACH
        items[k : k + 1, 0:leaves] = jnp.where(new, leaf + place * 64 + times * 4096, 0)
    empty = (2 * FAR_REACH + 1) * leaves
    place = far[...] - (near[0:1, 0:1] - FAR_REACH * leaves)
    items[slots : slots + leaves, 0 : far.shape[1]] = jnp.where(far[...] >= 0, place, empty)

    arriving[0].wait()
    width = probes.shape[1]
    edge = NEAR_REACH * leaf_size
    for side, start in ((out, width - edge), (out_first, 0)):
        for j in range(edge // 128):
            lanes = slice(start + j * 128, start + (j + 1) * 128)
            side[pairs + j] = probes[:, lanes]
            side[pairs + edge // 128, j : j + 1, :] = points[0:1, lanes]
            side[pairs + 1 + edge // 128, j : j + 1, :] = points[1:2, lanes]

    def leaf_probes(c):
        return stacked_halves(probes[:, c * leaf_size : (c + 1) * leaf_size])

    def summed(wide):
        return wide[:16] + wide[16:] + exchanged(wide[:16])

    skeletons = []
    for m in range(pairs):
        if m % (pairs // CHUNKS) == 0:
            arriving[1 + m // (pairs // CHUNKS)].wait()
        left = jnp.concatenate([leaf_probes(2 * m), leaf_probes(2 * m + 1)], axis=0)
        right = jnp.concatenate([stacked_halves(basis[2 * m]), stacked_halves(basis[2 * m + 1])], axis=0)
        wide = contract(left, right, ((1,), (1,)))
        even, odd = summed(wide[:32, : 2 * rank]), summed(wide[32:, 2 * rank :])
        pair = jnp.where(low_lanes, even, exchanged(odd))
        out[m] = pair
        out_first[m] = pair
        own[m] = pair
        skeletons.append(pair)
    for copy in arriving[1 + CHUNKS :]:
        copy.wait()
    high, low = halves(transfer_leaf[...].reshape(leaves * rank, rank))
    wide = jnp.dot(
        stacked_halves(jnp.concatenate(skeletons, axis=1)),
        jnp.concatenate([high, low], axis=1),
        preferred_element_type=f32,
    )
    box = summed(wide)[:, :rank]
    block = jnp.concatenate([box, product3(box, transfer_box[0])], axis=1)
    box_out[...] = block


def near_field(
    items, points, probes, left, right, out, values, source, target, total, listed, arriving, groups
):
    leaves, _, leaf_size = target.shape
    slots = items.shape[0] - leaves
    pieces = leaf_size // 128
    pairs = leaves // 2
    edge_blocks = NEAR_REACH * pieces

    count = jnp.int32(0)
    served = [c for begin, end in groups for c in range(begin, end)]
    for c in served:
        for k in range(slots):
            item = items[k, c]
            listed[count] = item
            count = count + jnp.where(item != 0, 1, 0)
    for u in range(TAIL_GROUP):
        listed[count + u] = served[0] + (served[0] + NEAR_REACH) * 64

    for copy in arriving:
        copy.wait()
    ones = jnp.ones((3, leaf_size), f32)
    pad = jnp.zeros((2, leaf_size), f32)
    window = {c + j for c in served for j in range(2 * NEAR_REACH + 1)}
    for w in sorted(window):
        own = NEAR_REACH <= w < NEAR_REACH + leaves
        if own:
            lanes = slice((w - NEAR_REACH) * leaf_size, (w - NEAR_REACH + 1) * leaf_size)
            place, value = points[:, lanes], probes[:, lanes]
        else:
            side = left if w < NEAR_REACH else right
            first = (w if w < NEAR_REACH else w - NEAR_REACH - leaves) * pieces
            runs = range(first, first + pieces)
            value = jnp.concatenate([side[pairs + j] for j in runs], axis=1)
            place = jnp.concatenate(
                [
                    jnp.concatenate(
                        [side[pairs + edge_blocks + d, j : j + 1, :] for j in runs], axis=1
                    )
                    for d in range(2)
                ],
                axis=0,
            )
        values[w] = stacked_halves(value)
        scaled = (place - 0.5) * coordinate_scale
        first = scaled.astype(bf16).astype(f32)
        second = (scaled - first).astype(bf16).astype(f32)
        kept = first + second
        norm = kept[0:1] * kept[0:1] + kept[1:2] * kept[1:2]
        norm1 = norm.astype(bf16).astype(f32)
        rest = norm - norm1
        norm2 = rest.astype(bf16).astype(f32)
        norms = jnp.concatenate([norm1, norm2, rest - norm2], axis=0)
        rows = jnp.concatenate([first, second, first, second, norms, ones, pad], axis=0)
        source[w] = rows.T.astype(bf16)
        if w - NEAR_REACH in served:
            target[w - NEAR_REACH] = jnp.concatenate(
                [-2.0 * first, -2.0 * first, -2.0 * second, -2.0 * second, ones, norms, pad], axis=0
            ).astype(bf16)
    total[...] = jnp.zeros_like(total)

    def tile(i):
        item = listed[i]
        c, s, times = item & 63, (item >> 6) & 63, item >> 12
        squared = jnp.dot(source[s], target[c], preferred_element_type=f32)
        squared = jnp.maximum(squared, tiny)
        distance = squared * lax.rsqrt(squared)
        high, low = halves((distance + 1.0 / ln2) * jnp.exp2(-distance))
        both = values[s]
        wide = jnp.dot(both, high, preferred_element_type=f32)
        rest = jnp.dot(both[:16], low, preferred_element_type=f32)
        return c, (wide[:16] + wide[16:] + rest) * (times.astype(f32) * ln2)

    def group(size, first):
        def step(t, carry):
            for c, term in [tile(first + t * size + u) for u in range(size)]:
                total[c] += term
            return carry

        return step

    full = count // GROUP
    lax.fori_loop(0, full, group(GROUP, 0), 0)
    rest = count - full * GROUP
    lax.fori_loop(0, (rest + TAIL_GROUP - 1) // TAIL_GROUP, group(TAIL_GROUP, full * GROUP), 0)
    for place, c in enumerate(served):
        out[:, place * leaf_size : (place + 1) * leaf_size] = total[c]


def fill_table(table, blocks, start):
    count, _, lanes = blocks.shape
    half = lanes // 2
    for m in range(count):
        block = blocks[m]
        swapped = jnp.concatenate([block[:, half:], block[:, :half]], axis=1)
        table[start + 2 * m] = stacked_halves(block)
        table[start + 2 * m + 1] = stacked_halves(swapped)


def picked(table, rows, low_lanes):
    pieces = []
    for k in range(0, len(rows) - 1, 2):
        pieces.append(jnp.where(low_lanes, table[rows[k]], table[rows[k + 1] ^ 1]))
    if len(rows) % 2:
        pieces.append(table[rows[-1]][:, : low_lanes.shape[1] // 2])
    return jnp.concatenate(pieces, axis=1)


def coupled_pairs(picks, couples):
    slots, rank, _ = couples.shape
    result = jnp.zeros((16, rank), f32)
    low_lanes = lax.broadcasted_iota(jnp.int32, (rank, 2 * rank), 1) < rank
    for start in range(0, slots, 8):
        pairs = (min(slots - start, 8) + 1) // 2
        highs, lows = [], []
        for m in range(pairs):
            even = couples[start + m]
            if start + pairs + m < slots:
                odd = couples[start + pairs + m]
            else:
                odd = jnp.zeros_like(even)
            high, low = halves(jnp.concatenate([even, odd], axis=1))
            highs.append(high)
            lows.append(low)
        right = jnp.concatenate(
            [jnp.concatenate(highs, axis=0), jnp.concatenate(lows, axis=0)], axis=1
        )
        left = jnp.concatenate(
            [picks(start, pairs), picks(start + pairs, pairs)], axis=0
        )
        wide = jnp.dot(left, right, preferred_element_type=f32)
        first = wide[:16, : 2 * rank] + wide[16:32, : 2 * rank] + wide[:16, 2 * rank :]
        second = wide[32:48, : 2 * rank] + wide[48:, : 2 * rank] + wide[32:48, 2 * rank :]
        result = result + first[:, :rank] + second[:, rank:]
    return result


def coupled(both, couples):
    count, rank, _ = couples.shape
    high, low = halves(couples.reshape(count * rank, rank))
    wide = jnp.dot(both, jnp.concatenate([high, low], axis=1), preferred_element_type=f32)
    return wide[:16, :rank] + wide[16:, :rank] + wide[:16, rank:]


def inner_kernel(
    items, box, points_in, probes_in, out, sent_out,
    points, probes, values, source, target, total, listed, held_semaphores, sent, sent_semaphore,
    *, groups
):
    held = copies([(points_in, points), (probes_in, probes)], held_semaphores)
    for i in range(sent.shape[0]):
        sent[i] = box[...]
    (sending,) = copies([(sent, sent_out)], sent_semaphore)
    near_field(
        items, points, probes, None, None, out, values, source, target, total, listed, held, groups
    )
    sending.wait()


def field_kernel(
    items, points_in, probes_in, left, right, before_in, middle_in, after_in, couples_in, out,
    far_out, points, probes, values, source, target, total, listed, held_semaphores, table, couples,
    semaphores, before, middle, after, window_semaphores, *, groups
):
    leaves, slots, rank, _ = couples.shape
    steps = leaves // FAR_STEP

    held = copies([(points_in, points), (probes_in, probes)], held_semaphores)

    window = copies(
        [(before_in, before), (middle_in, middle), (after_in, after)], window_semaphores
    )

    def arriving(step):
        run = pl.ds(step * FAR_STEP, FAR_STEP)
        return pltpu.make_async_copy(couples_in.at[run], couples.at[run], semaphores.at[step])

    def start(step, carry):
        arriving(step).start()
        return carry

    lax.fori_loop(0, steps, start, 0)
    near_field(
        items, points, probes, left, right, out, values, source, target, total, listed, held, groups
    )

    empty = (2 * FAR_REACH + 1) * leaves
    low_lanes = lax.broadcasted_iota(jnp.int32, (32, 2 * rank), 1) < rank
    for copy in window:
        copy.wait()
    for b in range(3):
        for place, blocks in ((b, before), (3 + b, middle), (6 + b, after)):
            fill_table(table, blocks.at[b], place * leaves)
    table[empty] = jnp.zeros_like(table[empty])
    table[empty + 1] = jnp.zeros_like(table[empty])
    first_row = items.shape[0] - leaves

    def far_leaf(c):
        def picks(start, count):
            listed_here = range(start, start + count)
            rows = [items[first_row + c, k] if k < slots else empty for k in listed_here]
            return picked(table, rows, low_lanes)

        return coupled_pairs(picks, couples.at[c])

    def far_step(step, carry):
        arriving(step).wait()
        for u in range(0, FAR_STEP, 2):
            c = step * FAR_STEP + u
            far_out[c // 2] = jnp.concatenate([far_leaf(c), far_leaf(c + 1)], axis=1)
        return carry

    lax.fori_loop(0, steps, far_step, 0)


def down_kernel(
    box_list, column_list, boxes_in, couple_box_in, couple_column_in,
    transfer_box_in, far_in, inner_in, outer_in, transfer_in, basis_in, out,
    gathered, couple_box, couple_column, transfer_box, far_leaf, inner, outer, transfer_leaf, basis,
    semaphores,
):
    leaves, rank, leaf_size = basis.shape
    slots, column_slots = box_list.shape[1], column_list.shape[1]
    low_lanes = lax.broadcasted_iota(jnp.int32, (32, 2 * rank), 1) < rank
    arriving = copies(
        [
            (boxes_in, gathered),
            (couple_box_in, couple_box),
            (couple_column_in, couple_column),
            (transfer_box_in, transfer_box),
            (far_in, far_leaf),
            (inner_in, inner),
            (outer_in, outer),
        ]
        + parts(transfer_in, transfer_leaf)
        + parts(basis_in, basis),
        semaphores,
    )
    later = 7 + CHUNKS
    for copy in arriving[:4]:
        copy.wait()

    def box_row(entry):
        return jnp.where(entry >= 0, entry, 0)

    def pick(k):
        entry = box_list[0, k]
        return gathered[box_row(entry)] * jnp.where(entry >= 0, 1.0, 0.0)

    pieces = []
    for k in range(0, slots, 2):
        if k + 1 < slots:
            pieces.append(stacked_halves(jnp.where(low_lanes[:16], pick(k), exchanged(pick(k + 1)))))
        else:
            pieces.append(stacked_halves(pick(k))[:, :rank])
    far_box = coupled(jnp.concatenate(pieces, axis=1), couple_box[0])

    columns = []
    for k in range(column_slots):
        row = column_list[0, k]
        block = gathered[box_row(row * 4)]
        for j in range(1, 4):
            block = block + gathered[box_row(row * 4 + j)]
        columns.append(block * jnp.where(row >= 0, 1.0, 0.0))
    pieces = [
        stacked_halves(jnp.where(low_lanes[:16], exchanged(columns[k]), columns[k + 1]))
        for k in range(0, column_slots, 2)
    ]
    far_column = coupled(jnp.concatenate(pieces, axis=1), couple_column[0])
    down_box = far_box + product3(far_column, transfer_box[0], ((1,), (1,)))

    for copy in arriving[4:later]:
        copy.wait()
    high, low = halves(transfer_leaf[...].reshape(leaves * rank, rank))
    both = stacked_halves(down_box)
    wide = contract(both, high, ((1,), (1,)))
    from_box = wide[:16] + wide[16:] + contract(both[:16], low, ((1,), (1,)))

    lane = lax.broadcasted_iota(jnp.int32, (16, 4 * rank), 1)
    for m in range(leaves // 4):
        if m % (leaves // 4 // CHUNKS) == 0:
            arriving[later + m // (leaves // 4 // CHUNKS)].wait()
        down = from_box[:, m * 4 * rank : (m + 1) * 4 * rank]
        down = down + jnp.concatenate([far_leaf[2 * m], far_leaf[2 * m + 1]], axis=1)
        own_rows = [
            jnp.where((lane >= j * rank) & (lane < (j + 1) * rank), down, 0.0) for j in range(4)
        ]
        left = stacked_halves(jnp.concatenate(own_rows, axis=0))
        high, low = halves(basis[4 * m : 4 * m + 4].reshape(4 * rank, leaf_size))
        wide = jnp.dot(left, high, preferred_element_type=f32)
        rest = jnp.dot(left[:64], low, preferred_element_type=f32)
        result = wide[:64] + wide[64:] + rest
        for j in range(4):
            c = 4 * m + j
            held, place = outer, c if c < NEAR_REACH else c - leaves + 2 * NEAR_REACH
            if NEAR_REACH <= c < leaves - NEAR_REACH:
                held, place = inner, c - NEAR_REACH
            near_value = held[:, place * leaf_size : (place + 1) * leaf_size]
            lanes = slice(c * leaf_size, (c + 1) * leaf_size)
            out[:, lanes] = near_value + result[16 * j : 16 * j + 16]


def whole(count):
    return [pl.BlockSpec(memory_space=pltpu.VMEM)] * count


def scalars(count):
    return [pl.BlockSpec(memory_space=pltpu.SMEM)] * count


def params(mebibytes):
    return pltpu.CompilerParams(vmem_limit_bytes=mebibytes * 2**20)


def cost(flops):
    return pl.CostEstimate(flops=flops, bytes_accessed=2**20, transcendentals=0)


def shifted(array, axis, by):
    devices = lax.axis_size(axis)
    return lax.ppermute(array, axis, [(i, (i + by) % devices) for i in range(devices)])


def hbm(count):
    return [pl.BlockSpec(memory_space=pl.ANY)] * count


def like(array):
    return pltpu.VMEM(array.shape, array.dtype)


def copy_semaphores(count):
    return pltpu.SemaphoreType.DMA((count,))


def per_device(
    points,
    probes,
    basis,
    transfer_leaf,
    transfer_box,
    couple_leaf,
    couple_box,
    couple_column,
    near_list,
    far_list,
    box_list,
    column_list,
):
    leaves, leaf_size, rank = basis.shape
    probe_count = probes.shape[0]
    near_slots = near_list.T
    basis = basis.transpose(0, 2, 1)
    pairs = leaves // 2
    blocks = pairs + NEAR_REACH * leaf_size // 128 + 2

    edges = jax.ShapeDtypeStruct((blocks, probe_count, 2 * rank), f32)
    bundle_last, bundle_first, own, box, items = pl.pallas_call(
        skeleton_kernel,
        out_shape=(
            edges,
            edges,
            jax.ShapeDtypeStruct((pairs, probe_count, 2 * rank), f32),
            jax.ShapeDtypeStruct((probe_count, 2 * rank), f32),
            jax.ShapeDtypeStruct((near_slots.shape[0] + leaves, 128), jnp.int32),
        ),
        in_specs=whole(3) + hbm(3) + whole(1),
        out_specs=tuple(whole(5)),
        scratch_shapes=[like(probes), like(basis), like(transfer_leaf)]
        + [copy_semaphores(1 + 2 * CHUNKS)],
        compiler_params=params(60),
        name="skeletons",
    )(near_slots, far_list, points, probes, basis, transfer_leaf, transfer_box)

    left, right = shifted(bundle_last, ring, 1), shifted(bundle_first, ring, -1)

    window = leaves + 2 * NEAR_REACH
    near_scratch = [
        like(points),
        like(probes),
        pltpu.VMEM((window, 2 * probe_count, leaf_size), bf16),
        pltpu.VMEM((window, leaf_size, FEATURES), bf16),
        pltpu.VMEM((leaves, FEATURES, leaf_size), bf16),
        pltpu.VMEM((leaves, probe_count, leaf_size), f32),
        pltpu.SMEM((leaves * near_slots.shape[0] + 2 * GROUP,), jnp.int32),
        copy_semaphores(2),
    ]
    inner = ((NEAR_REACH, leaves - NEAR_REACH),)
    outer = ((0, NEAR_REACH), (leaves - NEAR_REACH, leaves))
    half = jax.ShapeDtypeStruct((probe_count, probes.shape[1] // 2), f32)
    copies_of_box = (lax.axis_size(ring), probe_count, 2 * rank)
    near_inner, sent = pl.pallas_call(
        functools.partial(inner_kernel, groups=inner),
        out_shape=(half, jax.ShapeDtypeStruct(copies_of_box, f32)),
        in_specs=scalars(1) + whole(1) + hbm(2),
        out_specs=tuple(whole(1) + hbm(1)),
        scratch_shapes=near_scratch + [pltpu.VMEM(copies_of_box, f32), copy_semaphores(1)],
        compiler_params=params(60),
        cost_estimate=cost(10_000_000_000),
        name="near_inner",
    )(items, box, points, probes)

    sent, left, right, own = lax.optimization_barrier((sent, left, right, own))
    middle = jnp.stack([left[:pairs], own, right[:pairs]])
    before, after = shifted(middle, ring, 3), shifted(middle, ring, -3)
    boxes = lax.all_to_all(sent, ring, 0, 0, tiled=True)

    near_outer, far_leaf = pl.pallas_call(
        functools.partial(field_kernel, groups=outer),
        out_shape=(half, jax.ShapeDtypeStruct((pairs, probe_count, 2 * rank), f32)),
        in_specs=scalars(1) + hbm(2) + whole(2) + hbm(4),
        out_specs=tuple(whole(2)),
        scratch_shapes=near_scratch
        + [
            pltpu.VMEM(((2 * FAR_REACH + 1) * leaves + 2, 2 * probe_count, 2 * rank), bf16),
            like(couple_leaf),
            copy_semaphores(leaves // FAR_STEP),
        ]
        + [like(middle)] * 3
        + [copy_semaphores(3)],
        compiler_params=params(60),
        cost_estimate=cost(20_000_000_000),
        name="near_far",
    )(items, points, probes, left, right, before, middle, after, couple_leaf)

    held = (boxes, couple_box, couple_column, transfer_box, far_leaf, near_inner, near_outer)
    held += (transfer_leaf, basis)
    return pl.pallas_call(
        down_kernel,
        out_shape=jax.ShapeDtypeStruct(probes.shape, f32),
        in_specs=scalars(2) + hbm(9),
        out_specs=pl.BlockSpec(memory_space=pltpu.VMEM),
        scratch_shapes=[like(array) for array in held] + [copy_semaphores(7 + 2 * CHUNKS)],
        compiler_params=params(60),
        name="down",
    )(box_list, column_list, *held)


def solution(mesh):
    placed = (
        P(None, ring),
        P(None, ring),
        P(ring, None, None),
        P(ring, None, None),
        P(ring, None, None),
        P(ring, None, None, None),
        P(ring, None, None, None),
        P("leaf", None, None, None),
        P(ring, None),
        P(ring, None),
        P(ring, None),
        P("leaf", None),
    )
    return jax.shard_map(
        per_device, mesh=mesh, in_specs=placed, out_specs=P(None, ring), check_vma=False
    )
```

```python
import functools
import math

import jax
import jax.numpy as jnp
from jax import lax
from jax.experimental import pallas as pl
from jax.experimental.pallas import tpu as pltpu
from jax.sharding import PartitionSpec as P

NEAR_REACH = 8
FAR_REACH = 4
FEATURES = 16
GROUP = 16
TAIL_GROUP = 4
FAR_STEP = 4
CHUNKS = 4

matern_rate = math.sqrt(3.0) / 0.1
coordinate_scale = matern_rate * math.log2(math.e)
ln2 = math.log(2.0)
tiny = 1e-20
f32 = jnp.float32
bf16 = jnp.bfloat16
vmem_bytes = 60 * 2**20
ring = ("leaf", "sub")


def halves(array):
    high = array.astype(bf16)
    return high, (array - high.astype(f32)).astype(bf16)


def stacked_halves(array):
    return jnp.concatenate(halves(array), axis=0)


def contract(left, right, dims):
    return lax.dot_general(left, right, (dims, ((), ())), preferred_element_type=f32)


def product3(left, right, dims=((1,), (0,))):
    rows = left.shape[0]
    high, low = halves(right)
    both = stacked_halves(left)
    wide = contract(both, high, dims)
    return wide[:rows] + wide[rows:] + contract(both[:rows], low, dims)


def copies(pairs, semaphores):
    made = [
        pltpu.make_async_copy(source, held, semaphores.at[i])
        for i, (source, held) in enumerate(pairs)
    ]
    for copy in made:
        copy.start()
    return made


def parts(source, held):
    length = source.shape[0] // CHUNKS
    runs = [pl.ds(i * length, length) for i in range(CHUNKS)]
    return [(source.at[run], held.at[run]) for run in runs]


def exchanged(block):
    half = block.shape[1] // 2
    return jnp.concatenate([block[:, half:], block[:, :half]], axis=1)


def skeleton_kernel(
    near, far, points, probes_in, basis_in, transfer_in, transfer_box, out, out_first, own, box_out, items,
    probes, basis, transfer_leaf, semaphores, later_semaphore,
):
    leaves, rank, leaf_size = basis.shape
    arriving = copies([(probes_in, probes)] + parts(basis_in, basis), semaphores)
    slots = near.shape[0]
    pairs = leaves // 2
    low_lanes = lax.broadcasted_iota(jnp.int32, (16, 2 * rank), 1) < rank

    leaf = lax.broadcasted_iota(jnp.int32, (1, leaves), 1)
    rows = [near[k : k + 1, :] for k in range(slots)]
    for k in range(slots):
        new = rows[k] >= 0
        times = jnp.ones_like(leaf)
        for j in range(k):
            new = new & (rows[j] != rows[k])
        for j in range(k + 1, slots):
            times = times + jnp.where(rows[j] == rows[k], 1, 0)
        place = rows[k] - rows[0] + leaf + NEAR_REACH
        items[k : k + 1, 0:leaves] = jnp.where(new, leaf + place * 64 + times * 4096, 0)
    empty = (2 * FAR_REACH + 1) * leaves
    place = far[...] - (near[0:1, 0:1] - FAR_REACH * leaves)
    items[slots : slots + leaves, 0 : far.shape[1]] = jnp.where(far[...] >= 0, place, empty)

    arriving[0].wait()
    width = probes.shape[1]
    edge = NEAR_REACH * leaf_size
    for side, start in ((out, width - edge), (out_first, 0)):
        for j in range(edge // 128):
            lanes = slice(start + j * 128, start + (j + 1) * 128)
            side[pairs + j] = probes[:, lanes]
            side[pairs + edge // 128, j : j + 1, :] = points[0:1, lanes]
            side[pairs + 1 + edge // 128, j : j + 1, :] = points[1:2, lanes]

    def leaf_probes(c):
        return stacked_halves(probes[:, c * leaf_size : (c + 1) * leaf_size])

    def summed(wide):
        return wide[:16] + wide[16:] + exchanged(wide[:16])

    skeletons = []
    for m in range(pairs):
        if m % (pairs // CHUNKS) == 0:
            arriving[1 + m // (pairs // CHUNKS)].wait()
        if m == 0:
            later = copies([(transfer_in, transfer_leaf)], later_semaphore)
        left = jnp.concatenate([leaf_probes(2 * m), leaf_probes(2 * m + 1)], axis=0)
        right = jnp.concatenate([stacked_halves(basis[2 * m]), stacked_halves(basis[2 * m + 1])], axis=0)
        wide = contract(left, right, ((1,), (1,)))
        even, odd = summed(wide[:32, : 2 * rank]), summed(wide[32:, 2 * rank :])
        pair = jnp.where(low_lanes, even, exchanged(odd))
        out[m] = pair
        out_first[m] = pair
        own[m] = pair
        skeletons.append(pair)
    later[0].wait()
    high, low = halves(transfer_leaf[...].reshape(leaves * rank, rank))
    wide = jnp.dot(
        stacked_halves(jnp.concatenate(skeletons, axis=1)),
        jnp.concatenate([high, low], axis=1),
        preferred_element_type=f32,
    )
    box = summed(wide)[:, :rank]
    block = jnp.concatenate([box, product3(box, transfer_box[0])], axis=1)
    box_out[...] = block


def near_field(
    items, points, probes, left, right, out, values, source, target, total, listed, arriving, groups
):
    leaves, _, leaf_size = target.shape
    slots = items.shape[0] - leaves
    pieces = leaf_size // 128
    pairs = leaves // 2
    edge_blocks = NEAR_REACH * pieces

    count = jnp.int32(0)
    served = [c for begin, end in groups for c in range(begin, end)]
    for c in served:
        for k in range(slots):
            item = items[k, c]
            listed[count] = item
            count = count + jnp.where(item != 0, 1, 0)
    for u in range(TAIL_GROUP):
        listed[count + u] = served[0] + (served[0] + NEAR_REACH) * 64

    for copy in arriving:
        copy.wait()
    ones = jnp.ones((3, leaf_size), f32)
    pad = jnp.zeros((2, leaf_size), f32)
    window = {c + j for c in served for j in range(2 * NEAR_REACH + 1)}
    for w in sorted(window):
        own = NEAR_REACH <= w < NEAR_REACH + leaves
        if own:
            lanes = slice((w - NEAR_REACH) * leaf_size, (w - NEAR_REACH + 1) * leaf_size)
            place, value = points[:, lanes], probes[:, lanes]
        else:
            side = left if w < NEAR_REACH else right
            first = (w if w < NEAR_REACH else w - NEAR_REACH - leaves) * pieces
            runs = range(first, first + pieces)
            value = jnp.concatenate([side[pairs + j] for j in runs], axis=1)
            place = jnp.concatenate(
                [
                    jnp.concatenate(
                        [side[pairs + edge_blocks + d, j : j + 1, :] for j in runs], axis=1
                    )
                    for d in range(2)
                ],
                axis=0,
            )
        values[w] = stacked_halves(value)
        scaled = (place - 0.5) * coordinate_scale
        first = scaled.astype(bf16).astype(f32)
        second = (scaled - first).astype(bf16).astype(f32)
        kept = first + second
        norm = kept[0:1] * kept[0:1] + kept[1:2] * kept[1:2]
        norm1 = norm.astype(bf16).astype(f32)
        rest = norm - norm1
        norm2 = rest.astype(bf16).astype(f32)
        norms = jnp.concatenate([norm1, norm2, rest - norm2], axis=0)
        rows = jnp.concatenate([first, second, first, second, norms, ones, pad], axis=0)
        source[w] = rows.T.astype(bf16)
        if w - NEAR_REACH in served:
            target[w - NEAR_REACH] = jnp.concatenate(
                [-2.0 * first, -2.0 * first, -2.0 * second, -2.0 * second, ones, norms, pad], axis=0
            ).astype(bf16)
    total[...] = jnp.zeros_like(total)

    def tile(i):
        item = listed[i]
        c, s, times = item & 63, (item >> 6) & 63, item >> 12
        squared = jnp.dot(source[s], target[c], preferred_element_type=f32)
        squared = jnp.maximum(squared, tiny)
        distance = squared * lax.rsqrt(squared)
        high, low = halves((distance + 1.0 / ln2) * jnp.exp2(-distance))
        both = values[s]
        wide = jnp.dot(both, high, preferred_element_type=f32)
        rest = jnp.dot(both[:16], low, preferred_element_type=f32)
        return c, (wide[:16] + wide[16:] + rest) * (times.astype(f32) * ln2)

    def group(size, first):
        def step(t, carry):
            for c, term in [tile(first + t * size + u) for u in range(size)]:
                total[c] += term
            return carry

        return step

    full = count // GROUP
    lax.fori_loop(0, full, group(GROUP, 0), 0)
    rest = count - full * GROUP
    lax.fori_loop(0, (rest + TAIL_GROUP - 1) // TAIL_GROUP, group(TAIL_GROUP, full * GROUP), 0)
    for place, c in enumerate(served):
        out[:, place * leaf_size : (place + 1) * leaf_size] = total[c]


def fill_table(table, blocks, start):
    count, _, lanes = blocks.shape
    half = lanes // 2
    for m in range(count):
        block = blocks[m]
        swapped = jnp.concatenate([block[:, half:], block[:, :half]], axis=1)
        table[start + 2 * m] = stacked_halves(block)
        table[start + 2 * m + 1] = stacked_halves(swapped)


def picked(table, rows, low_lanes):
    pieces = []
    for k in range(0, len(rows) - 1, 2):
        pieces.append(jnp.where(low_lanes, table[rows[k]], table[rows[k + 1] ^ 1]))
    if len(rows) % 2:
        pieces.append(table[rows[-1]][:, : low_lanes.shape[1] // 2])
    return jnp.concatenate(pieces, axis=1)


def coupled_pairs(picks, couples):
    slots, rank, _ = couples.shape
    result = jnp.zeros((16, rank), f32)
    low_lanes = lax.broadcasted_iota(jnp.int32, (rank, 2 * rank), 1) < rank
    for start in range(0, slots, 8):
        pairs = (min(slots - start, 8) + 1) // 2
        highs, lows = [], []
        for m in range(pairs):
            even = couples[start + m]
            if start + pairs + m < slots:
                odd = couples[start + pairs + m]
            else:
                odd = jnp.zeros_like(even)
            high, low = halves(jnp.concatenate([even, odd], axis=1))
            highs.append(high)
            lows.append(low)
        right = jnp.concatenate(
            [jnp.concatenate(highs, axis=0), jnp.concatenate(lows, axis=0)], axis=1
        )
        left = jnp.concatenate(
            [picks(start, pairs), picks(start + pairs, pairs)], axis=0
        )
        wide = jnp.dot(left, right, preferred_element_type=f32)
        first = wide[:16, : 2 * rank] + wide[16:32, : 2 * rank] + wide[:16, 2 * rank :]
        second = wide[32:48, : 2 * rank] + wide[48:, : 2 * rank] + wide[32:48, 2 * rank :]
        result = result + first[:, :rank] + second[:, rank:]
    return result


def coupled(both, couples):
    count, rank, _ = couples.shape
    high, low = halves(couples.reshape(count * rank, rank))
    wide = jnp.dot(both, jnp.concatenate([high, low], axis=1), preferred_element_type=f32)
    return wide[:16, :rank] + wide[16:, :rank] + wide[:16, rank:]


def inner_kernel(
    items, box, points_in, probes_in, out, sent_out,
    points, probes, values, source, target, total, listed, held_semaphores, sent, sent_semaphore,
    *, groups
):
    held = copies([(points_in, points), (probes_in, probes)], held_semaphores)
    for i in range(sent.shape[0]):
        sent[i] = box[...]
    (sending,) = copies([(sent, sent_out)], sent_semaphore)
    near_field(
        items, points, probes, None, None, out, values, source, target, total, listed, held, groups
    )
    sending.wait()


def field_kernel(
    items, points_in, probes_in, left, right, before_in, middle_in, after_in, couples_in, out,
    far_out, points, probes, values, source, target, total, listed, held_semaphores, table, couples,
    semaphores, before, middle, after, window_semaphores, *, groups
):
    leaves, slots, rank, _ = couples.shape
    steps = leaves // FAR_STEP

    held = copies([(points_in, points), (probes_in, probes)], held_semaphores)

    window = copies(
        [(before_in, before), (middle_in, middle), (after_in, after)], window_semaphores
    )

    def arriving(step):
        run = pl.ds(step * FAR_STEP, FAR_STEP)
        return pltpu.make_async_copy(couples_in.at[run], couples.at[run], semaphores.at[step])

    def start(step, carry):
        arriving(step).start()
        return carry

    lax.fori_loop(0, steps, start, 0)
    near_field(
        items, points, probes, left, right, out, values, source, target, total, listed, held, groups
    )

    empty = (2 * FAR_REACH + 1) * leaves
    low_lanes = lax.broadcasted_iota(jnp.int32, (32, 2 * rank), 1) < rank
    for copy in window:
        copy.wait()
    for b in range(3):
        for place, blocks in ((b, before), (3 + b, middle), (6 + b, after)):
            fill_table(table, blocks.at[b], place * leaves)
    table[empty] = jnp.zeros_like(table[empty])
    table[empty + 1] = jnp.zeros_like(table[empty])
    first_row = items.shape[0] - leaves

    def far_leaf(c):
        def picks(start, count):
            listed_here = range(start, start + count)
            rows = [items[first_row + c, k] if k < slots else empty for k in listed_here]
            return picked(table, rows, low_lanes)

        return coupled_pairs(picks, couples.at[c])

    def far_step(step, carry):
        arriving(step).wait()
        for u in range(0, FAR_STEP, 2):
            c = step * FAR_STEP + u
            far_out[c // 2] = jnp.concatenate([far_leaf(c), far_leaf(c + 1)], axis=1)
        return carry

    lax.fori_loop(0, steps, far_step, 0)


def down_kernel(
    box_list, column_list, gathered, couple_box_in, couple_column_in,
    transfer_box_in, far_in, inner_in, outer_in, transfer_in, basis_in, out,
    couple_box, couple_column, transfer_box, far_leaf, inner, outer, transfer_leaf, basis,
    semaphores,
):
    leaves, rank, leaf_size = basis.shape
    slots, column_slots = box_list.shape[1], column_list.shape[1]
    low_lanes = lax.broadcasted_iota(jnp.int32, (32, 2 * rank), 1) < rank
    arriving = copies(
        [
            (couple_box_in, couple_box),
            (couple_column_in, couple_column),
            (transfer_box_in, transfer_box),
            (far_in, far_leaf),
            (inner_in, inner),
            (outer_in, outer),
        ]
        + parts(transfer_in, transfer_leaf)
        + parts(basis_in, basis),
        semaphores,
    )
    later = 6 + CHUNKS
    for copy in arriving[:3]:
        copy.wait()

    def box_row(entry):
        return jnp.where(entry >= 0, entry, 0)

    def pick(k):
        entry = box_list[0, k]
        return gathered[box_row(entry)] * jnp.where(entry >= 0, 1.0, 0.0)

    pieces = []
    for k in range(0, slots, 2):
        if k + 1 < slots:
            pieces.append(stacked_halves(jnp.where(low_lanes[:16], pick(k), exchanged(pick(k + 1)))))
        else:
            pieces.append(stacked_halves(pick(k))[:, :rank])
    far_box = coupled(jnp.concatenate(pieces, axis=1), couple_box[0])

    columns = []
    for k in range(column_slots):
        row = column_list[0, k]
        block = gathered[box_row(row * 4)]
        for j in range(1, 4):
            block = block + gathered[box_row(row * 4 + j)]
        columns.append(block * jnp.where(row >= 0, 1.0, 0.0))
    pieces = [
        stacked_halves(jnp.where(low_lanes[:16], exchanged(columns[k]), columns[k + 1]))
        for k in range(0, column_slots, 2)
    ]
    far_column = coupled(jnp.concatenate(pieces, axis=1), couple_column[0])
    down_box = far_box + product3(far_column, transfer_box[0], ((1,), (1,)))

    for copy in arriving[3:later]:
        copy.wait()
    high, low = halves(transfer_leaf[...].reshape(leaves * rank, rank))
    both = stacked_halves(down_box)
    wide = contract(both, high, ((1,), (1,)))
    from_box = wide[:16] + wide[16:] + contract(both[:16], low, ((1,), (1,)))

    lane = lax.broadcasted_iota(jnp.int32, (16, 4 * rank), 1)
    for m in range(leaves // 4):
        if m % (leaves // 4 // CHUNKS) == 0:
            arriving[later + m // (leaves // 4 // CHUNKS)].wait()
        down = from_box[:, m * 4 * rank : (m + 1) * 4 * rank]
        down = down + jnp.concatenate([far_leaf[2 * m], far_leaf[2 * m + 1]], axis=1)
        own_rows = [
            jnp.where((lane >= j * rank) & (lane < (j + 1) * rank), down, 0.0) for j in range(4)
        ]
        left = stacked_halves(jnp.concatenate(own_rows, axis=0))
        high, low = halves(basis[4 * m : 4 * m + 4].reshape(4 * rank, leaf_size))
        wide = jnp.dot(left, high, preferred_element_type=f32)
        rest = jnp.dot(left[:64], low, preferred_element_type=f32)
        result = wide[:64] + wide[64:] + rest
        for j in range(4):
            c = 4 * m + j
            held, place = outer, c if c < NEAR_REACH else c - leaves + 2 * NEAR_REACH
            if NEAR_REACH <= c < leaves - NEAR_REACH:
                held, place = inner, c - NEAR_REACH
            near_value = held[:, place * leaf_size : (place + 1) * leaf_size]
            lanes = slice(c * leaf_size, (c + 1) * leaf_size)
            out[:, lanes] = near_value + result[16 * j : 16 * j + 16]


def whole(count):
    return [pl.BlockSpec(memory_space=pltpu.VMEM)] * count


def scalars(count):
    return [pl.BlockSpec(memory_space=pltpu.SMEM)] * count


def params(mebibytes):
    return pltpu.CompilerParams(vmem_limit_bytes=mebibytes * 2**20)


def cost(flops):
    return pl.CostEstimate(flops=flops, bytes_accessed=2**20, transcendentals=0)


def shifted(array, axis, by):
    devices = lax.axis_size(axis)
    return lax.ppermute(array, axis, [(i, (i + by) % devices) for i in range(devices)])


def hbm(count):
    return [pl.BlockSpec(memory_space=pl.ANY)] * count


def like(array):
    return pltpu.VMEM(array.shape, array.dtype)


def copy_semaphores(count):
    return pltpu.SemaphoreType.DMA((count,))


def per_device(
    points,
    probes,
    basis,
    transfer_leaf,
    transfer_box,
    couple_leaf,
    couple_box,
    couple_column,
    near_list,
    far_list,
    box_list,
    column_list,
):
    leaves, leaf_size, rank = basis.shape
    probe_count = probes.shape[0]
    near_slots = near_list.T
    basis = basis.transpose(0, 2, 1)
    pairs = leaves // 2
    blocks = pairs + NEAR_REACH * leaf_size // 128 + 2

    edges = jax.ShapeDtypeStruct((blocks, probe_count, 2 * rank), f32)
    bundle_last, bundle_first, own, box, items = pl.pallas_call(
        skeleton_kernel,
        out_shape=(
            edges,
            edges,
            jax.ShapeDtypeStruct((pairs, probe_count, 2 * rank), f32),
            jax.ShapeDtypeStruct((probe_count, 2 * rank), f32),
            jax.ShapeDtypeStruct((near_slots.shape[0] + leaves, 128), jnp.int32),
        ),
        in_specs=whole(3) + hbm(3) + whole(1),
        out_specs=tuple(whole(5)),
        scratch_shapes=[like(probes), like(basis), like(transfer_leaf)]
        + [copy_semaphores(1 + CHUNKS), copy_semaphores(1)],
        compiler_params=params(60),
        name="skeletons",
    )(near_slots, far_list, points, probes, basis, transfer_leaf, transfer_box)

    left, right = shifted(bundle_last, ring, 1), shifted(bundle_first, ring, -1)

    window = leaves + 2 * NEAR_REACH
    near_scratch = [
        like(points),
        like(probes),
        pltpu.VMEM((window, 2 * probe_count, leaf_size), bf16),
        pltpu.VMEM((window, leaf_size, FEATURES), bf16),
        pltpu.VMEM((leaves, FEATURES, leaf_size), bf16),
        pltpu.VMEM((leaves, probe_count, leaf_size), f32),
        pltpu.SMEM((leaves * near_slots.shape[0] + 2 * GROUP,), jnp.int32),
        copy_semaphores(2),
    ]
    inner = ((NEAR_REACH, leaves - NEAR_REACH),)
    outer = ((0, NEAR_REACH), (leaves - NEAR_REACH, leaves))
    half = jax.ShapeDtypeStruct((probe_count, probes.shape[1] // 2), f32)
    copies_of_box = (lax.axis_size(ring), probe_count, 2 * rank)
    near_inner, sent = pl.pallas_call(
        functools.partial(inner_kernel, groups=inner),
        out_shape=(half, jax.ShapeDtypeStruct(copies_of_box, f32)),
        in_specs=scalars(1) + whole(1) + hbm(2),
        out_specs=tuple(whole(1) + hbm(1)),
        scratch_shapes=near_scratch + [pltpu.VMEM(copies_of_box, f32), copy_semaphores(1)],
        compiler_params=params(60),
        cost_estimate=cost(10_000_000_000),
        name="near_inner",
    )(items, box, points, probes)

    sent, left, right, own = lax.optimization_barrier((sent, left, right, own))
    middle = jnp.stack([left[:pairs], own, right[:pairs]])
    before, after = shifted(middle, ring, 3), shifted(middle, ring, -3)
    boxes = lax.all_to_all(sent, ring, 0, 0, tiled=True)

    near_outer, far_leaf = pl.pallas_call(
        functools.partial(field_kernel, groups=outer),
        out_shape=(half, jax.ShapeDtypeStruct((pairs, probe_count, 2 * rank), f32)),
        in_specs=scalars(1) + hbm(2) + whole(2) + hbm(4),
        out_specs=tuple(whole(2)),
        scratch_shapes=near_scratch
        + [
            pltpu.VMEM(((2 * FAR_REACH + 1) * leaves + 2, 2 * probe_count, 2 * rank), bf16),
            like(couple_leaf),
            copy_semaphores(leaves // FAR_STEP),
        ]
        + [like(middle)] * 3
        + [copy_semaphores(3)],
        compiler_params=params(60),
        cost_estimate=cost(20_000_000_000),
        name="near_far",
    )(items, points, probes, left, right, before, middle, after, couple_leaf)

    held = (couple_box, couple_column, transfer_box, far_leaf, near_inner, near_outer)
    held += (transfer_leaf, basis)
    return pl.pallas_call(
        down_kernel,
        out_shape=jax.ShapeDtypeStruct(probes.shape, f32),
        in_specs=scalars(2) + whole(1) + hbm(8),
        out_specs=pl.BlockSpec(memory_space=pltpu.VMEM),
        scratch_shapes=[like(array) for array in held] + [copy_semaphores(6 + 2 * CHUNKS)],
        compiler_params=params(60),
        name="down",
    )(box_list, column_list, boxes, *held)


def solution(mesh):
    placed = (
        P(None, ring),
        P(None, ring),
        P(ring, None, None),
        P(ring, None, None),
        P(ring, None, None),
        P(ring, None, None, None),
        P(ring, None, None, None),
        P("leaf", None, None, None),
        P(ring, None),
        P(ring, None),
        P(ring, None),
        P("leaf", None),
    )
    return jax.shard_map(
        per_device, mesh=mesh, in_specs=placed, out_specs=P(None, ring), check_vma=False
    )
```

```python
import functools
import math

import jax
import jax.numpy as jnp
from jax import lax
from jax.experimental import pallas as pl
from jax.experimental.pallas import tpu as pltpu
from jax.sharding import PartitionSpec as P

NEAR_REACH = 8
FAR_REACH = 4
FEATURES = 16
GROUP = 16
TAIL_GROUP = 4
FAR_STEP = 4
CHUNKS = 4

matern_rate = math.sqrt(3.0) / 0.1
coordinate_scale = matern_rate * math.log2(math.e)
ln2 = math.log(2.0)
tiny = 1e-20
f32 = jnp.float32
bf16 = jnp.bfloat16
vmem_bytes = 60 * 2**20
ring = ("leaf", "sub")


def halves(array):
    high = array.astype(bf16)
    return high, (array - high.astype(f32)).astype(bf16)


def stacked_halves(array):
    return jnp.concatenate(halves(array), axis=0)


def contract(left, right, dims):
    return lax.dot_general(left, right, (dims, ((), ())), preferred_element_type=f32)


def product3(left, right, dims=((1,), (0,))):
    rows = left.shape[0]
    high, low = halves(right)
    both = stacked_halves(left)
    wide = contract(both, high, dims)
    return wide[:rows] + wide[rows:] + contract(both[:rows], low, dims)


def copies(pairs, semaphores):
    made = [
        pltpu.make_async_copy(source, held, semaphores.at[i])
        for i, (source, held) in enumerate(pairs)
    ]
    for copy in made:
        copy.start()
    return made


def parts(source, held):
    length = source.shape[0] // CHUNKS
    runs = [pl.ds(i * length, length) for i in range(CHUNKS)]
    return [(source.at[run], held.at[run]) for run in runs]


def exchanged(block):
    half = block.shape[1] // 2
    return jnp.concatenate([block[:, half:], block[:, :half]], axis=1)


def skeleton_kernel(
    near, far, points, probes_in, basis_in, transfer_in, transfer_box, out, out_first, own, box_out, items,
    probes, basis, transfer_leaf, semaphores, later_semaphore,
):
    leaves, rank, leaf_size = basis.shape
    arriving = copies([(probes_in, probes)] + parts(basis_in, basis), semaphores)
    slots = near.shape[0]
    pairs = leaves // 2
    low_lanes = lax.broadcasted_iota(jnp.int32, (16, 2 * rank), 1) < rank

    leaf = lax.broadcasted_iota(jnp.int32, (1, leaves), 1)
    rows = [near[k : k + 1, :] for k in range(slots)]
    for k in range(slots):
        new = rows[k] >= 0
        times = jnp.ones_like(leaf)
        for j in range(k):
            new = new & (rows[j] != rows[k])
        for j in range(k + 1, slots):
            times = times + jnp.where(rows[j] == rows[k], 1, 0)
        place = rows[k] - rows[0] + leaf + NEAR_REACH
        items[k : k + 1, 0:leaves] = jnp.where(new, leaf + place * 64 + times * 4096, 0)
    empty = (2 * FAR_REACH + 1) * leaves
    place = far[...] - (near[0:1, 0:1] - FAR_REACH * leaves)
    items[slots : slots + leaves, 0 : far.shape[1]] = jnp.where(far[...] >= 0, place, empty)

    arriving[0].wait()
    width = probes.shape[1]
    edge = NEAR_REACH * leaf_size
    for side, start in ((out, width - edge), (out_first, 0)):
        for j in range(edge // 128):
            lanes = slice(start + j * 128, start + (j + 1) * 128)
            side[pairs + j] = probes[:, lanes]
            side[pairs + edge // 128, j : j + 1, :] = points[0:1, lanes]
            side[pairs + 1 + edge // 128, j : j + 1, :] = points[1:2, lanes]

    def leaf_probes(c):
        return stacked_halves(probes[:, c * leaf_size : (c + 1) * leaf_size])

    def summed(wide):
        return wide[:16] + wide[16:] + exchanged(wide[:16])

    skeletons = []
    for m in range(pairs):
        if m % (pairs // CHUNKS) == 0:
            arriving[1 + m // (pairs // CHUNKS)].wait()
        if m == 0:
            later = copies([(transfer_in, transfer_leaf)], later_semaphore)
        left = jnp.concatenate([leaf_probes(2 * m), leaf_probes(2 * m + 1)], axis=0)
        right = jnp.concatenate([stacked_halves(basis[2 * m]), stacked_halves(basis[2 * m + 1])], axis=0)
        wide = contract(left, right, ((1,), (1,)))
        even, odd = summed(wide[:32, : 2 * rank]), summed(wide[32:, 2 * rank :])
        pair = jnp.where(low_lanes, even, exchanged(odd))
        out[m] = pair
        out_first[m] = pair
        own[m] = pair
        skeletons.append(pair)
    later[0].wait()
    high, low = halves(transfer_leaf[...].reshape(leaves * rank, rank))
    wide = jnp.dot(
        stacked_halves(jnp.concatenate(skeletons, axis=1)),
        jnp.concatenate([high, low], axis=1),
        preferred_element_type=f32,
    )
    box = summed(wide)[:, :rank]
    block = jnp.concatenate([box, product3(box, transfer_box[0])], axis=1)
    box_out[...] = block


def near_field(
    items, points, probes, left, right, out, values, source, target, total, listed, arriving, groups
):
    leaves, _, leaf_size = target.shape
    slots = items.shape[0] - leaves
    pieces = leaf_size // 128
    pairs = leaves // 2
    edge_blocks = NEAR_REACH * pieces

    count = jnp.int32(0)
    served = [c for begin, end in groups for c in range(begin, end)]
    for c in served:
        for k in range(slots):
            item = items[k, c]
            listed[count] = item
            count = count + jnp.where(item != 0, 1, 0)
    for u in range(TAIL_GROUP):
        listed[count + u] = served[0] + (served[0] + NEAR_REACH) * 64

    for copy in arriving:
        copy.wait()
    ones = jnp.ones((3, leaf_size), f32)
    pad = jnp.zeros((2, leaf_size), f32)
    window = {c + j for c in served for j in range(2 * NEAR_REACH + 1)}
    for w in sorted(window):
        own = NEAR_REACH <= w < NEAR_REACH + leaves
        if own:
            lanes = slice((w - NEAR_REACH) * leaf_size, (w - NEAR_REACH + 1) * leaf_size)
            place, value = points[:, lanes], probes[:, lanes]
        else:
            side = left if w < NEAR_REACH else right
            first = (w if w < NEAR_REACH else w - NEAR_REACH - leaves) * pieces
            runs = range(first, first + pieces)
            value = jnp.concatenate([side[pairs + j] for j in runs], axis=1)
            place = jnp.concatenate(
                [
                    jnp.concatenate(
                        [side[pairs + edge_blocks + d, j : j + 1, :] for j in runs], axis=1
                    )
                    for d in range(2)
                ],
                axis=0,
            )
        values[w] = stacked_halves(value)
        scaled = (place - 0.5) * coordinate_scale
        first = scaled.astype(bf16).astype(f32)
        second = (scaled - first).astype(bf16).astype(f32)
        kept = first + second
        norm = kept[0:1] * kept[0:1] + kept[1:2] * kept[1:2]
        norm1 = norm.astype(bf16).astype(f32)
        rest = norm - norm1
        norm2 = rest.astype(bf16).astype(f32)
        norms = jnp.concatenate([norm1, norm2, rest - norm2], axis=0)
        rows = jnp.concatenate([first, second, first, second, norms, ones, pad], axis=0)
        source[w] = rows.T.astype(bf16)
        if w - NEAR_REACH in served:
            target[w - NEAR_REACH] = jnp.concatenate(
                [-2.0 * first, -2.0 * first, -2.0 * second, -2.0 * second, ones, norms, pad], axis=0
            ).astype(bf16)
    total[...] = jnp.zeros_like(total)

    def tile(i):
        item = listed[i]
        c, s, times = item & 63, (item >> 6) & 63, item >> 12
        squared = jnp.dot(source[s], target[c], preferred_element_type=f32)
        squared = jnp.maximum(squared, tiny)
        distance = squared * lax.rsqrt(squared)
        high, low = halves((distance + 1.0 / ln2) * jnp.exp2(-distance))
        both = values[s]
        wide = jnp.dot(both, high, preferred_element_type=f32)
        rest = jnp.dot(both[:16], low, preferred_element_type=f32)
        return c, (wide[:16] + wide[16:] + rest) * (times.astype(f32) * ln2)

    def group(size, first):
        def step(t, carry):
            for c, term in [tile(first + t * size + u) for u in range(size)]:
                total[c] += term
            return carry

        return step

    full = count // GROUP
    lax.fori_loop(0, full, group(GROUP, 0), 0)
    rest = count - full * GROUP
    lax.fori_loop(0, (rest + TAIL_GROUP - 1) // TAIL_GROUP, group(TAIL_GROUP, full * GROUP), 0)
    for place, c in enumerate(served):
        out[:, place * leaf_size : (place + 1) * leaf_size] = total[c]


def fill_table(table, blocks, start):
    count, _, lanes = blocks.shape
    half = lanes // 2
    for m in range(count):
        block = blocks[m]
        swapped = jnp.concatenate([block[:, half:], block[:, :half]], axis=1)
        table[start + 2 * m] = stacked_halves(block)
        table[start + 2 * m + 1] = stacked_halves(swapped)


def picked(table, rows, low_lanes):
    pieces = []
    for k in range(0, len(rows) - 1, 2):
        pieces.append(jnp.where(low_lanes, table[rows[k]], table[rows[k + 1] ^ 1]))
    if len(rows) % 2:
        pieces.append(table[rows[-1]][:, : low_lanes.shape[1] // 2])
    return jnp.concatenate(pieces, axis=1)


def coupled_pairs(picks, couples):
    slots, rank, _ = couples.shape
    result = jnp.zeros((16, rank), f32)
    low_lanes = lax.broadcasted_iota(jnp.int32, (rank, 2 * rank), 1) < rank
    for start in range(0, slots, 8):
        pairs = (min(slots - start, 8) + 1) // 2
        highs, lows = [], []
        for m in range(pairs):
            even = couples[start + m]
            if start + pairs + m < slots:
                odd = couples[start + pairs + m]
            else:
                odd = jnp.zeros_like(even)
            high, low = halves(jnp.concatenate([even, odd], axis=1))
            highs.append(high)
            lows.append(low)
        right = jnp.concatenate(
            [jnp.concatenate(highs, axis=0), jnp.concatenate(lows, axis=0)], axis=1
        )
        left = jnp.concatenate(
            [picks(start, pairs), picks(start + pairs, pairs)], axis=0
        )
        wide = jnp.dot(left, right, preferred_element_type=f32)
        first = wide[:16, : 2 * rank] + wide[16:32, : 2 * rank] + wide[:16, 2 * rank :]
        second = wide[32:48, : 2 * rank] + wide[48:, : 2 * rank] + wide[32:48, 2 * rank :]
        result = result + first[:, :rank] + second[:, rank:]
    return result


def coupled(both, couples):
    count, rank, _ = couples.shape
    high, low = halves(couples.reshape(count * rank, rank))
    wide = jnp.dot(both, jnp.concatenate([high, low], axis=1), preferred_element_type=f32)
    return wide[:16, :rank] + wide[16:, :rank] + wide[:16, rank:]


def inner_kernel(
    items, box, points_in, probes_in, out, sent_out,
    points, probes, values, source, target, total, listed, held_semaphores, sent, sent_semaphore,
    *, groups
):
    held = copies([(points_in, points), (probes_in, probes)], held_semaphores)
    for i in range(sent.shape[0]):
        sent[i] = box[...]
    (sending,) = copies([(sent, sent_out)], sent_semaphore)
    near_field(
        items, points, probes, None, None, out, values, source, target, total, listed, held, groups
    )
    sending.wait()


def field_kernel(
    items, points_in, probes_in, left, right, before_in, middle_in, after_in, couples_in, out,
    far_out, points, probes, values, source, target, total, listed, held_semaphores, table, couples,
    semaphores, before, middle, after, window_semaphores, *, groups
):
    leaves, slots, rank, _ = couples.shape
    steps = leaves // FAR_STEP

    held = copies([(points_in, points), (probes_in, probes)], held_semaphores)

    window = copies(
        [(before_in, before), (middle_in, middle), (after_in, after)], window_semaphores
    )

    def arriving(step):
        run = pl.ds(step * FAR_STEP, FAR_STEP)
        return pltpu.make_async_copy(couples_in.at[run], couples.at[run], semaphores.at[step])

    def start(step, carry):
        arriving(step).start()
        return carry

    lax.fori_loop(0, steps, start, 0)
    near_field(
        items, points, probes, left, right, out, values, source, target, total, listed, held, groups
    )

    empty = (2 * FAR_REACH + 1) * leaves
    low_lanes = lax.broadcasted_iota(jnp.int32, (32, 2 * rank), 1) < rank
    for copy in window:
        copy.wait()
    for b in range(3):
        for place, blocks in ((b, before), (3 + b, middle), (6 + b, after)):
            fill_table(table, blocks.at[b], place * leaves)
    table[empty] = jnp.zeros_like(table[empty])
    table[empty + 1] = jnp.zeros_like(table[empty])
    first_row = items.shape[0] - leaves

    def far_leaf(c):
        def picks(start, count):
            listed_here = range(start, start + count)
            rows = [items[first_row + c, k] if k < slots else empty for k in listed_here]
            return picked(table, rows, low_lanes)

        return coupled_pairs(picks, couples.at[c])

    def far_step(step, carry):
        arriving(step).wait()
        for u in range(0, FAR_STEP, 2):
            c = step * FAR_STEP + u
            far_out[c // 2] = jnp.concatenate([far_leaf(c), far_leaf(c + 1)], axis=1)
        return carry

    lax.fori_loop(0, steps, far_step, 0)


def down_kernel(
    box_list, column_list, boxes_in, couple_box_in, couple_column_in,
    transfer_box_in, far_in, inner_in, outer_in, transfer_in, basis_in, out,
    gathered, couple_box, couple_column, transfer_box, far_leaf, inner, outer, transfer_leaf, basis,
    semaphores,
):
    leaves, rank, leaf_size = basis.shape
    slots, column_slots = box_list.shape[1], column_list.shape[1]
    low_lanes = lax.broadcasted_iota(jnp.int32, (32, 2 * rank), 1) < rank
    arriving = copies(
        [
            (boxes_in, gathered),
            (couple_box_in, couple_box),
            (couple_column_in, couple_column),
            (transfer_box_in, transfer_box),
            (far_in, far_leaf),
            (inner_in, inner),
            (outer_in, outer),
        ]
        + parts(transfer_in, transfer_leaf)
        + parts(basis_in, basis),
        semaphores,
    )
    later = 7 + CHUNKS
    for copy in arriving[:4]:
        copy.wait()

    def box_row(entry):
        return jnp.where(entry >= 0, entry, 0)

    def pick(k):
        entry = box_list[0, k]
        return gathered[box_row(entry)] * jnp.where(entry >= 0, 1.0, 0.0)

    pieces = []
    for k in range(0, slots, 2):
        if k + 1 < slots:
            pieces.append(stacked_halves(jnp.where(low_lanes[:16], pick(k), exchanged(pick(k + 1)))))
        else:
            pieces.append(stacked_halves(pick(k))[:, :rank])
    far_box = coupled(jnp.concatenate(pieces, axis=1), couple_box[0])

    columns = []
    for k in range(column_slots):
        row = column_list[0, k]
        block = gathered[box_row(row * 4)]
        for j in range(1, 4):
            block = block + gathered[box_row(row * 4 + j)]
        columns.append(block * jnp.where(row >= 0, 1.0, 0.0))
    pieces = [
        stacked_halves(jnp.where(low_lanes[:16], exchanged(columns[k]), columns[k + 1]))
        for k in range(0, column_slots, 2)
    ]
    far_column = coupled(jnp.concatenate(pieces, axis=1), couple_column[0])
    down_box = far_box + product3(far_column, transfer_box[0], ((1,), (1,)))

    for copy in arriving[4:later]:
        copy.wait()
    high, low = halves(transfer_leaf[...].reshape(leaves * rank, rank))
    both = stacked_halves(down_box)
    wide = contract(both, high, ((1,), (1,)))
    from_box = wide[:16] + wide[16:] + contract(both[:16], low, ((1,), (1,)))

    lane = lax.broadcasted_iota(jnp.int32, (16, 4 * rank), 1)
    for m in range(leaves // 4):
        if m % (leaves // 4 // CHUNKS) == 0:
            arriving[later + m // (leaves // 4 // CHUNKS)].wait()
        down = from_box[:, m * 4 * rank : (m + 1) * 4 * rank]
        down = down + jnp.concatenate([far_leaf[2 * m], far_leaf[2 * m + 1]], axis=1)
        own_rows = [
            jnp.where((lane >= j * rank) & (lane < (j + 1) * rank), down, 0.0) for j in range(4)
        ]
        left = stacked_halves(jnp.concatenate(own_rows, axis=0))
        high, low = halves(basis[4 * m : 4 * m + 4].reshape(4 * rank, leaf_size))
        wide = jnp.dot(left, high, preferred_element_type=f32)
        rest = jnp.dot(left[:64], low, preferred_element_type=f32)
        result = wide[:64] + wide[64:] + rest
        for j in range(4):
            c = 4 * m + j
            held, place = outer, c if c < NEAR_REACH else c - leaves + 2 * NEAR_REACH
            if NEAR_REACH <= c < leaves - NEAR_REACH:
                held, place = inner, c - NEAR_REACH
            near_value = held[:, place * leaf_size : (place + 1) * leaf_size]
            lanes = slice(c * leaf_size, (c + 1) * leaf_size)
            out[:, lanes] = near_value + result[16 * j : 16 * j + 16]


def whole(count):
    return [pl.BlockSpec(memory_space=pltpu.VMEM)] * count


def scalars(count):
    return [pl.BlockSpec(memory_space=pltpu.SMEM)] * count


def params(mebibytes):
    return pltpu.CompilerParams(vmem_limit_bytes=mebibytes * 2**20)


def cost(flops):
    return pl.CostEstimate(flops=flops, bytes_accessed=2**20, transcendentals=0)


def shifted(array, axis, by):
    devices = lax.axis_size(axis)
    return lax.ppermute(array, axis, [(i, (i + by) % devices) for i in range(devices)])


def hbm(count):
    return [pl.BlockSpec(memory_space=pl.ANY)] * count


def like(array):
    return pltpu.VMEM(array.shape, array.dtype)


def copy_semaphores(count):
    return pltpu.SemaphoreType.DMA((count,))


def per_device(
    points,
    probes,
    basis,
    transfer_leaf,
    transfer_box,
    couple_leaf,
    couple_box,
    couple_column,
    near_list,
    far_list,
    box_list,
    column_list,
):
    leaves, leaf_size, rank = basis.shape
    probe_count = probes.shape[0]
    near_slots = near_list.T
    basis = basis.transpose(0, 2, 1)
    pairs = leaves // 2
    blocks = pairs + NEAR_REACH * leaf_size // 128 + 2

    edges = jax.ShapeDtypeStruct((blocks, probe_count, 2 * rank), f32)
    bundle_last, bundle_first, own, box, items = pl.pallas_call(
        skeleton_kernel,
        out_shape=(
            edges,
            edges,
            jax.ShapeDtypeStruct((pairs, probe_count, 2 * rank), f32),
            jax.ShapeDtypeStruct((probe_count, 2 * rank), f32),
            jax.ShapeDtypeStruct((near_slots.shape[0] + leaves, 128), jnp.int32),
        ),
        in_specs=whole(3) + hbm(3) + whole(1),
        out_specs=tuple(whole(5)),
        scratch_shapes=[like(probes), like(basis), like(transfer_leaf)]
        + [copy_semaphores(1 + CHUNKS), copy_semaphores(1)],
        compiler_params=params(60),
        name="skeletons",
    )(near_slots, far_list, points, probes, basis, transfer_leaf, transfer_box)

    left, right = shifted(bundle_last, ring, 1), shifted(bundle_first, ring, -1)

    window = leaves + 2 * NEAR_REACH
    near_scratch = [
        like(points),
        like(probes),
        pltpu.VMEM((window, 2 * probe_count, leaf_size), bf16),
        pltpu.VMEM((window, leaf_size, FEATURES), bf16),
        pltpu.VMEM((leaves, FEATURES, leaf_size), bf16),
        pltpu.VMEM((leaves, probe_count, leaf_size), f32),
        pltpu.SMEM((leaves * near_slots.shape[0] + 2 * GROUP,), jnp.int32),
        copy_semaphores(2),
    ]
    inner = ((NEAR_REACH, leaves - NEAR_REACH),)
    outer = ((0, NEAR_REACH), (leaves - NEAR_REACH, leaves))
    half = jax.ShapeDtypeStruct((probe_count, probes.shape[1] // 2), f32)
    copies_of_box = (lax.axis_size(ring), probe_count, 2 * rank)
    near_inner, sent = pl.pallas_call(
        functools.partial(inner_kernel, groups=inner),
        out_shape=(half, jax.ShapeDtypeStruct(copies_of_box, f32)),
        in_specs=scalars(1) + whole(1) + hbm(2),
        out_specs=tuple(whole(1) + hbm(1)),
        scratch_shapes=near_scratch + [pltpu.VMEM(copies_of_box, f32), copy_semaphores(1)],
        compiler_params=params(60),
        cost_estimate=cost(10_000_000_000),
        name="near_inner",
    )(items, box, points, probes)

    sent, left, right, own = lax.optimization_barrier((sent, left, right, own))
    middle = jnp.stack([left[:pairs], own, right[:pairs]])
    before, after = shifted(middle, ring, 3), shifted(middle, ring, -3)
    boxes = lax.all_to_all(sent, ring, 0, 0, tiled=True)

    near_outer, far_leaf = pl.pallas_call(
        functools.partial(field_kernel, groups=outer),
        out_shape=(half, jax.ShapeDtypeStruct((pairs, probe_count, 2 * rank), f32)),
        in_specs=scalars(1) + hbm(2) + whole(2) + hbm(4),
        out_specs=tuple(whole(2)),
        scratch_shapes=near_scratch
        + [
            pltpu.VMEM(((2 * FAR_REACH + 1) * leaves + 2, 2 * probe_count, 2 * rank), bf16),
            like(couple_leaf),
            copy_semaphores(leaves // FAR_STEP),
        ]
        + [like(middle)] * 3
        + [copy_semaphores(3)],
        compiler_params=params(63),
        cost_estimate=cost(20_000_000_000),
        name="near_far",
    )(items, points, probes, left, right, before, middle, after, couple_leaf)

    held = (boxes, couple_box, couple_column, transfer_box, far_leaf, near_inner, near_outer)
    held += (transfer_leaf, basis)
    return pl.pallas_call(
        down_kernel,
        out_shape=jax.ShapeDtypeStruct(probes.shape, f32),
        in_specs=scalars(2) + hbm(9),
        out_specs=pl.BlockSpec(memory_space=pltpu.VMEM),
        scratch_shapes=[like(array) for array in held] + [copy_semaphores(7 + 2 * CHUNKS)],
        compiler_params=params(60),
        name="down",
    )(box_list, column_list, *held)


def solution(mesh):
    placed = (
        P(None, ring),
        P(None, ring),
        P(ring, None, None),
        P(ring, None, None),
        P(ring, None, None),
        P(ring, None, None, None),
        P(ring, None, None, None),
        P("leaf", None, None, None),
        P(ring, None),
        P(ring, None),
        P(ring, None),
        P("leaf", None),
    )
    return jax.shard_map(
        per_device, mesh=mesh, in_specs=placed, out_specs=P(None, ring), check_vma=False
    )
```

```python
import functools
import math

import jax
import jax.numpy as jnp
from jax import lax
from jax.experimental import pallas as pl
from jax.experimental.pallas import tpu as pltpu
from jax.sharding import PartitionSpec as P

NEAR_REACH = 8
FAR_REACH = 4
FEATURES = 16
GROUP = 16
TAIL_GROUP = 4
FAR_STEP = 4
CHUNKS = 8

matern_rate = math.sqrt(3.0) / 0.1
coordinate_scale = matern_rate * math.log2(math.e)
ln2 = math.log(2.0)
tiny = 1e-20
f32 = jnp.float32
bf16 = jnp.bfloat16
vmem_bytes = 60 * 2**20
ring = ("leaf", "sub")


def halves(array):
    high = array.astype(bf16)
    return high, (array - high.astype(f32)).astype(bf16)


def stacked_halves(array):
    return jnp.concatenate(halves(array), axis=0)


def contract(left, right, dims):
    return lax.dot_general(left, right, (dims, ((), ())), preferred_element_type=f32)


def product3(left, right, dims=((1,), (0,))):
    rows = left.shape[0]
    high, low = halves(right)
    both = stacked_halves(left)
    wide = contract(both, high, dims)
    return wide[:rows] + wide[rows:] + contract(both[:rows], low, dims)


def copies(pairs, semaphores):
    made = [
        pltpu.make_async_copy(source, held, semaphores.at[i])
        for i, (source, held) in enumerate(pairs)
    ]
    for copy in made:
        copy.start()
    return made


def parts(source, held):
    length = source.shape[0] // CHUNKS
    runs = [pl.ds(i * length, length) for i in range(CHUNKS)]
    return [(source.at[run], held.at[run]) for run in runs]


def exchanged(block):
    half = block.shape[1] // 2
    return jnp.concatenate([block[:, half:], block[:, :half]], axis=1)


def skeleton_kernel(
    near, far, points, probes_in, basis_in, transfer_in, transfer_box, out, out_first, own, box_out, items,
    probes, basis, transfer_leaf, semaphores, later_semaphore,
):
    leaves, rank, leaf_size = basis.shape
    arriving = copies([(probes_in, probes)] + parts(basis_in, basis), semaphores)
    slots = near.shape[0]
    pairs = leaves // 2
    low_lanes = lax.broadcasted_iota(jnp.int32, (16, 2 * rank), 1) < rank

    leaf = lax.broadcasted_iota(jnp.int32, (1, leaves), 1)
    rows = [near[k : k + 1, :] for k in range(slots)]
    for k in range(slots):
        new = rows[k] >= 0
        times = jnp.ones_like(leaf)
        for j in range(k):
            new = new & (rows[j] != rows[k])
        for j in range(k + 1, slots):
            times = times + jnp.where(rows[j] == rows[k], 1, 0)
        place = rows[k] - rows[0] + leaf + NEAR_REACH
        items[k : k + 1, 0:leaves] = jnp.where(new, leaf + place * 64 + times * 4096, 0)
    empty = (2 * FAR_REACH + 1) * leaves
    place = far[...] - (near[0:1, 0:1] - FAR_REACH * leaves)
    items[slots : slots + leaves, 0 : far.shape[1]] = jnp.where(far[...] >= 0, place, empty)

    arriving[0].wait()
    width = probes.shape[1]
    edge = NEAR_REACH * leaf_size
    for side, start in ((out, width - edge), (out_first, 0)):
        for j in range(edge // 128):
            lanes = slice(start + j * 128, start + (j + 1) * 128)
            side[pairs + j] = probes[:, lanes]
            side[pairs + edge // 128, j : j + 1, :] = points[0:1, lanes]
            side[pairs + 1 + edge // 128, j : j + 1, :] = points[1:2, lanes]

    def leaf_probes(c):
        return stacked_halves(probes[:, c * leaf_size : (c + 1) * leaf_size])

    def summed(wide):
        return wide[:16] + wide[16:] + exchanged(wide[:16])

    skeletons = []
    for m in range(pairs):
        if m % (pairs // CHUNKS) == 0:
            arriving[1 + m // (pairs // CHUNKS)].wait()
        if m == 0:
            later = copies([(transfer_in, transfer_leaf)], later_semaphore)
        left = jnp.concatenate([leaf_probes(2 * m), leaf_probes(2 * m + 1)], axis=0)
        right = jnp.concatenate([stacked_halves(basis[2 * m]), stacked_halves(basis[2 * m + 1])], axis=0)
        wide = contract(left, right, ((1,), (1,)))
        even, odd = summed(wide[:32, : 2 * rank]), summed(wide[32:, 2 * rank :])
        pair = jnp.where(low_lanes, even, exchanged(odd))
        out[m] = pair
        out_first[m] = pair
        own[m] = pair
        skeletons.append(pair)
    later[0].wait()
    high, low = halves(transfer_leaf[...].reshape(leaves * rank, rank))
    wide = jnp.dot(
        stacked_halves(jnp.concatenate(skeletons, axis=1)),
        jnp.concatenate([high, low], axis=1),
        preferred_element_type=f32,
    )
    box = summed(wide)[:, :rank]
    block = jnp.concatenate([box, product3(box, transfer_box[0])], axis=1)
    box_out[...] = block


def near_field(
    items, points, probes, left, right, out, values, source, target, total, listed, arriving, groups
):
    leaves, _, leaf_size = target.shape
    slots = items.shape[0] - leaves
    pieces = leaf_size // 128
    pairs = leaves // 2
    edge_blocks = NEAR_REACH * pieces

    count = jnp.int32(0)
    served = [c for begin, end in groups for c in range(begin, end)]
    for c in served:
        for k in range(slots):
            item = items[k, c]
            listed[count] = item
            count = count + jnp.where(item != 0, 1, 0)
    for u in range(TAIL_GROUP):
        listed[count + u] = served[0] + (served[0] + NEAR_REACH) * 64

    for copy in arriving:
        copy.wait()
    ones = jnp.ones((3, leaf_size), f32)
    pad = jnp.zeros((2, leaf_size), f32)
    window = {c + j for c in served for j in range(2 * NEAR_REACH + 1)}
    for w in sorted(window):
        own = NEAR_REACH <= w < NEAR_REACH + leaves
        if own:
            lanes = slice((w - NEAR_REACH) * leaf_size, (w - NEAR_REACH + 1) * leaf_size)
            place, value = points[:, lanes], probes[:, lanes]
        else:
            side = left if w < NEAR_REACH else right
            first = (w if w < NEAR_REACH else w - NEAR_REACH - leaves) * pieces
            runs = range(first, first + pieces)
            value = jnp.concatenate([side[pairs + j] for j in runs], axis=1)
            place = jnp.concatenate(
                [
                    jnp.concatenate(
                        [side[pairs + edge_blocks + d, j : j + 1, :] for j in runs], axis=1
                    )
                    for d in range(2)
                ],
                axis=0,
            )
        values[w] = stacked_halves(value)
        scaled = (place - 0.5) * coordinate_scale
        first = scaled.astype(bf16).astype(f32)
        second = (scaled - first).astype(bf16).astype(f32)
        kept = first + second
        norm = kept[0:1] * kept[0:1] + kept[1:2] * kept[1:2]
        norm1 = norm.astype(bf16).astype(f32)
        rest = norm - norm1
        norm2 = rest.astype(bf16).astype(f32)
        norms = jnp.concatenate([norm1, norm2, rest - norm2], axis=0)
        rows = jnp.concatenate([first, second, first, second, norms, ones, pad], axis=0)
        source[w] = rows.T.astype(bf16)
        if w - NEAR_REACH in served:
            target[w - NEAR_REACH] = jnp.concatenate(
                [-2.0 * first, -2.0 * first, -2.0 * second, -2.0 * second, ones, norms, pad], axis=0
            ).astype(bf16)
    total[...] = jnp.zeros_like(total)

    def tile(i):
        item = listed[i]
        c, s, times = item & 63, (item >> 6) & 63, item >> 12
        squared = jnp.dot(source[s], target[c], preferred_element_type=f32)
        squared = jnp.maximum(squared, tiny)
        distance = squared * lax.rsqrt(squared)
        high, low = halves((distance + 1.0 / ln2) * jnp.exp2(-distance))
        both = values[s]
        wide = jnp.dot(both, high, preferred_element_type=f32)
        rest = jnp.dot(both[:16], low, preferred_element_type=f32)
        return c, (wide[:16] + wide[16:] + rest) * (times.astype(f32) * ln2)

    def group(size, first):
        def step(t, carry):
            for c, term in [tile(first + t * size + u) for u in range(size)]:
                total[c] += term
            return carry

        return step

    full = count // GROUP
    lax.fori_loop(0, full, group(GROUP, 0), 0)
    rest = count - full * GROUP
    lax.fori_loop(0, (rest + TAIL_GROUP - 1) // TAIL_GROUP, group(TAIL_GROUP, full * GROUP), 0)
    for place, c in enumerate(served):
        out[:, place * leaf_size : (place + 1) * leaf_size] = total[c]


def fill_table(table, blocks, start):
    count, _, lanes = blocks.shape
    half = lanes // 2
    for m in range(count):
        block = blocks[m]
        swapped = jnp.concatenate([block[:, half:], block[:, :half]], axis=1)
        table[start + 2 * m] = stacked_halves(block)
        table[start + 2 * m + 1] = stacked_halves(swapped)


def picked(table, rows, low_lanes):
    pieces = []
    for k in range(0, len(rows) - 1, 2):
        pieces.append(jnp.where(low_lanes, table[rows[k]], table[rows[k + 1] ^ 1]))
    if len(rows) % 2:
        pieces.append(table[rows[-1]][:, : low_lanes.shape[1] // 2])
    return jnp.concatenate(pieces, axis=1)


def coupled_pairs(picks, couples):
    slots, rank, _ = couples.shape
    result = jnp.zeros((16, rank), f32)
    low_lanes = lax.broadcasted_iota(jnp.int32, (rank, 2 * rank), 1) < rank
    for start in range(0, slots, 8):
        pairs = (min(slots - start, 8) + 1) // 2
        highs, lows = [], []
        for m in range(pairs):
            even = couples[start + m]
            if start + pairs + m < slots:
                odd = couples[start + pairs + m]
            else:
                odd = jnp.zeros_like(even)
            high, low = halves(jnp.concatenate([even, odd], axis=1))
            highs.append(high)
            lows.append(low)
        right = jnp.concatenate(
            [jnp.concatenate(highs, axis=0), jnp.concatenate(lows, axis=0)], axis=1
        )
        left = jnp.concatenate(
            [picks(start, pairs), picks(start + pairs, pairs)], axis=0
        )
        wide = jnp.dot(left, right, preferred_element_type=f32)
        first = wide[:16, : 2 * rank] + wide[16:32, : 2 * rank] + wide[:16, 2 * rank :]
        second = wide[32:48, : 2 * rank] + wide[48:, : 2 * rank] + wide[32:48, 2 * rank :]
        result = result + first[:, :rank] + second[:, rank:]
    return result


def coupled(both, couples):
    count, rank, _ = couples.shape
    high, low = halves(couples.reshape(count * rank, rank))
    wide = jnp.dot(both, jnp.concatenate([high, low], axis=1), preferred_element_type=f32)
    return wide[:16, :rank] + wide[16:, :rank] + wide[:16, rank:]


def inner_kernel(
    items, box, points_in, probes_in, out, sent_out,
    points, probes, values, source, target, total, listed, held_semaphores, sent, sent_semaphore,
    *, groups
):
    held = copies([(points_in, points), (probes_in, probes)], held_semaphores)
    for i in range(sent.shape[0]):
        sent[i] = box[...]
    (sending,) = copies([(sent, sent_out)], sent_semaphore)
    near_field(
        items, points, probes, None, None, out, values, source, target, total, listed, held, groups
    )
    sending.wait()


def field_kernel(
    items, points_in, probes_in, left, right, before_in, middle_in, after_in, couples_in, out,
    far_out, points, probes, values, source, target, total, listed, held_semaphores, table, couples,
    semaphores, before, middle, after, window_semaphores, *, groups
):
    leaves, slots, rank, _ = couples.shape
    steps = leaves // FAR_STEP

    held = copies([(points_in, points), (probes_in, probes)], held_semaphores)

    window = copies(
        [(before_in, before), (middle_in, middle), (after_in, after)], window_semaphores
    )

    def arriving(step):
        run = pl.ds(step * FAR_STEP, FAR_STEP)
        return pltpu.make_async_copy(couples_in.at[run], couples.at[run], semaphores.at[step])

    def start(step, carry):
        arriving(step).start()
        return carry

    lax.fori_loop(0, steps, start, 0)
    near_field(
        items, points, probes, left, right, out, values, source, target, total, listed, held, groups
    )

    empty = (2 * FAR_REACH + 1) * leaves
    low_lanes = lax.broadcasted_iota(jnp.int32, (32, 2 * rank), 1) < rank
    for copy in window:
        copy.wait()
    for b in range(3):
        for place, blocks in ((b, before), (3 + b, middle), (6 + b, after)):
            fill_table(table, blocks.at[b], place * leaves)
    table[empty] = jnp.zeros_like(table[empty])
    table[empty + 1] = jnp.zeros_like(table[empty])
    first_row = items.shape[0] - leaves

    def far_leaf(c):
        def picks(start, count):
            listed_here = range(start, start + count)
            rows = [items[first_row + c, k] if k < slots else empty for k in listed_here]
            return picked(table, rows, low_lanes)

        return coupled_pairs(picks, couples.at[c])

    def far_step(step, carry):
        arriving(step).wait()
        for u in range(0, FAR_STEP, 2):
            c = step * FAR_STEP + u
            far_out[c // 2] = jnp.concatenate([far_leaf(c), far_leaf(c + 1)], axis=1)
        return carry

    lax.fori_loop(0, steps, far_step, 0)


def down_kernel(
    box_list, column_list, boxes_in, couple_box_in, couple_column_in,
    transfer_box_in, far_in, inner_in, outer_in, transfer_in, basis_in, out,
    gathered, couple_box, couple_column, transfer_box, far_leaf, inner, outer, transfer_leaf, basis,
    semaphores,
):
    leaves, rank, leaf_size = basis.shape
    slots, column_slots = box_list.shape[1], column_list.shape[1]
    low_lanes = lax.broadcasted_iota(jnp.int32, (32, 2 * rank), 1) < rank
    arriving = copies(
        [
            (boxes_in, gathered),
            (couple_box_in, couple_box),
            (couple_column_in, couple_column),
            (transfer_box_in, transfer_box),
            (far_in, far_leaf),
            (inner_in, inner),
            (outer_in, outer),
        ]
        + parts(transfer_in, transfer_leaf)
        + parts(basis_in, basis),
        semaphores,
    )
    later = 7 + CHUNKS
    for copy in arriving[:4]:
        copy.wait()

    def box_row(entry):
        return jnp.where(entry >= 0, entry, 0)

    def pick(k):
        entry = box_list[0, k]
        return gathered[box_row(entry)] * jnp.where(entry >= 0, 1.0, 0.0)

    pieces = []
    for k in range(0, slots, 2):
        if k + 1 < slots:
            pieces.append(stacked_halves(jnp.where(low_lanes[:16], pick(k), exchanged(pick(k + 1)))))
        else:
            pieces.append(stacked_halves(pick(k))[:, :rank])
    far_box = coupled(jnp.concatenate(pieces, axis=1), couple_box[0])

    columns = []
    for k in range(column_slots):
        row = column_list[0, k]
        block = gathered[box_row(row * 4)]
        for j in range(1, 4):
            block = block + gathered[box_row(row * 4 + j)]
        columns.append(block * jnp.where(row >= 0, 1.0, 0.0))
    pieces = [
        stacked_halves(jnp.where(low_lanes[:16], exchanged(columns[k]), columns[k + 1]))
        for k in range(0, column_slots, 2)
    ]
    far_column = coupled(jnp.concatenate(pieces, axis=1), couple_column[0])
    down_box = far_box + product3(far_column, transfer_box[0], ((1,), (1,)))

    for copy in arriving[4:later]:
        copy.wait()
    high, low = halves(transfer_leaf[...].reshape(leaves * rank, rank))
    both = stacked_halves(down_box)
    wide = contract(both, high, ((1,), (1,)))
    from_box = wide[:16] + wide[16:] + contract(both[:16], low, ((1,), (1,)))

    lane = lax.broadcasted_iota(jnp.int32, (16, 4 * rank), 1)
    for m in range(leaves // 4):
        if m % (leaves // 4 // CHUNKS) == 0:
            arriving[later + m // (leaves // 4 // CHUNKS)].wait()
        down = from_box[:, m * 4 * rank : (m + 1) * 4 * rank]
        down = down + jnp.concatenate([far_leaf[2 * m], far_leaf[2 * m + 1]], axis=1)
        own_rows = [
            jnp.where((lane >= j * rank) & (lane < (j + 1) * rank), down, 0.0) for j in range(4)
        ]
        left = stacked_halves(jnp.concatenate(own_rows, axis=0))
        high, low = halves(basis[4 * m : 4 * m + 4].reshape(4 * rank, leaf_size))
        wide = jnp.dot(left, high, preferred_element_type=f32)
        rest = jnp.dot(left[:64], low, preferred_element_type=f32)
        result = wide[:64] + wide[64:] + rest
        for j in range(4):
            c = 4 * m + j
            held, place = outer, c if c < NEAR_REACH else c - leaves + 2 * NEAR_REACH
            if NEAR_REACH <= c < leaves - NEAR_REACH:
                held, place = inner, c - NEAR_REACH
            near_value = held[:, place * leaf_size : (place + 1) * leaf_size]
            lanes = slice(c * leaf_size, (c + 1) * leaf_size)
            out[:, lanes] = near_value + result[16 * j : 16 * j + 16]


def whole(count):
    return [pl.BlockSpec(memory_space=pltpu.VMEM)] * count


def scalars(count):
    return [pl.BlockSpec(memory_space=pltpu.SMEM)] * count


def params(mebibytes):
    return pltpu.CompilerParams(vmem_limit_bytes=mebibytes * 2**20)


def cost(flops):
    return pl.CostEstimate(flops=flops, bytes_accessed=2**20, transcendentals=0)


def shifted(array, axis, by):
    devices = lax.axis_size(axis)
    return lax.ppermute(array, axis, [(i, (i + by) % devices) for i in range(devices)])


def hbm(count):
    return [pl.BlockSpec(memory_space=pl.ANY)] * count


def like(array):
    return pltpu.VMEM(array.shape, array.dtype)


def copy_semaphores(count):
    return pltpu.SemaphoreType.DMA((count,))


def per_device(
    points,
    probes,
    basis,
    transfer_leaf,
    transfer_box,
    couple_leaf,
    couple_box,
    couple_column,
    near_list,
    far_list,
    box_list,
    column_list,
):
    leaves, leaf_size, rank = basis.shape
    probe_count = probes.shape[0]
    near_slots = near_list.T
    basis = basis.transpose(0, 2, 1)
    pairs = leaves // 2
    blocks = pairs + NEAR_REACH * leaf_size // 128 + 2

    edges = jax.ShapeDtypeStruct((blocks, probe_count, 2 * rank), f32)
    bundle_last, bundle_first, own, box, items = pl.pallas_call(
        skeleton_kernel,
        out_shape=(
            edges,
            edges,
            jax.ShapeDtypeStruct((pairs, probe_count, 2 * rank), f32),
            jax.ShapeDtypeStruct((probe_count, 2 * rank), f32),
            jax.ShapeDtypeStruct((near_slots.shape[0] + leaves, 128), jnp.int32),
        ),
        in_specs=whole(3) + hbm(3) + whole(1),
        out_specs=tuple(whole(5)),
        scratch_shapes=[like(probes), like(basis), like(transfer_leaf)]
        + [copy_semaphores(1 + CHUNKS), copy_semaphores(1)],
        compiler_params=params(60),
        name="skeletons",
    )(near_slots, far_list, points, probes, basis, transfer_leaf, transfer_box)

    left, right = shifted(bundle_last, ring, 1), shifted(bundle_first, ring, -1)

    window = leaves + 2 * NEAR_REACH
    near_scratch = [
        like(points),
        like(probes),
        pltpu.VMEM((window, 2 * probe_count, leaf_size), bf16),
        pltpu.VMEM((window, leaf_size, FEATURES), bf16),
        pltpu.VMEM((leaves, FEATURES, leaf_size), bf16),
        pltpu.VMEM((leaves, probe_count, leaf_size), f32),
        pltpu.SMEM((leaves * near_slots.shape[0] + 2 * GROUP,), jnp.int32),
        copy_semaphores(2),
    ]
    inner = ((NEAR_REACH, leaves - NEAR_REACH),)
    outer = ((0, NEAR_REACH), (leaves - NEAR_REACH, leaves))
    half = jax.ShapeDtypeStruct((probe_count, probes.shape[1] // 2), f32)
    copies_of_box = (lax.axis_size(ring), probe_count, 2 * rank)
    near_inner, sent = pl.pallas_call(
        functools.partial(inner_kernel, groups=inner),
        out_shape=(half, jax.ShapeDtypeStruct(copies_of_box, f32)),
        in_specs=scalars(1) + whole(1) + hbm(2),
        out_specs=tuple(whole(1) + hbm(1)),
        scratch_shapes=near_scratch + [pltpu.VMEM(copies_of_box, f32), copy_semaphores(1)],
        compiler_params=params(60),
        cost_estimate=cost(10_000_000_000),
        name="near_inner",
    )(items, box, points, probes)

    sent, left, right, own = lax.optimization_barrier((sent, left, right, own))
    middle = jnp.stack([left[:pairs], own, right[:pairs]])
    before, after = shifted(middle, ring, 3), shifted(middle, ring, -3)
    boxes = lax.all_to_all(sent, ring, 0, 0, tiled=True)

    near_outer, far_leaf = pl.pallas_call(
        functools.partial(field_kernel, groups=outer),
        out_shape=(half, jax.ShapeDtypeStruct((pairs, probe_count, 2 * rank), f32)),
        in_specs=scalars(1) + hbm(2) + whole(2) + hbm(4),
        out_specs=tuple(whole(2)),
        scratch_shapes=near_scratch
        + [
            pltpu.VMEM(((2 * FAR_REACH + 1) * leaves + 2, 2 * probe_count, 2 * rank), bf16),
            like(couple_leaf),
            copy_semaphores(leaves // FAR_STEP),
        ]
        + [like(middle)] * 3
        + [copy_semaphores(3)],
        compiler_params=params(63),
        cost_estimate=cost(20_000_000_000),
        name="near_far",
    )(items, points, probes, left, right, before, middle, after, couple_leaf)

    held = (boxes, couple_box, couple_column, transfer_box, far_leaf, near_inner, near_outer)
    held += (transfer_leaf, basis)
    return pl.pallas_call(
        down_kernel,
        out_shape=jax.ShapeDtypeStruct(probes.shape, f32),
        in_specs=scalars(2) + hbm(9),
        out_specs=pl.BlockSpec(memory_space=pltpu.VMEM),
        scratch_shapes=[like(array) for array in held] + [copy_semaphores(7 + 2 * CHUNKS)],
        compiler_params=params(60),
        name="down",
    )(box_list, column_list, *held)


def solution(mesh):
    placed = (
        P(None, ring),
        P(None, ring),
        P(ring, None, None),
        P(ring, None, None),
        P(ring, None, None),
        P(ring, None, None, None),
        P(ring, None, None, None),
        P("leaf", None, None, None),
        P(ring, None),
        P(ring, None),
        P(ring, None),
        P("leaf", None),
    )
    return jax.shard_map(
        per_device, mesh=mesh, in_specs=placed, out_specs=P(None, ring), check_vma=False
    )
```
